256 devices in a mesh: pair: 8 (over x, y_lo), grid: 32 (over z, y_hi, core).
Axes of the slice: x: 4, y: 4 (y_hi: 2, y_lo: 2; y = y_hi * 2 + y_lo), z: 8, core: 2. Of those that a mesh axis runs over, the one named last changes fastest.
Arguments:
- orbital_b: bfloat16 [16, 1408, 9600], P(None, 'pair', 'grid'), may hold values from -0.15625 to 0.15625
- pair_list: int32 [8, 2], replicated, may hold values from 0 to 15
- eps_occ: float32 [16], replicated, may hold values from -2 to -0.3
- eps_vir: float32 [1408], replicated, may hold values from 0.2 to 3
Outputs:
- density: float32 [1408, 1408], P('grid', 'pair')
The draws below stay inside these ranges and needn't reach their ends.
All inputs are finite; a program needn't handle non-finite values.
Results may differ from the reference program's by a relative error of at most 0.0012.
Values may be sent and summed in bfloat16 or wider, within the bound.
No kernel may reach another device: no remote copies, remote signals or barrier semaphores. Data moves between devices by JAX's collectives and lax.ppermute only.
A program may use at most 64 MiB of HBM per device.

```python
import jax
import jax.numpy as jnp

V = 1408
NAUX = 9600
OCC = 16
N_PAIR = 8


def plant(result, own_key, smallest, top_value):
    place = [jax.random.randint(jax.random.fold_in(own_key, axis), (), 0, length) for axis, length in enumerate(result.shape)]
    longest = result.shape.index(max(result.shape))
    neighbour = place[:longest] + [(place[longest] + 1) % result.shape[longest]] + place[longest + 1:]
    return result.at[tuple(place)].set(smallest).at[tuple(neighbour)].set(top_value)


def levels(own_key, dims, pieces, least, top_value):
    loudness = 1.0
    for position, shards_of in pieces:
        heights = jax.random.uniform(jax.random.fold_in(jax.random.fold_in(own_key, 6), position), (shards_of,), jnp.float32, least / len(pieces), top_value / len(pieces))
        loudness = loudness * jnp.repeat(jnp.exp(heights), dims[position] // shards_of).reshape((-1,) + (1,) * (len(dims) - 1 - position))
    return loudness


def normal_values(own_key, shape, deviation, most, pieces=(), kind=jnp.bfloat16):
    level = levels(own_key, shape, pieces, -0.22, 0.18) if pieces else 1.0
    drawn = jax.random.normal(own_key, shape, jnp.float32) * deviation * level
    return jnp.minimum(jnp.maximum(drawn, -most), most).astype(kind)


def setup_inputs(seed: int = 0) -> dict:
    keys = jax.random.split(jax.random.key(seed), 5)
    orbital_b = normal_values(keys[0], (OCC, V, NAUX), (0.6 * (NAUX * V) ** -0.25), 0.15625, ((1, 8), (2, 32)))
    pair_list = plant(jax.random.randint(keys[1], (N_PAIR, 2), 0, OCC), jax.random.fold_in(keys[1], 1), 0, OCC - 1).astype(jnp.int32)
    eps_occ = jnp.clip(jax.random.uniform(keys[2], (OCC,), jnp.float32, -2.0, -0.3), -2.0, -0.3)
    eps_vir = jnp.clip(jax.random.uniform(keys[3], (V,), jnp.float32, 0.2, 3.0), 0.2, 3.0)
    return {"orbital_b": orbital_b, "pair_list": pair_list, "eps_occ": eps_occ, "eps_vir": eps_vir}


def reference(orbital_b, pair_list, eps_occ, eps_vir):
    density = jnp.zeros((V, V), jnp.float32)
    for group in range(N_PAIR):
        first = pair_list[group, 0]
        second = pair_list[group, 1]
        integrals = jnp.dot(orbital_b[first], orbital_b[second].T, preferred_element_type=jnp.float32)
        denom = eps_vir[:, None] + eps_vir[None, :] - eps_occ[first] - eps_occ[second]
        amps = integrals / denom
        tilde = (2.0 * amps - amps.T).astype(jnp.bfloat16)
        amps16 = amps.astype(jnp.bfloat16)
        density = density + jnp.dot(tilde, amps16.T, preferred_element_type=jnp.float32)
        density = density + jnp.dot(tilde.T, amps16, preferred_element_type=jnp.float32)
    return density
```

```python
import functools

import jax
import jax.numpy as jnp
from jax import lax
from jax.experimental import pallas as pl
from jax.experimental.pallas import tpu as pltpu
from jax.sharding import Mesh
from jax.sharding import PartitionSpec as P

F32 = jnp.float32
BF16 = jnp.bfloat16
SLABS = ("x", "yl")
VMEM = pl.BlockSpec(memory_space=pltpu.VMEM)
SMEM = pl.BlockSpec(memory_space=pltpu.SMEM)
LIMIT = 48 * 1024 * 1024


def swap(value, axis):
    return lax.ppermute(value, axis, [(0, 1), (1, 0)])


def shift(value, axis, step):
    size = lax.axis_size(axis)
    return lax.ppermute(value, axis, [(i, (i + step) % size) for i in range(size)])


def dot_nt(a, b):
    return lax.dot_general(a, b, (((1,), (1,)), ((), ())), preferred_element_type=F32)


def integral_kernel(padded, where_ref, near_ref, far_ref, out_ref):
    sources, rows, naux = near_ref.shape
    half = sources // 2
    slab = rows - 2 * padded
    start = pl.multiple_of(where_ref[1] * padded, padded)
    total = None
    for ref in (near_ref, far_ref):
        for y in range(2):
            a = ref[half * y : half * (y + 1), pl.ds(start, padded), :].reshape(half * padded, naux)
            b = ref[half * y : half * (y + 1), 2 * padded :, :].reshape(half * slab, naux)
            term = dot_nt(a, b)
            total = term if total is None else total + term
    out_ref[...] = total


def density_kernel(nz, width, padded, where_ref, rows_ref, *refs):
    pieces = refs[: 2 * nz]
    out_ref, natural, blocks, highs = refs[2 * nz :]
    z, c, chunk = where_ref[0], where_ref[1], where_ref[2]
    nvir = rows_ref.shape[1]
    slab = nvir // nz

    def join(own, far):
        first, second = jnp.where(c == 0, own, far), jnp.where(c == 0, far, own)
        parts = []
        for y in range(2):
            for piece in (first, second):
                parts.append(piece[:, y * padded : y * padded + width])
        return jnp.concatenate(parts, axis=1)

    def pad(block):
        zeros = jnp.zeros((block.shape[0], padded - width), block.dtype)
        halves = []
        for h in range(2):
            parts = []
            for y in range(2):
                at = (2 * y + h) * width
                parts += [block[:, at : at + width], zeros]
            halves.append(jnp.concatenate(parts, axis=1))
        return jnp.where(c == 0, halves[0], halves[1]), jnp.where(c == 0, halves[1], halves[0])

    rows = rows_ref[...]
    column = lax.broadcasted_iota(jnp.int32, rows.shape, 1)
    row = lax.broadcasted_iota(jnp.int32, rows.shape, 0)
    pick = jnp.where((column == chunk * width + row) & (row < width), 1.0, 0.0).astype(BF16)
    flipped = []
    for i in range(2 * nz):
        value = pieces[i][...]
        high = value.astype(BF16)
        rest = value - high.astype(F32)
        middle = rest.astype(BF16)
        low = (rest - middle.astype(F32)).astype(BF16)
        highs[i] = high
        flipped.append(dot_nt(pick, high) + (dot_nt(pick, middle) + dot_nt(pick, low)))
    for k in range(nz):
        natural[k] = rows[:, k * slab : (k + 1) * slab]
    for r in range(nz):
        blocks[lax.rem(z + r, nz)] = join(flipped[2 * r], flipped[2 * r + 1])
    turned = jnp.concatenate([blocks[k] for k in range(nz)], axis=1)
    tilde = (2.0 * rows - turned).astype(BF16)
    total = None
    for r in range(nz):
        own, far = pad(natural[lax.rem(z + r, nz)])
        for i, mine in ((2 * r, own), (2 * r + 1, far)):
            tilde_t = (2.0 * flipped[i] - mine).astype(BF16)
            term = jnp.dot(tilde_t, highs[i], preferred_element_type=F32)
            total = term if total is None else total + term
    for k in range(nz):
        out_ref[k] = total[:, k * slab : (k + 1) * slab]
    for r in range(nz):
        at = lax.rem(z + r, nz)
        out_ref[at] += join(dot_nt(tilde, highs[2 * r]), dot_nt(tilde, highs[2 * r + 1]))


def local(orbital_b, pair_list, eps_occ, eps_vir):
    slab, naux = orbital_b.shape[1:]
    nvir = eps_vir.shape[0]
    z, yh, c = (lax.axis_index(a) for a in ("z", "yh", "c"))
    nz = lax.axis_size("z")
    width = slab // 4
    padded = (width + 8) // 8 * 8
    group = lax.axis_index(SLABS)
    chunk = z * 4 + yh * 2 + c
    where = jnp.stack([z, c, chunk])

    left = orbital_b[pair_list[:, 0]].reshape(8, 2, 2, width, naux)
    left = jnp.pad(left, ((0, 0), (0, 0), (0, 0), (0, padded - width), (0, 0)))
    left = left.reshape(8, 2, 2 * padded, naux).transpose(1, 0, 2, 3)
    right = jnp.broadcast_to(orbital_b[pair_list[:, 1]][None], (2, 8, slab, naux))
    outgoing = jnp.concatenate([left, right], axis=2).reshape(16, 2 * padded + slab, naux)
    near = lax.all_to_all(outgoing, ("yh", "x", "yl"), split_axis=0, concat_axis=0, tiled=True)
    far = swap(near, "c")

    part = pl.pallas_call(
        functools.partial(integral_kernel, padded),
        out_shape=jax.ShapeDtypeStruct((8 * padded, nvir), F32),
        in_specs=[SMEM, VMEM, VMEM],
        out_specs=VMEM,
        compiler_params=pltpu.CompilerParams(vmem_limit_bytes=LIMIT),
    )(where, near, far).reshape(8, padded, nvir)

    def own(offset):
        return lax.dynamic_index_in_dim(part, lax.rem(z + offset, nz), 0, keepdims=False)

    cut = padded // 2
    up = shift(own(nz // 2)[:cut], "z", 1)
    down = shift(own(nz // 2)[cut:], "z", -1)
    up = jnp.concatenate([up, jnp.zeros_like(down)])
    down = jnp.concatenate([jnp.zeros_like(down), down])
    for step in range(nz // 2 - 1, 0, -1):
        up = shift(own(step) + up, "z", 1)
        down = shift(own(nz - step) + down, "z", -1)
    k_rows = own(0) + (up + down)

    chosen = lax.dynamic_index_in_dim(pair_list, group, 0, keepdims=False)
    shift_occ = eps_occ[chosen[0]] + eps_occ[chosen[1]]
    row_eps = lax.dynamic_slice_in_dim(eps_vir, chunk * width, width, 0)
    row_eps = jnp.pad(row_eps, (0, padded - width), constant_values=1.0)
    amp_rows = k_rows / (row_eps[:, None] + eps_vir[None, :] - shift_occ)

    mine = amp_rows
    other = swap(mine, "yh")
    both = jnp.where(yh == 0, jnp.stack([mine, other]), jnp.stack([other, mine]))
    ring = {0: both}
    up = down = both
    for step in range(1, nz // 2):
        up = shift(up, "z", 1)
        down = shift(down, "z", -1)
        ring[nz - step] = up
        ring[step] = down
    ring[nz // 2] = jnp.stack([shift(up[0], "z", 1), shift(down[1], "z", -1)])
    pieces = []
    for r in range(nz):
        for piece in (ring[r], swap(ring[r], "c")):
            pieces.append(piece.reshape(2 * padded, nvir))

    added = pl.pallas_call(
        functools.partial(density_kernel, nz, width, padded),
        out_shape=jax.ShapeDtypeStruct((nz, padded, slab), F32),
        in_specs=[SMEM] + [VMEM] * (2 * nz + 1),
        out_specs=VMEM,
        scratch_shapes=[pltpu.VMEM((nz, padded, slab), F32)] * 2 + [pltpu.VMEM((2 * nz, 2 * padded, nvir), BF16)],
        compiler_params=pltpu.CompilerParams(vmem_limit_bytes=LIMIT),
    )(where, amp_rows, *pieces)
    added = lax.all_to_all(added, SLABS, split_axis=0, concat_axis=0, tiled=True)
    return jnp.sum(added, axis=0)[:width]


def solution(mesh):
    fine = Mesh(mesh.devices.reshape(4, 2, 8, 2, 2), ("x", "yl", "z", "yh", "c"))
    pair, grid = SLABS, ("z", "yh", "c")
    in_specs = (P(None, pair, grid), P(), P(), P())
    return jax.shard_map(local, mesh=fine, in_specs=in_specs, out_specs=P(grid, pair), check_vma=False)
```

```python
import functools

import jax
import jax.numpy as jnp
from jax import lax
from jax.experimental import pallas as pl
from jax.experimental.pallas import tpu as pltpu
from jax.sharding import Mesh
from jax.sharding import PartitionSpec as P

F32 = jnp.float32
BF16 = jnp.bfloat16
SLABS = ("x", "yl")
VMEM = pl.BlockSpec(memory_space=pltpu.VMEM)
SMEM = pl.BlockSpec(memory_space=pltpu.SMEM)
PARAMS = pltpu.CompilerParams(vmem_limit_bytes=48 * 1024 * 1024)


def swap(value, axis):
    return lax.ppermute(value, axis, [(0, 1), (1, 0)])


def shift(value, axis, step):
    size = lax.axis_size(axis)
    return lax.ppermute(value, axis, [(i, (i + step) % size) for i in range(size)])


def dot_nt(a, b):
    return lax.dot_general(a, b, (((1,), (1,)), ((), ())), preferred_element_type=F32)


def split3(value):
    high = value.astype(BF16)
    rest = value - high.astype(F32)
    middle = rest.astype(BF16)
    return high, middle, (rest - middle.astype(F32)).astype(BF16)


def cost(flops, moved):
    return pl.CostEstimate(flops=flops, bytes_accessed=moved, transcendentals=0)


def integral_kernel(padded, where_ref, pair_ref, occ_ref, vir_ref, near_ref, far_ref, out_ref, denom_ref):
    sources, rows, naux = near_ref.shape
    half = sources // 2
    slab = rows - 2 * padded
    c, chunk, group = where_ref[1], where_ref[2], where_ref[3]
    start = pl.multiple_of(c * padded, padded)
    total = None
    for ref in (near_ref, far_ref):
        for y in range(2):
            a = ref[half * y : half * (y + 1), pl.ds(start, padded), :].reshape(half * padded, naux)
            b = ref[half * y : half * (y + 1), 2 * padded :, :].reshape(half * slab, naux)
            term = dot_nt(a, b)
            total = term if total is None else total + term
    out_ref[...] = total
    columns = jnp.broadcast_to(vir_ref[...], denom_ref.shape)
    place = lax.broadcasted_iota(jnp.int32, denom_ref.shape, 1)
    row = lax.broadcasted_iota(jnp.int32, denom_ref.shape, 0)
    width = slab // 4
    own = jnp.sum(jnp.where(place == chunk * width + row, columns, 0.0), axis=1, keepdims=True)
    denom_ref[...] = (own + columns) - occ_ref[pair_ref[group, 0]] - occ_ref[pair_ref[group, 1]]


def turn_kernel(nz, width, padded, where_ref, near_ref, far_ref, out_ref):
    part = where_ref[4]
    nvir = near_ref.shape[1]
    slab = nvir // nz
    column = lax.broadcasted_iota(jnp.int32, (padded, slab), 1)
    row = lax.broadcasted_iota(jnp.int32, (padded, slab), 0)
    pick = jnp.where((column == part * width + row) & (row < width), 1.0, 0.0).astype(BF16)
    for slot, ref in enumerate((near_ref, far_ref)):
        for k in range(nz):
            high, middle, low = split3(ref[:, k * slab : (k + 1) * slab])
            out_ref[k, slot] = dot_nt(pick, high) + (dot_nt(pick, middle) + dot_nt(pick, low))


def density_pieces(steps, nz, width, padded, where_ref, tilde, tilde_t_ref, pieces, total, blocks_ref):
    z, c = where_ref[0], where_ref[1]
    for n, r in enumerate(steps):
        at = lax.rem(z + r, nz)
        sides = []
        for slot in range(2):
            piece = pieces[2 * n + slot][...]
            term = jnp.dot(tilde_t_ref[at, slot], piece, preferred_element_type=F32)
            total = term if total is None else total + term
            sides.append(dot_nt(tilde, piece))
        blocks_ref[at] = join(c, sides[0], sides[1], width, padded)
    return total


def join(c, near, far, width, padded):
    first, second = jnp.where(c == 0, near, far), jnp.where(c == 0, far, near)
    parts = []
    for y in range(2):
        for piece in (first, second):
            parts.append(piece[:, y * padded : y * padded + width])
    return jnp.concatenate(parts, axis=1)


def early_kernel(steps, nz, width, padded, where_ref, rows_ref, turned_ref, *refs):
    pieces = refs[: 2 * len(steps)]
    total_ref, blocks_ref, tilde_ref, tilde_t_ref = refs[2 * len(steps) :]
    c = where_ref[1]
    slab = rows_ref.shape[1] // nz
    rows = rows_ref[...]
    zeros = jnp.zeros((padded, padded - width), F32)
    turned = []
    for k in range(nz):
        mine = rows[:, k * slab : (k + 1) * slab]
        halves = []
        for h in range(2):
            parts = []
            for y in range(2):
                at = (2 * y + h) * width
                parts += [mine[:, at : at + width], zeros]
            halves.append(jnp.concatenate(parts, axis=1))
        near, far = turned_ref[k, 0], turned_ref[k, 1]
        tilde_t_ref[k, 0] = (2.0 * near - jnp.where(c == 0, halves[0], halves[1])).astype(BF16)
        tilde_t_ref[k, 1] = (2.0 * far - jnp.where(c == 0, halves[1], halves[0])).astype(BF16)
        turned.append(join(c, near, far, width, padded))
    tilde = (2.0 * rows - jnp.concatenate(turned, axis=1)).astype(BF16)
    tilde_ref[...] = tilde
    total_ref[...] = density_pieces(steps, nz, width, padded, where_ref, tilde, tilde_t_ref, pieces, None, blocks_ref)


def late_kernel(steps, nz, width, padded, where_ref, total_ref, blocks_ref, tilde_ref, tilde_t_ref, *refs):
    pieces, out_ref = refs[: 2 * len(steps)], refs[-1]
    slab = total_ref.shape[1] // nz
    for k in range(nz):
        out_ref[k] = blocks_ref[k]
    total = density_pieces(
        steps, nz, width, padded, where_ref, tilde_ref[...], tilde_t_ref, pieces, total_ref[...], out_ref
    )
    for k in range(nz):
        out_ref[k] += total[:, k * slab : (k + 1) * slab]


def local(orbital_b, pair_list, eps_occ, eps_vir):
    slab, naux = orbital_b.shape[1:]
    nvir = eps_vir.shape[0]
    z, yh, c = (lax.axis_index(a) for a in ("z", "yh", "c"))
    nz = lax.axis_size("z")
    width = slab // 4
    padded = (width + 8) // 8 * 8
    where = jnp.stack([z, c, z * 4 + yh * 2 + c, lax.axis_index(SLABS), yh * 2 + c])

    left = orbital_b[pair_list[:, 0]].reshape(8, 2, 2, width, naux)
    left = jnp.pad(left, ((0, 0), (0, 0), (0, 0), (0, padded - width), (0, 0)))
    left = left.reshape(8, 2, 2 * padded, naux).transpose(1, 0, 2, 3)
    right = jnp.broadcast_to(orbital_b[pair_list[:, 1]][None], (2, 8, slab, naux))
    outgoing = jnp.concatenate([left, right], axis=2).reshape(16, 2 * padded + slab, naux)
    near = lax.all_to_all(outgoing, ("yh", "x", "yl"), split_axis=0, concat_axis=0, tiled=True)
    far = swap(near, "c")

    part, denom = pl.pallas_call(
        functools.partial(integral_kernel, padded),
        out_shape=(jax.ShapeDtypeStruct((8 * padded, nvir), F32), jax.ShapeDtypeStruct((padded, nvir), F32)),
        in_specs=[SMEM, SMEM, SMEM, VMEM, VMEM, VMEM],
        out_specs=(VMEM, VMEM),
        compiler_params=PARAMS,
    )(where, pair_list, eps_occ, eps_vir[None], near, far)
    part = part.reshape(8, padded, nvir)

    def own(offset):
        return lax.dynamic_index_in_dim(part, lax.rem(z + offset, nz), 0, keepdims=False)

    cut = padded // 2
    up = shift(own(nz // 2)[:cut], "z", 1)
    down = shift(own(nz // 2)[cut:], "z", -1)
    up = jnp.concatenate([up, jnp.zeros_like(down)])
    down = jnp.concatenate([jnp.zeros_like(down), down])
    for step in range(nz // 2 - 1, 0, -1):
        up = shift(own(step) + up, "z", 1)
        down = shift(own(nz - step) + down, "z", -1)
    amp_rows = (own(0) + (up + down)) / denom

    other = swap(amp_rows, "yh")
    both = jnp.where(yh == 0, jnp.stack([amp_rows, other]), jnp.stack([other, amp_rows]))
    both16 = both.astype(BF16)
    ring = {0: both16}
    up = down = both16
    for step in range(1, nz // 2):
        up = shift(up, "z", 1)
        down = shift(down, "z", -1)
        ring[nz - step] = up
        ring[step] = down
    ring[nz // 2] = jnp.stack([shift(up[0], "z", 1), shift(down[1], "z", -1)])

    both = both.reshape(2 * padded, nvir)
    turned = pl.pallas_call(
        functools.partial(turn_kernel, nz, width, padded),
        out_shape=jax.ShapeDtypeStruct((nz, 2, padded, 2 * padded), F32),
        in_specs=[SMEM, VMEM, VMEM],
        out_specs=VMEM,
        compiler_params=PARAMS,
        cost_estimate=cost(6 * 4 * padded * padded * nvir, 4 * 4 * padded * nvir),
    )(where, both, swap(both, "c"))
    turned = lax.all_to_all(turned, "z", split_axis=0, concat_axis=0, tiled=True)

    def gathered(steps):
        pieces = []
        for r in steps:
            pieces += [ring[r].reshape(2 * padded, nvir), swap(ring[r], "c").reshape(2 * padded, nvir)]
        return pieces

    soon = (0, 1, nz - 1, 2, nz - 2)
    late = (3, nz - 3, nz // 2)
    state = pl.pallas_call(
        functools.partial(early_kernel, soon, nz, width, padded),
        out_shape=(
            jax.ShapeDtypeStruct((padded, nvir), F32),
            jax.ShapeDtypeStruct((nz, padded, slab), F32),
            jax.ShapeDtypeStruct((padded, nvir), BF16),
            jax.ShapeDtypeStruct((nz, 2, padded, 2 * padded), BF16),
        ),
        in_specs=[SMEM] + [VMEM] * (2 + 2 * len(soon)),
        out_specs=(VMEM,) * 4,
        compiler_params=PARAMS,
        cost_estimate=cost(len(soon) * 8 * padded * padded * nvir, len(soon) * 8 * padded * nvir),
    )(where, amp_rows, turned, *gathered(soon))
    added = pl.pallas_call(
        functools.partial(late_kernel, late, nz, width, padded),
        out_shape=jax.ShapeDtypeStruct((nz, padded, slab), F32),
        in_specs=[SMEM] + [VMEM] * (4 + 2 * len(late)),
        out_specs=VMEM,
        compiler_params=PARAMS,
        cost_estimate=cost(len(late) * 8 * padded * padded * nvir, len(late) * 8 * padded * nvir),
    )(where, *state, *gathered(late))
    added = lax.all_to_all(added, SLABS, split_axis=0, concat_axis=0, tiled=True)
    return jnp.sum(added, axis=0)[:width]


def solution(mesh):
    fine = Mesh(mesh.devices.reshape(4, 2, 8, 2, 2), ("x", "yl", "z", "yh", "c"))
    pair, grid = SLABS, ("z", "yh", "c")
    in_specs = (P(None, pair, grid), P(), P(), P())
    return jax.shard_map(local, mesh=fine, in_specs=in_specs, out_specs=P(grid, pair), check_vma=False)
```

```python
import functools

import jax
import jax.numpy as jnp
from jax import lax
from jax.experimental import pallas as pl
from jax.experimental.pallas import tpu as pltpu
from jax.sharding import Mesh
from jax.sharding import PartitionSpec as P

F32 = jnp.float32
BF16 = jnp.bfloat16
SLABS = ("x", "yl")
VMEM = pl.BlockSpec(memory_space=pltpu.VMEM)
SMEM = pl.BlockSpec(memory_space=pltpu.SMEM)


def params(mib):
    return pltpu.CompilerParams(vmem_limit_bytes=mib * 1024 * 1024)


def swap(value, axis):
    return lax.ppermute(value, axis, [(0, 1), (1, 0)])


def shift(value, axis, step):
    size = lax.axis_size(axis)
    return lax.ppermute(value, axis, [(i, (i + step) % size) for i in range(size)])


def dot_nt(a, b):
    return lax.dot_general(a, b, (((1,), (1,)), ((), ())), preferred_element_type=F32)


def split3(value):
    high = value.astype(BF16)
    rest = value - high.astype(F32)
    middle = rest.astype(BF16)
    return high, middle, (rest - middle.astype(F32)).astype(BF16)


def cost(flops, moved):
    return pl.CostEstimate(flops=flops, bytes_accessed=moved, transcendentals=0)


def factor_product(ref, left, padded):
    sources, rows, naux = ref.shape
    half = sources // 2
    slab = rows - 2 * padded
    total = None
    for y in range(2):
        b = ref[half * y : half * (y + 1), 2 * padded :, :].reshape(half * slab, naux)
        term = dot_nt(left(y), b)
        total = term if total is None else total + term
    return total


def all_rows(ref, start, padded):
    half = ref.shape[0] // 2

    def left(y):
        return ref[half * y : half * (y + 1), pl.ds(start, padded), :].reshape(half * padded, ref.shape[2])

    return left


def near_kernel(padded, where_ref, near_ref, out_ref):
    start = pl.multiple_of(where_ref[1] * padded, padded)
    out_ref[...] = factor_product(near_ref, all_rows(near_ref, start, padded), padded).reshape(out_ref.shape)


def first_kernel(padded, where_ref, near_part_ref, far_ref, up_ref, down_ref):
    nz = near_part_ref.shape[0]
    half = far_ref.shape[0] // 2
    start = pl.multiple_of(where_ref[1] * padded, padded)
    at = lax.rem(where_ref[0] + nz // 2, nz)
    total = factor_product(far_ref, lambda y: far_ref[half * y + at, pl.ds(start, padded), :], padded)
    total = total + near_part_ref[at]
    up_ref[...] = total[: padded // 2]
    down_ref[...] = total[padded // 2 :]


def rest_kernel(padded, where_ref, pair_ref, occ_ref, vir_ref, near_part_ref, far_ref, out_ref, denom_ref):
    start = pl.multiple_of(where_ref[1] * padded, padded)
    total = factor_product(far_ref, all_rows(far_ref, start, padded), padded)
    out_ref[...] = near_part_ref[...] + total.reshape(out_ref.shape)
    chunk, group, width = where_ref[2], where_ref[3], where_ref[5]
    columns = jnp.broadcast_to(vir_ref[...], denom_ref.shape)
    place = lax.broadcasted_iota(jnp.int32, denom_ref.shape, 1)
    row = lax.broadcasted_iota(jnp.int32, denom_ref.shape, 0)
    own = jnp.sum(jnp.where(place == chunk * width + row, columns, 0.0), axis=1, keepdims=True)
    denom_ref[...] = (own + columns) - occ_ref[pair_ref[group, 0]] - occ_ref[pair_ref[group, 1]]


def hop_kernel(step, where_ref, part_ref, up_in, down_in, up_ref, down_ref):
    nz, rows = part_ref.shape[:2]
    above = lax.rem(where_ref[0] + step, nz)
    below = lax.rem(where_ref[0] + nz - step, nz)
    taken = up_in.shape[0]
    up_ref[:taken] = part_ref[above, :taken] + up_in[...]
    down_ref[rows - taken :] = part_ref[below, rows - taken :] + down_in[...]
    if taken < rows:
        up_ref[taken:] = part_ref[above, taken:]
        down_ref[: rows - taken] = part_ref[below, : rows - taken]


def amplitude_kernel(where_ref, part_ref, up_in, down_in, denom_ref, out_ref):
    out_ref[...] = (part_ref[where_ref[0]] + (up_in[...] + down_in[...])) / denom_ref[...]


def turn_kernel(nz, width, padded, where_ref, near_ref, far_ref, out_ref):
    part = where_ref[4]
    nvir = near_ref.shape[1]
    slab = nvir // nz
    column = lax.broadcasted_iota(jnp.int32, (padded, slab), 1)
    row = lax.broadcasted_iota(jnp.int32, (padded, slab), 0)
    pick = jnp.where((column == part * width + row) & (row < width), 1.0, 0.0).astype(BF16)
    for slot, ref in enumerate((near_ref, far_ref)):
        for k in range(nz):
            high, middle, low = split3(ref[:, k * slab : (k + 1) * slab])
            out_ref[k, slot] = dot_nt(pick, high) + (dot_nt(pick, middle) + dot_nt(pick, low))


def density_pieces(steps, nz, width, padded, where_ref, tilde, tilde_t_ref, pieces, total, blocks_ref):
    z, c = where_ref[0], where_ref[1]
    for n, r in enumerate(steps):
        at = lax.rem(z + r, nz)
        sides = []
        for slot in range(2):
            piece = pieces[2 * n + slot]
            piece = jnp.concatenate([ref[...] for ref in piece], axis=0) if isinstance(piece, tuple) else piece[...]
            term = jnp.dot(tilde_t_ref[at, slot], piece, preferred_element_type=F32)
            total = term if total is None else total + term
            sides.append(dot_nt(tilde, piece))
        blocks_ref[at] = join(c, sides[0], sides[1], width, padded)
    return total


def join(c, near, far, width, padded):
    first, second = jnp.where(c == 0, near, far), jnp.where(c == 0, far, near)
    parts = []
    for y in range(2):
        for piece in (first, second):
            parts.append(piece[:, y * padded : y * padded + width])
    return jnp.concatenate(parts, axis=1)


def early_kernel(steps, nz, width, padded, where_ref, rows_ref, turned_ref, *refs):
    pieces = refs[: 2 * len(steps)]
    total_ref, blocks_ref, tilde_ref, tilde_t_ref = refs[2 * len(steps) :]
    c = where_ref[1]
    slab = rows_ref.shape[1] // nz
    rows = rows_ref[...]
    zeros = jnp.zeros((padded, padded - width), F32)
    turned = []
    for k in range(nz):
        mine = rows[:, k * slab : (k + 1) * slab]
        halves = []
        for h in range(2):
            parts = []
            for y in range(2):
                at = (2 * y + h) * width
                parts += [mine[:, at : at + width], zeros]
            halves.append(jnp.concatenate(parts, axis=1))
        near, far = turned_ref[k, 0], turned_ref[k, 1]
        tilde_t_ref[k, 0] = (2.0 * near - jnp.where(c == 0, halves[0], halves[1])).astype(BF16)
        tilde_t_ref[k, 1] = (2.0 * far - jnp.where(c == 0, halves[1], halves[0])).astype(BF16)
        turned.append(join(c, near, far, width, padded))
    tilde = (2.0 * rows - jnp.concatenate(turned, axis=1)).astype(BF16)
    tilde_ref[...] = tilde
    total_ref[...] = density_pieces(steps, nz, width, padded, where_ref, tilde, tilde_t_ref, pieces, None, blocks_ref)


def late_kernel(steps, nz, width, padded, where_ref, total_ref, blocks_ref, tilde_ref, tilde_t_ref, *refs):
    pieces, out_ref = list(refs[: 2 * len(steps) - 2]), refs[-1]
    pieces += [refs[-5:-3], refs[-3:-1]]
    slab = total_ref.shape[1] // nz
    for k in range(nz):
        out_ref[k] = blocks_ref[k]
    total = density_pieces(
        steps, nz, width, padded, where_ref, tilde_ref[...], tilde_t_ref, pieces, total_ref[...], out_ref
    )
    for k in range(nz):
        out_ref[k] += total[:, k * slab : (k + 1) * slab]


def local(orbital_b, pair_list, eps_occ, eps_vir):
    slab, naux = orbital_b.shape[1:]
    nvir = eps_vir.shape[0]
    z, yh, c = (lax.axis_index(a) for a in ("z", "yh", "c"))
    nz = lax.axis_size("z")
    width = slab // 4
    padded = (width + 8) // 8 * 8
    where = jnp.stack([z, c, z * 4 + yh * 2 + c, lax.axis_index(SLABS), yh * 2 + c, jnp.int32(width)])

    left = orbital_b[pair_list[:, 0]].reshape(8, 2, 2, width, naux)
    left = jnp.pad(left, ((0, 0), (0, 0), (0, 0), (0, padded - width), (0, 0)))
    left = left.reshape(8, 2, 2 * padded, naux).transpose(1, 0, 2, 3)
    right = jnp.broadcast_to(orbital_b[pair_list[:, 1]][None], (2, 8, slab, naux))
    outgoing = jnp.concatenate([left, right], axis=2).reshape(16, 2 * padded + slab, naux)
    near = lax.all_to_all(outgoing, ("yh", "x", "yl"), split_axis=0, concat_axis=0, tiled=True)
    far = swap(near, "c")

    whole = jax.ShapeDtypeStruct((8, padded, nvir), F32)
    rows = jax.ShapeDtypeStruct((padded, nvir), F32)
    halves = jax.ShapeDtypeStruct((padded // 2, nvir), F32)
    flops = 16 * padded * 8 * slab * 2 * naux
    near_part = pl.pallas_call(
        functools.partial(near_kernel, padded),
        out_shape=whole,
        in_specs=[SMEM, VMEM],
        out_specs=VMEM,
        compiler_params=params(16),
        cost_estimate=cost(flops, 0),
    )(where, near)
    up, down = pl.pallas_call(
        functools.partial(first_kernel, padded),
        out_shape=(halves, halves),
        in_specs=[SMEM, VMEM, VMEM],
        out_specs=(VMEM, VMEM),
        compiler_params=params(16),
        cost_estimate=cost(flops // 8, 0),
    )(where, near_part, far)
    up, down = shift(up, "z", 1), shift(down, "z", -1)
    part, denom = pl.pallas_call(
        functools.partial(rest_kernel, padded),
        out_shape=(whole, rows),
        in_specs=[SMEM, SMEM, SMEM, VMEM, VMEM, VMEM],
        out_specs=(VMEM, VMEM),
        compiler_params=params(20),
        cost_estimate=cost(flops, 0),
    )(where, pair_list, eps_occ, eps_vir[None], near_part, far)
    for step in range(nz // 2 - 1, 0, -1):
        up, down = pl.pallas_call(
            functools.partial(hop_kernel, step),
            out_shape=(rows, rows),
            in_specs=[SMEM, VMEM, VMEM, VMEM],
            out_specs=(VMEM, VMEM),
            compiler_params=params(8),
        )(where, part, up, down)
        up, down = shift(up, "z", 1), shift(down, "z", -1)
    amp_rows = pl.pallas_call(
        amplitude_kernel,
        out_shape=rows,
        in_specs=[SMEM, VMEM, VMEM, VMEM, VMEM],
        out_specs=VMEM,
        compiler_params=params(8),
    )(where, part, up, down, denom)

    other = swap(amp_rows, "yh")
    both = jnp.where(yh == 0, jnp.stack([amp_rows, other]), jnp.stack([other, amp_rows]))
    both16 = both.astype(BF16)
    ring = {0: both16}
    up, down = shift(both16, "z", 1), shift(both16, "z", -1)

    both = both.reshape(2 * padded, nvir)
    turned = pl.pallas_call(
        functools.partial(turn_kernel, nz, width, padded),
        out_shape=jax.ShapeDtypeStruct((nz, 2, padded, 2 * padded), F32),
        in_specs=[SMEM, VMEM, VMEM],
        out_specs=VMEM,
        compiler_params=params(8),
        cost_estimate=cost(6 * 4 * padded * padded * nvir, 4 * 4 * padded * nvir),
    )(where, both, swap(both, "c"))
    up, down, turned = lax.optimization_barrier((up, down, turned))
    turned = lax.all_to_all(turned, "z", split_axis=0, concat_axis=0, tiled=True)
    for step in range(1, nz // 2):
        ring[nz - step] = up
        ring[step] = down
        if step == nz // 2 - 1:
            up, down, turned = lax.optimization_barrier((up, down, turned))
            up, down = shift(up[0], "z", 1), shift(down[1], "z", -1)
        else:
            up, down = shift(up, "z", 1), shift(down, "z", -1)

    def gathered(steps):
        pieces = []
        for r in steps:
            pieces += [ring[r].reshape(2 * padded, nvir), swap(ring[r], "c").reshape(2 * padded, nvir)]
        return pieces

    soon = (0, 1, nz - 1, 2, nz - 2)
    late = (3, nz - 3)
    state = pl.pallas_call(
        functools.partial(early_kernel, soon, nz, width, padded),
        out_shape=(
            jax.ShapeDtypeStruct((padded, nvir), F32),
            jax.ShapeDtypeStruct((nz, padded, slab), F32),
            jax.ShapeDtypeStruct((padded, nvir), BF16),
            jax.ShapeDtypeStruct((nz, 2, padded, 2 * padded), BF16),
        ),
        in_specs=[SMEM] + [VMEM] * (2 + 2 * len(soon)),
        out_specs=(VMEM,) * 4,
        compiler_params=params(16),
        cost_estimate=cost(len(soon) * 8 * padded * padded * nvir, len(soon) * 8 * padded * nvir),
    )(where, amp_rows, turned, *gathered(soon))
    up, down, state = lax.optimization_barrier((up, down, state))
    added = pl.pallas_call(
        functools.partial(late_kernel, (*late, nz // 2), nz, width, padded),
        out_shape=jax.ShapeDtypeStruct((nz, padded, slab), F32),
        in_specs=[SMEM] + [VMEM] * (8 + 2 * len(late)),
        out_specs=VMEM,
        compiler_params=params(16),
        cost_estimate=cost(len(late) * 8 * padded * padded * nvir, len(late) * 8 * padded * nvir),
    )(where, *state, *gathered(late), up, down, swap(up, "c"), swap(down, "c"))
    added = lax.all_to_all(added, SLABS, split_axis=0, concat_axis=0, tiled=True)
    return jnp.sum(added, axis=0)[:width]


def solution(mesh):
    fine = Mesh(mesh.devices.reshape(4, 2, 8, 2, 2), ("x", "yl", "z", "yh", "c"))
    pair, grid = SLABS, ("z", "yh", "c")
    in_specs = (P(None, pair, grid), P(), P(), P())
    return jax.shard_map(local, mesh=fine, in_specs=in_specs, out_specs=P(grid, pair), check_vma=False)
```

```python
import functools

import jax
import jax.numpy as jnp
from jax import lax
from jax.experimental import pallas as pl
from jax.experimental.pallas import tpu as pltpu
from jax.sharding import Mesh
from jax.sharding import PartitionSpec as P

F32 = jnp.float32
BF16 = jnp.bfloat16
SLABS = ("x", "yl")
VMEM = pl.BlockSpec(memory_space=pltpu.VMEM)
SMEM = pl.BlockSpec(memory_space=pltpu.SMEM)


def params(mib):
    return pltpu.CompilerParams(vmem_limit_bytes=mib * 1024 * 1024)


def swap(value, axis):
    return lax.ppermute(value, axis, [(0, 1), (1, 0)])


def shift(value, axis, step):
    size = lax.axis_size(axis)
    return lax.ppermute(value, axis, [(i, (i + step) % size) for i in range(size)])


def dot_nt(a, b):
    return lax.dot_general(a, b, (((1,), (1,)), ((), ())), preferred_element_type=F32)


def cost(flops, moved):
    return pl.CostEstimate(flops=flops, bytes_accessed=moved, transcendentals=0)


def factor_product(ref, left, padded):
    sources, rows, naux = ref.shape
    half = sources // 2
    slab = rows - 2 * padded
    total = None
    for y in range(2):
        b = ref[half * y : half * (y + 1), 2 * padded :, :].reshape(half * slab, naux)
        term = dot_nt(left(y), b)
        total = term if total is None else total + term
    return total


def all_rows(ref, start, padded):
    half = ref.shape[0] // 2

    def left(y):
        return ref[half * y : half * (y + 1), pl.ds(start, padded), :].reshape(half * padded, ref.shape[2])

    return left


def near_kernel(padded, where_ref, near_ref, out_ref):
    start = pl.multiple_of(where_ref[1] * padded, padded)
    out_ref[...] = factor_product(near_ref, all_rows(near_ref, start, padded), padded).reshape(out_ref.shape)


def first_kernel(padded, where_ref, near_part_ref, far_ref, up_ref, down_ref):
    nz = near_part_ref.shape[0]
    half = far_ref.shape[0] // 2
    start = pl.multiple_of(where_ref[1] * padded, padded)
    at = lax.rem(where_ref[0] + nz // 2, nz)
    total = factor_product(far_ref, lambda y: far_ref[half * y + at, pl.ds(start, padded), :], padded)
    total = total + near_part_ref[at]
    up_ref[...] = total[: padded // 2]
    down_ref[...] = total[padded // 2 :]


def rest_kernel(padded, where_ref, pair_ref, occ_ref, vir_ref, near_part_ref, far_ref, out_ref, denom_ref):
    start = pl.multiple_of(where_ref[1] * padded, padded)
    total = factor_product(far_ref, all_rows(far_ref, start, padded), padded)
    out_ref[...] = near_part_ref[...] + total.reshape(out_ref.shape)
    chunk, group, width = where_ref[2], where_ref[3], where_ref[5]
    columns = jnp.broadcast_to(vir_ref[...], denom_ref.shape)
    place = lax.broadcasted_iota(jnp.int32, denom_ref.shape, 1)
    row = lax.broadcasted_iota(jnp.int32, denom_ref.shape, 0)
    own = jnp.sum(jnp.where(place == chunk * width + row, columns, 0.0), axis=1, keepdims=True)
    denom_ref[...] = (own + columns) - occ_ref[pair_ref[group, 0]] - occ_ref[pair_ref[group, 1]]


def hop_kernel(step, where_ref, part_ref, up_in, down_in, up_ref, down_ref):
    nz, rows = part_ref.shape[:2]
    above = lax.rem(where_ref[0] + step, nz)
    below = lax.rem(where_ref[0] + nz - step, nz)
    taken = up_in.shape[0]
    up_ref[:taken] = part_ref[above, :taken] + up_in[...]
    down_ref[rows - taken :] = part_ref[below, rows - taken :] + down_in[...]
    if taken < rows:
        up_ref[taken:] = part_ref[above, taken:]
        down_ref[: rows - taken] = part_ref[below, : rows - taken]


def amplitude_kernel(where_ref, part_ref, up_in, down_in, denom_ref, out_ref, rounded_ref, blocks_ref):
    amps = (part_ref[where_ref[0]] + (up_in[...] + down_in[...])) / denom_ref[...]
    out_ref[...] = amps
    rounded_ref[...] = amps.astype(BF16)
    slab = blocks_ref.shape[2]
    for k in range(blocks_ref.shape[0]):
        blocks_ref[k] = amps[:, k * slab : (k + 1) * slab]


def outward_kernel(where_ref, columns_ref, out_ref):
    half = columns_ref.shape[2] // 2
    for k in range(columns_ref.shape[0]):
        columns = columns_ref[k]
        out_ref[k] = jnp.where(where_ref[6] == 0, columns[:, half:], columns[:, :half])


def inward_kernel(where_ref, columns_ref, other_ref, keep_ref, send_ref):
    c, yh = where_ref[1], where_ref[6]
    half = columns_ref.shape[2] // 2
    width = half // 2
    gap = jnp.zeros((columns_ref.shape[1], keep_ref.shape[2] // 2 - width), F32)
    for k in range(columns_ref.shape[0]):
        columns = columns_ref[k]
        own = jnp.where(yh == 0, columns[:, :half], columns[:, half:])
        other = other_ref[k]
        sides = []
        for h in range(2):
            at = h * width
            sides.append(jnp.concatenate([own[:, at : at + width], gap, other[:, at : at + width], gap], axis=1))
        keep_ref[k] = jnp.where(c == 0, sides[0], sides[1])
        send_ref[k] = jnp.where(c == 0, sides[1], sides[0])


def natural(c, yh, near, far, width, padded):
    parts = []
    for y in range(2):
        for h in range(2):
            side = jnp.where(c == h, near, far)
            parts.append(jnp.where(yh == y, side[:, :width], side[:, padded : padded + width]))
    return jnp.concatenate(parts, axis=1)


def relative(c, yh, block, width, padded):
    gap = jnp.zeros((block.shape[0], padded - width), block.dtype)
    sides = []
    for h in range(2):
        first, second = block[:, h * width : (h + 1) * width], block[:, (2 + h) * width : (3 + h) * width]
        own, other = jnp.where(yh == 0, first, second), jnp.where(yh == 0, second, first)
        sides.append(jnp.concatenate([own, gap, other, gap], axis=1))
    return jnp.where(c == 0, sides[0], sides[1]), jnp.where(c == 0, sides[1], sides[0])


def density_pieces(steps, nz, width, padded, where_ref, tilde, tilde_t_ref, pieces, total, blocks_ref):
    z, c, yh = where_ref[0], where_ref[1], where_ref[6]
    for n, r in enumerate(steps):
        at = lax.rem(z + r, nz)
        sides = []
        for slot in range(2):
            first, second = pieces[4 * n + 2 * slot], pieces[4 * n + 2 * slot + 1]
            piece = jnp.concatenate([first[...], second[...]], axis=0)
            term = jnp.dot(tilde_t_ref[at, slot], piece, preferred_element_type=F32)
            total = term if total is None else total + term
            sides.append(dot_nt(tilde, piece))
        blocks_ref[at] = natural(c, yh, sides[0], sides[1], width, padded)
    return total


def turn(block, padded):
    flipped = block.T
    return jnp.concatenate([flipped[:padded], flipped[padded:]], axis=1)


def early_kernel(steps, nz, width, padded, where_ref, rows_ref, near_ref, far_ref, *refs):
    pieces = refs[: 4 * len(steps)]
    total_ref, blocks_ref, tilde_ref, tilde_t_ref = refs[4 * len(steps) :]
    c, yh = where_ref[1], where_ref[6]
    slab = rows_ref.shape[1] // nz
    rows = rows_ref[...]
    turned = []
    for k in range(nz):
        near, far = turn(near_ref[k], padded), turn(far_ref[k], padded)
        mine = relative(c, yh, rows[:, k * slab : (k + 1) * slab], width, padded)
        tilde_t_ref[k, 0] = (2.0 * near - mine[0]).astype(BF16)
        tilde_t_ref[k, 1] = (2.0 * far - mine[1]).astype(BF16)
        turned.append(natural(c, yh, near, far, width, padded))
    tilde = (2.0 * rows - jnp.concatenate(turned, axis=1)).astype(BF16)
    tilde_ref[...] = tilde
    total_ref[...] = density_pieces(steps, nz, width, padded, where_ref, tilde, tilde_t_ref, pieces, None, blocks_ref)


def late_kernel(steps, nz, width, padded, where_ref, total_ref, blocks_ref, tilde_ref, tilde_t_ref, *refs):
    pieces, out_ref = refs[:-1], refs[-1]
    slab = total_ref.shape[1] // nz
    for k in range(nz):
        out_ref[k] = blocks_ref[k]
    total = density_pieces(
        steps, nz, width, padded, where_ref, tilde_ref[...], tilde_t_ref, pieces, total_ref[...], out_ref
    )
    for k in range(nz):
        out_ref[k] += total[:, k * slab : (k + 1) * slab]


def local(orbital_b, pair_list, eps_occ, eps_vir):
    slab, naux = orbital_b.shape[1:]
    nvir = eps_vir.shape[0]
    z, yh, c = (lax.axis_index(a) for a in ("z", "yh", "c"))
    nz = lax.axis_size("z")
    width = slab // 4
    padded = (width + 8) // 8 * 8
    where = jnp.stack([z, c, z * 4 + yh * 2 + c, lax.axis_index(SLABS), yh * 2 + c, jnp.int32(width), yh])

    left = orbital_b[pair_list[:, 0]].reshape(8, 2, 2, width, naux)
    left = jnp.pad(left, ((0, 0), (0, 0), (0, 0), (0, padded - width), (0, 0)))
    left = left.reshape(8, 2, 2 * padded, naux).transpose(1, 0, 2, 3)
    right = jnp.broadcast_to(orbital_b[pair_list[:, 1]][None], (2, 8, slab, naux))
    outgoing = jnp.concatenate([left, right], axis=2).reshape(16, 2 * padded + slab, naux)
    near = lax.all_to_all(outgoing, ("yh", "x", "yl"), split_axis=0, concat_axis=0, tiled=True)
    far = swap(near, "c")

    whole = jax.ShapeDtypeStruct((8, padded, nvir), F32)
    rows = jax.ShapeDtypeStruct((padded, nvir), F32)
    halves = jax.ShapeDtypeStruct((padded // 2, nvir), F32)
    flops = 16 * padded * 8 * slab * 2 * naux
    near_part = pl.pallas_call(
        functools.partial(near_kernel, padded),
        out_shape=whole,
        in_specs=[SMEM, VMEM],
        out_specs=VMEM,
        compiler_params=params(16),
        cost_estimate=cost(flops, 0),
    )(where, near)
    up, down = pl.pallas_call(
        functools.partial(first_kernel, padded),
        out_shape=(halves, halves),
        in_specs=[SMEM, VMEM, VMEM],
        out_specs=(VMEM, VMEM),
        compiler_params=params(16),
        cost_estimate=cost(flops // 8, 0),
    )(where, near_part, far)
    up, down = shift(up, "z", 1), shift(down, "z", -1)
    part, denom = pl.pallas_call(
        functools.partial(rest_kernel, padded),
        out_shape=(whole, rows),
        in_specs=[SMEM, SMEM, SMEM, VMEM, VMEM, VMEM],
        out_specs=(VMEM, VMEM),
        compiler_params=params(20),
        cost_estimate=cost(flops, 0),
    )(where, pair_list, eps_occ, eps_vir[None], near_part, far)
    for step in range(nz // 2 - 1, 0, -1):
        up, down = pl.pallas_call(
            functools.partial(hop_kernel, step),
            out_shape=(rows, rows),
            in_specs=[SMEM, VMEM, VMEM, VMEM],
            out_specs=(VMEM, VMEM),
            compiler_params=params(8),
        )(where, part, up, down)
        up, down = shift(up, "z", 1), shift(down, "z", -1)
    rows16 = jax.ShapeDtypeStruct((padded, nvir), BF16)
    amp_rows, mine, columns = pl.pallas_call(
        amplitude_kernel,
        out_shape=(rows, rows16, jax.ShapeDtypeStruct((nz, padded, slab), F32)),
        in_specs=[SMEM, VMEM, VMEM, VMEM, VMEM],
        out_specs=(VMEM,) * 3,
        compiler_params=params(8),
    )(where, part, up, down, denom)

    mine = (mine, swap(mine, "yh"))
    columns = lax.all_to_all(columns, "z", split_axis=0, concat_axis=0, tiled=True)
    outward = pl.pallas_call(
        outward_kernel,
        out_shape=jax.ShapeDtypeStruct((nz, padded, slab // 2), F32),
        in_specs=[SMEM, VMEM],
        out_specs=VMEM,
        compiler_params=params(8),
    )(where, columns)
    ring = {0: mine}
    up = down = mine
    for step in range(1, nz // 2 - 1):
        up, down = tuple(shift(v, "z", 1) for v in up), tuple(shift(v, "z", -1) for v in down)
        ring[nz - step], ring[step] = up, down
    up, down, outward = lax.optimization_barrier((up, down, outward))
    other = swap(outward, "yh")
    kept, sent = pl.pallas_call(
        inward_kernel,
        out_shape=(jax.ShapeDtypeStruct((nz, padded, 2 * padded), F32),) * 2,
        in_specs=[SMEM, VMEM, VMEM],
        out_specs=(VMEM, VMEM),
        compiler_params=params(8),
    )(where, columns, other)
    taken = swap(sent, "c")
    last = (tuple(shift(v, "z", -1) for v in down), tuple(shift(v, "z", 1) for v in up))
    last += ((shift(up[0], "z", 2), shift(down[1], "z", -2)),)

    def crossed(pieces):
        return [v for piece in pieces for v in (*piece, *(swap(v, "c") for v in piece))]

    soon = (0, 1, nz - 1, 2, nz - 2)
    late = (3, nz - 3, nz // 2)
    state = pl.pallas_call(
        functools.partial(early_kernel, soon, nz, width, padded),
        out_shape=(
            rows,
            jax.ShapeDtypeStruct((nz, padded, slab), F32),
            rows16,
            jax.ShapeDtypeStruct((nz, 2, padded, 2 * padded), BF16),
        ),
        in_specs=[SMEM] + [VMEM] * (3 + 4 * len(soon)),
        out_specs=(VMEM,) * 4,
        compiler_params=params(16),
        cost_estimate=cost(len(soon) * 8 * padded * padded * nvir, len(soon) * 8 * padded * nvir),
    )(where, amp_rows, kept, taken, *crossed(ring[r] for r in soon))
    last, state = lax.optimization_barrier((last, state))
    added = pl.pallas_call(
        functools.partial(late_kernel, late, nz, width, padded),
        out_shape=jax.ShapeDtypeStruct((nz, padded, slab), F32),
        in_specs=[SMEM] + [VMEM] * (4 + 4 * len(late)),
        out_specs=VMEM,
        compiler_params=params(16),
        cost_estimate=cost(len(late) * 8 * padded * padded * nvir, len(late) * 8 * padded * nvir),
    )(where, *state, *crossed(last))
    added = lax.all_to_all(added, SLABS, split_axis=0, concat_axis=0, tiled=True)
    return jnp.sum(added, axis=0)[:width]


def solution(mesh):
    fine = Mesh(mesh.devices.reshape(4, 2, 8, 2, 2), ("x", "yl", "z", "yh", "c"))
    pair, grid = SLABS, ("z", "yh", "c")
    in_specs = (P(None, pair, grid), P(), P(), P())
    return jax.shard_map(local, mesh=fine, in_specs=in_specs, out_specs=P(grid, pair), check_vma=False)
```

```python
import functools

import jax
import jax.numpy as jnp
from jax import lax
from jax.experimental import pallas as pl
from jax.experimental.pallas import tpu as pltpu
from jax.sharding import Mesh
from jax.sharding import PartitionSpec as P

F32 = jnp.float32
BF16 = jnp.bfloat16
SLABS = ("x", "yl")
VMEM = pl.BlockSpec(memory_space=pltpu.VMEM)
SMEM = pl.BlockSpec(memory_space=pltpu.SMEM)


def params(mib):
    return pltpu.CompilerParams(vmem_limit_bytes=mib * 1024 * 1024)


def swap(value, axis):
    return lax.ppermute(value, axis, [(0, 1), (1, 0)])


def shift(value, axis, step):
    size = lax.axis_size(axis)
    return lax.ppermute(value, axis, [(i, (i + step) % size) for i in range(size)])


def dot_nt(a, b):
    return lax.dot_general(a, b, (((1,), (1,)), ((), ())), preferred_element_type=F32)


def cost(flops, moved):
    return pl.CostEstimate(flops=flops, bytes_accessed=moved, transcendentals=0)


def factor_product(ref, left, padded):
    sources, rows, naux = ref.shape
    half = sources // 2
    slab = rows - 2 * padded
    total = None
    for y in range(2):
        b = ref[half * y : half * (y + 1), 2 * padded :, :].reshape(half * slab, naux)
        term = dot_nt(left(y), b)
        total = term if total is None else total + term
    return total


def all_rows(ref, start, padded):
    half = ref.shape[0] // 2

    def left(y):
        return ref[half * y : half * (y + 1), pl.ds(start, padded), :].reshape(half * padded, ref.shape[2])

    return left


def near_kernel(padded, where_ref, near_ref, out_ref):
    start = pl.multiple_of(where_ref[1] * padded, padded)
    out_ref[...] = factor_product(near_ref, all_rows(near_ref, start, padded), padded).reshape(out_ref.shape)


def first_kernel(padded, where_ref, near_part_ref, far_ref, up_ref, down_ref):
    nz = near_part_ref.shape[0]
    half = far_ref.shape[0] // 2
    start = pl.multiple_of(where_ref[1] * padded, padded)
    at = lax.rem(where_ref[0] + nz // 2, nz)
    total = factor_product(far_ref, lambda y: far_ref[half * y + at, pl.ds(start, padded), :], padded)
    total = total + near_part_ref[at]
    up_ref[...] = total[: padded // 2]
    down_ref[...] = total[padded // 2 :]


def rest_kernel(padded, where_ref, pair_ref, occ_ref, vir_ref, near_part_ref, far_ref, out_ref, denom_ref):
    start = pl.multiple_of(where_ref[1] * padded, padded)
    total = factor_product(far_ref, all_rows(far_ref, start, padded), padded)
    out_ref[...] = near_part_ref[...] + total.reshape(out_ref.shape)
    chunk, group, width = where_ref[2], where_ref[3], where_ref[5]
    columns = jnp.broadcast_to(vir_ref[...], denom_ref.shape)
    place = lax.broadcasted_iota(jnp.int32, denom_ref.shape, 1)
    row = lax.broadcasted_iota(jnp.int32, denom_ref.shape, 0)
    own = jnp.sum(jnp.where(place == chunk * width + row, columns, 0.0), axis=1, keepdims=True)
    denom_ref[...] = (own + columns) - occ_ref[pair_ref[group, 0]] - occ_ref[pair_ref[group, 1]]


def hop_kernel(step, where_ref, part_ref, up_in, down_in, up_ref, down_ref):
    nz, rows = part_ref.shape[:2]
    above = lax.rem(where_ref[0] + step, nz)
    below = lax.rem(where_ref[0] + nz - step, nz)
    taken = up_in.shape[0]
    up_ref[:taken] = part_ref[above, :taken] + up_in[...]
    down_ref[rows - taken :] = part_ref[below, rows - taken :] + down_in[...]
    if taken < rows:
        up_ref[taken:] = part_ref[above, taken:]
        down_ref[: rows - taken] = part_ref[below, : rows - taken]


def amplitude_kernel(where_ref, part_ref, up_in, down_in, denom_ref, out_ref, rounded_ref):
    amps = (part_ref[where_ref[0]] + (up_in[...] + down_in[...])) / denom_ref[...]
    out_ref[...] = amps
    rounded_ref[...] = amps.astype(BF16)


def blocks_kernel(rows_ref, after_ref, blocks_ref):
    slab = blocks_ref.shape[2]
    for k in range(blocks_ref.shape[0]):
        blocks_ref[k] = rows_ref[:, k * slab : (k + 1) * slab]


def halves_kernel(up_ref, down_ref, first_ref, second_ref):
    first_ref[...] = up_ref[: first_ref.shape[0]]
    second_ref[...] = down_ref[first_ref.shape[0] :]


def outward_kernel(where_ref, columns_ref, out_ref):
    half = columns_ref.shape[2] // 2
    for k in range(columns_ref.shape[0]):
        columns = columns_ref[k]
        out_ref[k] = jnp.where(where_ref[6] == 0, columns[:, half:], columns[:, :half])


def inward_kernel(where_ref, columns_ref, other_ref, keep_ref, send_ref):
    c, yh = where_ref[1], where_ref[6]
    half = columns_ref.shape[2] // 2
    width = half // 2
    gap = jnp.zeros((columns_ref.shape[1], keep_ref.shape[2] // 2 - width), F32)
    for k in range(columns_ref.shape[0]):
        columns = columns_ref[k]
        own = jnp.where(yh == 0, columns[:, :half], columns[:, half:])
        other = other_ref[k]
        sides = []
        for h in range(2):
            at = h * width
            sides.append(jnp.concatenate([own[:, at : at + width], gap, other[:, at : at + width], gap], axis=1))
        keep_ref[k] = jnp.where(c == 0, sides[0], sides[1])
        send_ref[k] = jnp.where(c == 0, sides[1], sides[0])


def natural(c, yh, near, far, width, padded):
    parts = []
    for y in range(2):
        for h in range(2):
            side = jnp.where(c == h, near, far)
            parts.append(jnp.where(yh == y, side[:, :width], side[:, padded : padded + width]))
    return jnp.concatenate(parts, axis=1)


def relative(c, yh, block, width, padded):
    gap = jnp.zeros((block.shape[0], padded - width), block.dtype)
    sides = []
    for h in range(2):
        first, second = block[:, h * width : (h + 1) * width], block[:, (2 + h) * width : (3 + h) * width]
        own, other = jnp.where(yh == 0, first, second), jnp.where(yh == 0, second, first)
        sides.append(jnp.concatenate([own, gap, other, gap], axis=1))
    return jnp.where(c == 0, sides[0], sides[1]), jnp.where(c == 0, sides[1], sides[0])


def density_pieces(steps, nz, width, padded, where_ref, tilde, tilde_t_ref, pieces, total, blocks_ref):
    z, c, yh = where_ref[0], where_ref[1], where_ref[6]
    pieces = list(pieces)
    for r in steps:
        at = lax.rem(z + r, nz)
        sides = []
        for slot in range(2):
            piece = pieces.pop(0)[...]
            if piece.shape[0] == padded:
                piece = jnp.concatenate([piece, pieces.pop(0)[...]], axis=0)
            term = jnp.dot(tilde_t_ref[at, slot], piece, preferred_element_type=F32)
            total = term if total is None else total + term
            sides.append(dot_nt(tilde, piece))
        blocks_ref[at] = natural(c, yh, sides[0], sides[1], width, padded)
    return total


def turn(block, padded):
    flipped = block.T
    return jnp.concatenate([flipped[:padded], flipped[padded:]], axis=1)


def early_kernel(steps, nz, width, padded, where_ref, rows_ref, near_ref, far_ref, *refs):
    pieces = refs[:-4]
    total_ref, blocks_ref, tilde_ref, tilde_t_ref = refs[-4:]
    c, yh = where_ref[1], where_ref[6]
    slab = rows_ref.shape[1] // nz
    rows = rows_ref[...]
    turned = []
    for k in range(nz):
        near, far = turn(near_ref[k], padded), turn(far_ref[k], padded)
        mine = relative(c, yh, rows[:, k * slab : (k + 1) * slab], width, padded)
        tilde_t_ref[k, 0] = (2.0 * near - mine[0]).astype(BF16)
        tilde_t_ref[k, 1] = (2.0 * far - mine[1]).astype(BF16)
        turned.append(natural(c, yh, near, far, width, padded))
    tilde = (2.0 * rows - jnp.concatenate(turned, axis=1)).astype(BF16)
    tilde_ref[...] = tilde
    total_ref[...] = density_pieces(steps, nz, width, padded, where_ref, tilde, tilde_t_ref, pieces, None, blocks_ref)


def late_kernel(steps, nz, width, padded, where_ref, total_ref, blocks_ref, tilde_ref, tilde_t_ref, *refs):
    pieces, out_ref = refs[:-1], refs[-1]
    slab = total_ref.shape[1] // nz
    for k in range(nz):
        out_ref[k] = blocks_ref[k]
    total = density_pieces(
        steps, nz, width, padded, where_ref, tilde_ref[...], tilde_t_ref, pieces, total_ref[...], out_ref
    )
    for k in range(nz):
        out_ref[k] += total[:, k * slab : (k + 1) * slab]


def local(orbital_b, pair_list, eps_occ, eps_vir):
    slab, naux = orbital_b.shape[1:]
    nvir = eps_vir.shape[0]
    z, yh, c = (lax.axis_index(a) for a in ("z", "yh", "c"))
    nz = lax.axis_size("z")
    width = slab // 4
    padded = (width + 8) // 8 * 8
    where = jnp.stack([z, c, z * 4 + yh * 2 + c, lax.axis_index(SLABS), yh * 2 + c, jnp.int32(width), yh])

    left = orbital_b[pair_list[:, 0]].reshape(8, 2, 2, width, naux)
    left = jnp.pad(left, ((0, 0), (0, 0), (0, 0), (0, padded - width), (0, 0)))
    left = left.reshape(8, 2, 2 * padded, naux).transpose(1, 0, 2, 3)
    right = jnp.broadcast_to(orbital_b[pair_list[:, 1]][None], (2, 8, slab, naux))
    outgoing = jnp.concatenate([left, right], axis=2).reshape(16, 2 * padded + slab, naux)
    near = lax.all_to_all(outgoing, ("yh", "x", "yl"), split_axis=0, concat_axis=0, tiled=True)
    far = swap(near, "c")

    whole = jax.ShapeDtypeStruct((8, padded, nvir), F32)
    rows = jax.ShapeDtypeStruct((padded, nvir), F32)
    halves = jax.ShapeDtypeStruct((padded // 2, nvir), F32)
    flops = 16 * padded * 8 * slab * 2 * naux
    near_part = pl.pallas_call(
        functools.partial(near_kernel, padded),
        out_shape=whole,
        in_specs=[SMEM, VMEM],
        out_specs=VMEM,
        compiler_params=params(16),
        cost_estimate=cost(flops, 0),
    )(where, near)
    up, down = pl.pallas_call(
        functools.partial(first_kernel, padded),
        out_shape=(halves, halves),
        in_specs=[SMEM, VMEM, VMEM],
        out_specs=(VMEM, VMEM),
        compiler_params=params(16),
        cost_estimate=cost(flops // 8, 0),
    )(where, near_part, far)
    up, down = shift(up, "z", 1), shift(down, "z", -1)
    part, denom = pl.pallas_call(
        functools.partial(rest_kernel, padded),
        out_shape=(whole, rows),
        in_specs=[SMEM, SMEM, SMEM, VMEM, VMEM, VMEM],
        out_specs=(VMEM, VMEM),
        compiler_params=params(20),
        cost_estimate=cost(flops, 0),
    )(where, pair_list, eps_occ, eps_vir[None], near_part, far)
    for step in range(nz // 2 - 1, 0, -1):
        up, down = pl.pallas_call(
            functools.partial(hop_kernel, step),
            out_shape=(rows, rows),
            in_specs=[SMEM, VMEM, VMEM, VMEM],
            out_specs=(VMEM, VMEM),
            compiler_params=params(8),
        )(where, part, up, down)
        up, down = shift(up, "z", 1), shift(down, "z", -1)
    rows16 = jax.ShapeDtypeStruct((padded, nvir), BF16)
    amp_rows, mine = pl.pallas_call(
        amplitude_kernel,
        out_shape=(rows, rows16),
        in_specs=[SMEM, VMEM, VMEM, VMEM, VMEM],
        out_specs=(VMEM, VMEM),
        compiler_params=params(8),
    )(where, part, up, down, denom)

    other = swap(mine, "yh")
    mine_far = swap(mine, "c")
    columns = pl.pallas_call(
        blocks_kernel,
        out_shape=jax.ShapeDtypeStruct((nz, padded, slab), F32),
        in_specs=[VMEM, VMEM],
        out_specs=VMEM,
        compiler_params=params(8),
    )(amp_rows, mine_far)
    columns = lax.all_to_all(columns, "z", split_axis=0, concat_axis=0, tiled=True)
    both = jnp.concatenate([mine, other])
    outward = pl.pallas_call(
        outward_kernel,
        out_shape=jax.ShapeDtypeStruct((nz, padded, slab // 2), F32),
        in_specs=[SMEM, VMEM],
        out_specs=VMEM,
        compiler_params=params(8),
    )(where, columns)
    ring = {}
    up = down = both
    for step in range(1, nz // 2 - 1):
        up, down = shift(up, "z", 1), shift(down, "z", -1)
        ring[nz - step], ring[step] = up, down
    far = {r: swap(ring[r], "c") for r in (1, nz - 1)}
    outward, other_far = swap(outward, "yh"), swap(other, "c")
    up, down, outward, far, other_far = lax.optimization_barrier((up, down, outward, far, other_far))
    kept, sent = pl.pallas_call(
        inward_kernel,
        out_shape=(jax.ShapeDtypeStruct((nz, padded, 2 * padded), F32),) * 2,
        in_specs=[SMEM, VMEM, VMEM],
        out_specs=(VMEM, VMEM),
        compiler_params=params(8),
    )(where, columns, outward)
    taken = swap(sent, "c")
    half = jax.ShapeDtypeStruct((padded, nvir), BF16)
    half_up, half_down = pl.pallas_call(
        halves_kernel,
        out_shape=(half, half),
        in_specs=[VMEM, VMEM],
        out_specs=(VMEM, VMEM),
        compiler_params=params(8),
    )(up, down)
    last = (shift(down, "z", -1), shift(up, "z", 1), shift(half_up, "z", 2), shift(half_down, "z", -2))

    soon = (0, 1, nz - 1, 2, nz - 2)
    late = (3, nz - 3, nz // 2)
    far.update({r: swap(ring[r], "c") for r in (2, nz - 2)})
    pieces = [v for r in soon[1:] for v in (ring[r], far[r])]
    state = pl.pallas_call(
        functools.partial(early_kernel, soon, nz, width, padded),
        out_shape=(
            rows,
            jax.ShapeDtypeStruct((nz, padded, slab), F32),
            rows16,
            jax.ShapeDtypeStruct((nz, 2, padded, 2 * padded), BF16),
        ),
        in_specs=[SMEM] + [VMEM] * (4 + 2 * len(soon)),
        out_specs=(VMEM,) * 4,
        compiler_params=params(16),
        cost_estimate=cost(len(soon) * 8 * padded * padded * nvir, len(soon) * 8 * padded * nvir),
    )(where, amp_rows, kept, taken, both, mine_far, other_far, *pieces)
    last, state = lax.optimization_barrier((last, state))
    added = pl.pallas_call(
        functools.partial(late_kernel, late, nz, width, padded),
        out_shape=jax.ShapeDtypeStruct((nz, padded, slab), F32),
        in_specs=[SMEM] + [VMEM] * (6 + 2 * len(late)),
        out_specs=VMEM,
        compiler_params=params(16),
        cost_estimate=cost(len(late) * 8 * padded * padded * nvir, len(late) * 8 * padded * nvir),
    )(
        where,
        *state,
        last[0],
        swap(last[0], "c"),
        last[1],
        swap(last[1], "c"),
        last[2],
        last[3],
        swap(last[2], "c"),
        swap(last[3], "c"),
    )
    added = lax.all_to_all(added, SLABS, split_axis=0, concat_axis=0, tiled=True)
    return jnp.sum(added, axis=0)[:width]


def solution(mesh):
    fine = Mesh(mesh.devices.reshape(4, 2, 8, 2, 2), ("x", "yl", "z", "yh", "c"))
    pair, grid = SLABS, ("z", "yh", "c")
    in_specs = (P(None, pair, grid), P(), P(), P())
    return jax.shard_map(local, mesh=fine, in_specs=in_specs, out_specs=P(grid, pair), check_vma=False)
```

```python
import functools

import jax
import jax.numpy as jnp
from jax import lax
from jax.experimental import pallas as pl
from jax.experimental.pallas import tpu as pltpu
from jax.sharding import Mesh
from jax.sharding import PartitionSpec as P

F32 = jnp.float32
BF16 = jnp.bfloat16
SLABS = ("x", "yl")
VMEM = pl.BlockSpec(memory_space=pltpu.VMEM)
SMEM = pl.BlockSpec(memory_space=pltpu.SMEM)


def params(mib):
    return pltpu.CompilerParams(vmem_limit_bytes=mib * 1024 * 1024)


def swap(value, axis):
    return lax.ppermute(value, axis, [(0, 1), (1, 0)])


def shift(value, axis, step):
    size = lax.axis_size(axis)
    return lax.ppermute(value, axis, [(i, (i + step) % size) for i in range(size)])


def dot_nt(a, b):
    return lax.dot_general(a, b, (((1,), (1,)), ((), ())), preferred_element_type=F32)


def cost(flops, moved):
    return pl.CostEstimate(flops=flops, bytes_accessed=moved, transcendentals=0)


def factor_product(ref, left, padded):
    sources, rows, naux = ref.shape
    half = sources // 2
    slab = rows - 2 * padded
    total = None
    for y in range(2):
        b = ref[half * y : half * (y + 1), 2 * padded :, :].reshape(half * slab, naux)
        term = dot_nt(left(y), b)
        total = term if total is None else total + term
    return total


def all_rows(ref, start, padded):
    half = ref.shape[0] // 2

    def left(y):
        return ref[half * y : half * (y + 1), pl.ds(start, padded), :].reshape(half * padded, ref.shape[2])

    return left


def near_kernel(padded, where_ref, near_ref, out_ref):
    start = pl.multiple_of(where_ref[1] * padded, padded)
    out_ref[...] = factor_product(near_ref, all_rows(near_ref, start, padded), padded).reshape(out_ref.shape)


def first_kernel(padded, where_ref, near_part_ref, far_ref, up_ref, down_ref):
    nz = near_part_ref.shape[0]
    half = far_ref.shape[0] // 2
    start = pl.multiple_of(where_ref[1] * padded, padded)
    at = lax.rem(where_ref[0] + nz // 2, nz)
    total = factor_product(far_ref, lambda y: far_ref[half * y + at, pl.ds(start, padded), :], padded)
    total = total + near_part_ref[at]
    up_ref[...] = total[: padded // 2]
    down_ref[...] = total[padded // 2 :]


def rest_kernel(padded, where_ref, pair_ref, occ_ref, vir_ref, near_part_ref, far_ref, out_ref, denom_ref):
    start = pl.multiple_of(where_ref[1] * padded, padded)
    total = factor_product(far_ref, all_rows(far_ref, start, padded), padded)
    out_ref[...] = near_part_ref[...] + total.reshape(out_ref.shape)
    chunk, group, width = where_ref[2], where_ref[3], where_ref[5]
    columns = jnp.broadcast_to(vir_ref[...], denom_ref.shape)
    place = lax.broadcasted_iota(jnp.int32, denom_ref.shape, 1)
    row = lax.broadcasted_iota(jnp.int32, denom_ref.shape, 0)
    own = jnp.sum(jnp.where(place == chunk * width + row, columns, 0.0), axis=1, keepdims=True)
    denom_ref[...] = (own + columns) - occ_ref[pair_ref[group, 0]] - occ_ref[pair_ref[group, 1]]


def hop_kernel(step, where_ref, part_ref, up_in, down_in, up_ref, down_ref):
    nz, rows = part_ref.shape[:2]
    above = lax.rem(where_ref[0] + step, nz)
    below = lax.rem(where_ref[0] + nz - step, nz)
    taken = up_in.shape[0]
    up_ref[:taken] = part_ref[above, :taken] + up_in[...]
    down_ref[rows - taken :] = part_ref[below, rows - taken :] + down_in[...]
    if taken < rows:
        up_ref[taken:] = part_ref[above, taken:]
        down_ref[: rows - taken] = part_ref[below, : rows - taken]


def amplitude_kernel(where_ref, part_ref, up_in, down_in, denom_ref, out_ref, rounded_ref):
    amps = (part_ref[where_ref[0]] + (up_in[...] + down_in[...])) / denom_ref[...]
    out_ref[...] = amps
    rounded_ref[...] = amps.astype(BF16)


def blocks_kernel(rows_ref, blocks_ref):
    slab = blocks_ref.shape[2]
    for k in range(blocks_ref.shape[0]):
        blocks_ref[k] = rows_ref[:, k * slab : (k + 1) * slab]


def halves_kernel(up_ref, down_ref, first_ref, second_ref):
    first_ref[...] = up_ref[: first_ref.shape[0]]
    second_ref[...] = down_ref[first_ref.shape[0] :]


def outward_kernel(where_ref, columns_ref, out_ref):
    half = columns_ref.shape[2] // 2
    for k in range(columns_ref.shape[0]):
        columns = columns_ref[k]
        out_ref[k] = jnp.where(where_ref[6] == 0, columns[:, half:], columns[:, :half])


def inward_kernel(where_ref, columns_ref, other_ref, keep_ref, send_ref):
    c, yh = where_ref[1], where_ref[6]
    half = columns_ref.shape[2] // 2
    width = half // 2
    gap = jnp.zeros((columns_ref.shape[1], keep_ref.shape[2] // 2 - width), F32)
    for k in range(columns_ref.shape[0]):
        columns = columns_ref[k]
        own = jnp.where(yh == 0, columns[:, :half], columns[:, half:])
        other = other_ref[k]
        sides = []
        for h in range(2):
            at = h * width
            sides.append(jnp.concatenate([own[:, at : at + width], gap, other[:, at : at + width], gap], axis=1))
        keep_ref[k] = jnp.where(c == 0, sides[0], sides[1])
        send_ref[k] = jnp.where(c == 0, sides[1], sides[0])


def natural(c, yh, near, far, width, padded):
    parts = []
    for y in range(2):
        for h in range(2):
            side = jnp.where(c == h, near, far)
            parts.append(jnp.where(yh == y, side[:, :width], side[:, padded : padded + width]))
    return jnp.concatenate(parts, axis=1)


def relative(c, yh, block, width, padded):
    gap = jnp.zeros((block.shape[0], padded - width), block.dtype)
    sides = []
    for h in range(2):
        first, second = block[:, h * width : (h + 1) * width], block[:, (2 + h) * width : (3 + h) * width]
        own, other = jnp.where(yh == 0, first, second), jnp.where(yh == 0, second, first)
        sides.append(jnp.concatenate([own, gap, other, gap], axis=1))
    return jnp.where(c == 0, sides[0], sides[1]), jnp.where(c == 0, sides[1], sides[0])


def density_pieces(steps, nz, width, padded, where_ref, tilde, tilde_t_ref, pieces, total, blocks_ref):
    z, c, yh = where_ref[0], where_ref[1], where_ref[6]
    pieces = list(pieces)
    for r in steps:
        at = lax.rem(z + r, nz)
        sides = []
        for slot in range(2):
            piece = pieces.pop(0)[...]
            if piece.shape[0] == padded:
                piece = jnp.concatenate([piece, pieces.pop(0)[...]], axis=0)
            term = jnp.dot(tilde_t_ref[at, slot], piece, preferred_element_type=F32)
            total = term if total is None else total + term
            sides.append(dot_nt(tilde, piece))
        blocks_ref[at] = natural(c, yh, sides[0], sides[1], width, padded)
    return total


def turn(block, padded):
    flipped = block.T
    return jnp.concatenate([flipped[:padded], flipped[padded:]], axis=1)


def early_kernel(steps, nz, width, padded, where_ref, rows_ref, near_ref, far_ref, *refs):
    pieces = refs[:-4]
    total_ref, blocks_ref, tilde_ref, tilde_t_ref = refs[-4:]
    c, yh = where_ref[1], where_ref[6]
    slab = rows_ref.shape[1] // nz
    rows = rows_ref[...]
    turned = []
    for k in range(nz):
        near, far = turn(near_ref[k], padded), turn(far_ref[k], padded)
        mine = relative(c, yh, rows[:, k * slab : (k + 1) * slab], width, padded)
        tilde_t_ref[k, 0] = (2.0 * near - mine[0]).astype(BF16)
        tilde_t_ref[k, 1] = (2.0 * far - mine[1]).astype(BF16)
        turned.append(natural(c, yh, near, far, width, padded))
    tilde = (2.0 * rows - jnp.concatenate(turned, axis=1)).astype(BF16)
    tilde_ref[...] = tilde
    total_ref[...] = density_pieces(steps, nz, width, padded, where_ref, tilde, tilde_t_ref, pieces, None, blocks_ref)


def late_kernel(steps, nz, width, padded, where_ref, total_ref, blocks_ref, tilde_ref, tilde_t_ref, *refs):
    pieces, out_ref = refs[:-1], refs[-1]
    slab = total_ref.shape[1] // nz
    for k in range(nz):
        out_ref[k] = blocks_ref[k]
    total = density_pieces(
        steps, nz, width, padded, where_ref, tilde_ref[...], tilde_t_ref, pieces, total_ref[...], out_ref
    )
    for k in range(nz):
        out_ref[k] += total[:, k * slab : (k + 1) * slab]


def local(orbital_b, pair_list, eps_occ, eps_vir):
    slab, naux = orbital_b.shape[1:]
    nvir = eps_vir.shape[0]
    z, yh, c = (lax.axis_index(a) for a in ("z", "yh", "c"))
    nz = lax.axis_size("z")
    width = slab // 4
    padded = (width + 8) // 8 * 8
    where = jnp.stack([z, c, z * 4 + yh * 2 + c, lax.axis_index(SLABS), yh * 2 + c, jnp.int32(width), yh])

    left = orbital_b[pair_list[:, 0]].reshape(8, 2, 2, width, naux)
    left = jnp.pad(left, ((0, 0), (0, 0), (0, 0), (0, padded - width), (0, 0)))
    left = left.reshape(8, 2, 2 * padded, naux).transpose(1, 0, 2, 3)
    right = jnp.broadcast_to(orbital_b[pair_list[:, 1]][None], (2, 8, slab, naux))
    outgoing = jnp.concatenate([left, right], axis=2).reshape(16, 2 * padded + slab, naux)
    near = lax.all_to_all(outgoing, ("yh", "x", "yl"), split_axis=0, concat_axis=0, tiled=True)
    far = swap(near, "c")

    whole = jax.ShapeDtypeStruct((8, padded, nvir), F32)
    rows = jax.ShapeDtypeStruct((padded, nvir), F32)
    halves = jax.ShapeDtypeStruct((padded // 2, nvir), F32)
    flops = 16 * padded * 8 * slab * 2 * naux
    near_part = pl.pallas_call(
        functools.partial(near_kernel, padded),
        out_shape=whole,
        in_specs=[SMEM, VMEM],
        out_specs=VMEM,
        compiler_params=params(16),
        cost_estimate=cost(flops, 0),
    )(where, near)
    up, down = pl.pallas_call(
        functools.partial(first_kernel, padded),
        out_shape=(halves, halves),
        in_specs=[SMEM, VMEM, VMEM],
        out_specs=(VMEM, VMEM),
        compiler_params=params(16),
        cost_estimate=cost(flops // 8, 0),
    )(where, near_part, far)
    up, down = shift(up, "z", 1), shift(down, "z", -1)
    part, denom = pl.pallas_call(
        functools.partial(rest_kernel, padded),
        out_shape=(whole, rows),
        in_specs=[SMEM, SMEM, SMEM, VMEM, VMEM, VMEM],
        out_specs=(VMEM, VMEM),
        compiler_params=params(20),
        cost_estimate=cost(flops, 0),
    )(where, pair_list, eps_occ, eps_vir[None], near_part, far)
    for step in range(nz // 2 - 1, 0, -1):
        up, down = pl.pallas_call(
            functools.partial(hop_kernel, step),
            out_shape=(rows, rows),
            in_specs=[SMEM, VMEM, VMEM, VMEM],
            out_specs=(VMEM, VMEM),
            compiler_params=params(8),
        )(where, part, up, down)
        up, down = shift(up, "z", 1), shift(down, "z", -1)
    rows16 = jax.ShapeDtypeStruct((padded, nvir), BF16)
    amp_rows, mine = pl.pallas_call(
        amplitude_kernel,
        out_shape=(rows, rows16),
        in_specs=[SMEM, VMEM, VMEM, VMEM, VMEM],
        out_specs=(VMEM, VMEM),
        compiler_params=params(8),
    )(where, part, up, down, denom)

    other = swap(mine, "yh")
    columns = pl.pallas_call(
        blocks_kernel,
        out_shape=jax.ShapeDtypeStruct((nz, padded, slab), F32),
        in_specs=[VMEM],
        out_specs=VMEM,
        compiler_params=params(8),
    )(amp_rows)
    other, _ = lax.optimization_barrier((other, columns))
    columns = lax.all_to_all(columns, "z", split_axis=0, concat_axis=0, tiled=True)
    both = jnp.concatenate([mine, other])
    outward = pl.pallas_call(
        outward_kernel,
        out_shape=jax.ShapeDtypeStruct((nz, padded, slab // 2), F32),
        in_specs=[SMEM, VMEM],
        out_specs=VMEM,
        compiler_params=params(8),
    )(where, columns)
    ring = {}
    up = down = both
    for step in range(1, nz // 2 - 1):
        up, down = shift(up, "z", 1), shift(down, "z", -1)
        ring[nz - step], ring[step] = up, down
        if step == 1:
            up, down, outward = lax.optimization_barrier((up, down, outward))
    far = {r: swap(ring[r], "c") for r in (1, nz - 1)}
    far[0] = swap(both, "c")
    outward = swap(outward, "yh")
    up, down, outward, far = lax.optimization_barrier((up, down, outward, far))
    kept, sent = pl.pallas_call(
        inward_kernel,
        out_shape=(jax.ShapeDtypeStruct((nz, padded, 2 * padded), F32),) * 2,
        in_specs=[SMEM, VMEM, VMEM],
        out_specs=(VMEM, VMEM),
        compiler_params=params(8),
    )(where, columns, outward)
    taken = swap(sent, "c")
    half = jax.ShapeDtypeStruct((padded, nvir), BF16)
    half_up, half_down = pl.pallas_call(
        halves_kernel,
        out_shape=(half, half),
        in_specs=[VMEM, VMEM],
        out_specs=(VMEM, VMEM),
        compiler_params=params(8),
    )(up, down)
    last = (shift(down, "z", -1), shift(up, "z", 1), shift(half_up, "z", 2), shift(half_down, "z", -2))

    soon = (0, 1, nz - 1, 2, nz - 2)
    late = (3, nz - 3, nz // 2)
    far.update({r: swap(ring[r], "c") for r in (2, nz - 2)})
    ring[0] = both
    pieces = [v for r in soon for v in (ring[r], far[r])]
    state = pl.pallas_call(
        functools.partial(early_kernel, soon, nz, width, padded),
        out_shape=(
            rows,
            jax.ShapeDtypeStruct((nz, padded, slab), F32),
            rows16,
            jax.ShapeDtypeStruct((nz, 2, padded, 2 * padded), BF16),
        ),
        in_specs=[SMEM] + [VMEM] * (3 + 2 * len(soon)),
        out_specs=(VMEM,) * 4,
        compiler_params=params(16),
        cost_estimate=cost(len(soon) * 8 * padded * padded * nvir, len(soon) * 8 * padded * nvir),
    )(where, amp_rows, kept, taken, *pieces)
    last, state = lax.optimization_barrier((last, state))
    added = pl.pallas_call(
        functools.partial(late_kernel, late, nz, width, padded),
        out_shape=jax.ShapeDtypeStruct((nz, padded, slab), F32),
        in_specs=[SMEM] + [VMEM] * (6 + 2 * len(late)),
        out_specs=VMEM,
        compiler_params=params(16),
        cost_estimate=cost(len(late) * 8 * padded * padded * nvir, len(late) * 8 * padded * nvir),
    )(
        where,
        *state,
        last[0],
        swap(last[0], "c"),
        last[1],
        swap(last[1], "c"),
        last[2],
        last[3],
        swap(last[2], "c"),
        swap(last[3], "c"),
    )
    added = lax.all_to_all(added, SLABS, split_axis=0, concat_axis=0, tiled=True)
    return jnp.sum(added, axis=0)[:width]


def solution(mesh):
    fine = Mesh(mesh.devices.reshape(4, 2, 8, 2, 2), ("x", "yl", "z", "yh", "c"))
    pair, grid = SLABS, ("z", "yh", "c")
    in_specs = (P(None, pair, grid), P(), P(), P())
    return jax.shard_map(local, mesh=fine, in_specs=in_specs, out_specs=P(grid, pair), check_vma=False)
```

```python
import functools

import jax
import jax.numpy as jnp
from jax import lax
from jax.experimental import pallas as pl
from jax.experimental.pallas import tpu as pltpu
from jax.sharding import Mesh
from jax.sharding import PartitionSpec as P

F32 = jnp.float32
BF16 = jnp.bfloat16
SLABS = ("x", "yl")
VMEM = pl.BlockSpec(memory_space=pltpu.VMEM)
SMEM = pl.BlockSpec(memory_space=pltpu.SMEM)


def params(mib):
    return pltpu.CompilerParams(vmem_limit_bytes=mib * 1024 * 1024)


def swap(value, axis):
    return lax.ppermute(value, axis, [(0, 1), (1, 0)])


def shift(value, axis, step):
    size = lax.axis_size(axis)
    return lax.ppermute(value, axis, [(i, (i + step) % size) for i in range(size)])


def dot_nt(a, b):
    return lax.dot_general(a, b, (((1,), (1,)), ((), ())), preferred_element_type=F32)


def cost(flops, moved):
    return pl.CostEstimate(flops=flops, bytes_accessed=moved, transcendentals=0)


def fill(side, width, padded, pair_ref, orbital_ref, put):
    half = orbital_ref.shape[1] // 2
    gap = jnp.zeros((padded - width, orbital_ref.shape[2]), BF16)
    for p in range(pair_ref.shape[0]):
        left = orbital_ref[pair_ref[p, 0]]
        right = orbital_ref[pair_ref[p, 1]]
        for y in range(2):
            at = (2 * y + side) * width
            put(p, y, jnp.concatenate([left[at : at + width], gap], axis=0))
        put(p, 2, right[side * half : (side + 1) * half])


def select_kernel(width, padded, where_ref, pair_ref, orbital_ref, out_ref):
    def put(p, block, value):
        out_ref[p, block * padded : block * padded + value.shape[0]] = value

    for c in range(2):

        @pl.when(where_ref[1] == c)
        def _():
            fill(1 - c, width, padded, pair_ref, orbital_ref, put)


def own_kernel(width, padded, where_ref, pair_ref, orbital_ref, out_ref):
    groups, naux = pair_ref.shape[0], orbital_ref.shape[2]
    for c in range(2):
        lanes = slice(c * naux, (c + 1) * naux)

        def put(p, block, value, lanes=lanes):
            if block < 2:
                out_ref[block * groups + p, :padded, lanes] = value
            else:
                for y in range(2):
                    out_ref[y * groups + p, padded:, lanes] = value

        @pl.when(where_ref[1] == c)
        def _(c=c, put=put):
            fill(c, width, padded, pair_ref, orbital_ref, put)


def other_kernel(padded, where_ref, taken_ref, own_ref, out_ref):
    groups, naux = taken_ref.shape[0], taken_ref.shape[2]
    for c in range(2):
        lanes = slice((1 - c) * naux, (2 - c) * naux)

        @pl.when(where_ref[1] == c)
        def _(lanes=lanes):
            for p in range(groups):
                for y in range(2):
                    out_ref[y * groups + p, :padded, lanes] = taken_ref[p, y * padded : (y + 1) * padded]
                    out_ref[y * groups + p, padded:, lanes] = taken_ref[p, 2 * padded :]


def half_product(left, right_ref, padded):
    sources = right_ref.shape[0]
    half = sources // 2
    total = None
    for y in range(2):
        right = jnp.concatenate([right_ref[half * y + k, padded:, :] for k in range(half)], axis=0)
        term = dot_nt(left(y), right)
        total = term if total is None else total + term
    return total


def all_rows(near_ref, padded):
    half = near_ref.shape[0] // 2

    def left(y):
        return near_ref[half * y : half * (y + 1), :padded, :].reshape(half * padded, near_ref.shape[2])

    return left


def near_kernel(padded, near_ref, out_ref):
    out_ref[...] = half_product(all_rows(near_ref, padded), near_ref, padded).reshape(out_ref.shape)


def first_kernel(padded, where_ref, near_part_ref, near_ref, far_ref, up_ref, down_ref):
    nz, width = near_part_ref.shape[0], near_part_ref.shape[2]
    half = near_ref.shape[0] // 2
    cut = padded // 2
    at = lax.rem(where_ref[0] + nz // 2, nz)
    total = half_product(lambda y: near_ref[half * y + at, :padded, :], far_ref, padded)
    near = near_part_ref[at]
    up_ref[...] = jnp.concatenate([near[:cut], total[:cut]], axis=1)
    down_ref[...] = jnp.concatenate([near[cut:], total[cut:]], axis=1)


def rest_kernel(padded, where_ref, pair_ref, occ_ref, vir_ref, near_part_ref, near_ref, far_ref, out_ref, denom_ref):
    total = half_product(all_rows(near_ref, padded), far_ref, padded).reshape(near_part_ref.shape)
    for k in range(near_part_ref.shape[0]):
        out_ref[k] = jnp.concatenate([near_part_ref[k], total[k]], axis=1)
    chunk, group, width = where_ref[2], where_ref[3], where_ref[5]
    columns = jnp.broadcast_to(vir_ref[...], denom_ref.shape)
    place = lax.broadcasted_iota(jnp.int32, denom_ref.shape, 1)
    row = lax.broadcasted_iota(jnp.int32, denom_ref.shape, 0)
    own = jnp.sum(jnp.where(place == chunk * width + row, columns, 0.0), axis=1, keepdims=True)
    denom_ref[...] = (own + columns) - occ_ref[pair_ref[group, 0]] - occ_ref[pair_ref[group, 1]]


def hop_kernel(step, where_ref, part_ref, up_in, down_in, up_ref, down_ref):
    nz, rows = part_ref.shape[:2]
    above = lax.rem(where_ref[0] + step, nz)
    below = lax.rem(where_ref[0] + nz - step, nz)
    taken = up_in.shape[0]
    up_ref[:taken] = part_ref[above, :taken] + up_in[...]
    down_ref[rows - taken :] = part_ref[below, rows - taken :] + down_in[...]
    if taken < rows:
        up_ref[taken:] = part_ref[above, taken:]
        down_ref[: rows - taken] = part_ref[below, : rows - taken]


def amplitude_kernel(where_ref, part_ref, up_in, down_in, denom_ref, out_ref, rounded_ref):
    sums = part_ref[where_ref[0]] + (up_in[...] + down_in[...])
    half = sums.shape[1] // 2
    near, far = sums[:, :half], sums[:, half:]
    halves = (jnp.where(where_ref[1] == 0, near, far), jnp.where(where_ref[1] == 0, far, near))
    step = half // part_ref.shape[0]
    parts = [h[:, k * step : (k + 1) * step] for k in range(part_ref.shape[0]) for h in halves]
    amps = jnp.concatenate(parts, axis=1) / denom_ref[...]
    out_ref[...] = amps
    rounded_ref[...] = amps.astype(BF16)


def blocks_kernel(rows_ref, blocks_ref):
    slab = blocks_ref.shape[2]
    for k in range(blocks_ref.shape[0]):
        blocks_ref[k] = rows_ref[:, k * slab : (k + 1) * slab]


def halves_kernel(up_ref, down_ref, first_ref, second_ref):
    first_ref[...] = up_ref[: first_ref.shape[0]]
    second_ref[...] = down_ref[first_ref.shape[0] :]


def outward_kernel(where_ref, columns_ref, out_ref):
    half = columns_ref.shape[2] // 2
    for k in range(columns_ref.shape[0]):
        columns = columns_ref[k]
        out_ref[k] = jnp.where(where_ref[6] == 0, columns[:, half:], columns[:, :half])


def inward_kernel(where_ref, columns_ref, other_ref, keep_ref, send_ref):
    c, yh = where_ref[1], where_ref[6]
    half = columns_ref.shape[2] // 2
    width = half // 2
    gap = jnp.zeros((columns_ref.shape[1], keep_ref.shape[2] // 2 - width), F32)
    for k in range(columns_ref.shape[0]):
        columns = columns_ref[k]
        own = jnp.where(yh == 0, columns[:, :half], columns[:, half:])
        other = other_ref[k]
        sides = []
        for h in range(2):
            at = h * width
            sides.append(jnp.concatenate([own[:, at : at + width], gap, other[:, at : at + width], gap], axis=1))
        keep_ref[k] = jnp.where(c == 0, sides[0], sides[1])
        send_ref[k] = jnp.where(c == 0, sides[1], sides[0])


def natural(c, yh, near, far, width, padded):
    parts = []
    for y in range(2):
        for h in range(2):
            side = jnp.where(c == h, near, far)
            parts.append(jnp.where(yh == y, side[:, :width], side[:, padded : padded + width]))
    return jnp.concatenate(parts, axis=1)


def relative(c, yh, block, width, padded):
    gap = jnp.zeros((block.shape[0], padded - width), block.dtype)
    sides = []
    for h in range(2):
        first, second = block[:, h * width : (h + 1) * width], block[:, (2 + h) * width : (3 + h) * width]
        own, other = jnp.where(yh == 0, first, second), jnp.where(yh == 0, second, first)
        sides.append(jnp.concatenate([own, gap, other, gap], axis=1))
    return jnp.where(c == 0, sides[0], sides[1]), jnp.where(c == 0, sides[1], sides[0])


def density_pieces(steps, nz, width, padded, where_ref, tilde, tilde_t_ref, pieces, total, blocks_ref):
    z, c, yh = where_ref[0], where_ref[1], where_ref[6]
    pieces = list(pieces)
    for r in steps:
        at = lax.rem(z + r, nz)
        sides = []
        for slot in range(2):
            piece = pieces.pop(0)[...]
            if piece.shape[0] == padded:
                piece = jnp.concatenate([piece, pieces.pop(0)[...]], axis=0)
            term = jnp.dot(tilde_t_ref[at, slot], piece, preferred_element_type=F32)
            total = term if total is None else total + term
            sides.append(dot_nt(tilde, piece))
        blocks_ref[at] = natural(c, yh, sides[0], sides[1], width, padded)
    return total


def turn(block, padded):
    flipped = block.T
    return jnp.concatenate([flipped[:padded], flipped[padded:]], axis=1)


def early_kernel(steps, nz, width, padded, where_ref, rows_ref, near_ref, far_ref, *refs):
    pieces = refs[:-4]
    total_ref, blocks_ref, tilde_ref, tilde_t_ref = refs[-4:]
    c, yh = where_ref[1], where_ref[6]
    slab = rows_ref.shape[1] // nz
    rows = rows_ref[...]
    turned = []
    for k in range(nz):
        near, far = turn(near_ref[k], padded), turn(far_ref[k], padded)
        mine = relative(c, yh, rows[:, k * slab : (k + 1) * slab], width, padded)
        tilde_t_ref[k, 0] = (2.0 * near - mine[0]).astype(BF16)
        tilde_t_ref[k, 1] = (2.0 * far - mine[1]).astype(BF16)
        turned.append(natural(c, yh, near, far, width, padded))
    tilde = (2.0 * rows - jnp.concatenate(turned, axis=1)).astype(BF16)
    tilde_ref[...] = tilde
    total_ref[...] = density_pieces(steps, nz, width, padded, where_ref, tilde, tilde_t_ref, pieces, None, blocks_ref)


def late_kernel(steps, nz, width, padded, where_ref, total_ref, blocks_ref, tilde_ref, tilde_t_ref, *refs):
    pieces, out_ref = refs[:-1], refs[-1]
    slab = total_ref.shape[1] // nz
    for k in range(nz):
        out_ref[k] = blocks_ref[k]
    total = density_pieces(
        steps, nz, width, padded, where_ref, tilde_ref[...], tilde_t_ref, pieces, total_ref[...], out_ref
    )
    for k in range(nz):
        out_ref[k] += total[:, k * slab : (k + 1) * slab]


def local(orbital_b, pair_list, eps_occ, eps_vir):
    slab, naux = orbital_b.shape[1:]
    nvir = eps_vir.shape[0]
    z, yh, c = (lax.axis_index(a) for a in ("z", "yh", "c"))
    nz = lax.axis_size("z")
    width = slab // 4
    padded = (width + 8) // 8 * 8
    where = jnp.stack([z, c, z * 4 + yh * 2 + c, lax.axis_index(SLABS), yh * 2 + c, jnp.int32(width), yh])

    sent = 2 * padded + slab // 2
    theirs = pl.pallas_call(
        functools.partial(select_kernel, width, padded),
        out_shape=jax.ShapeDtypeStruct((8, sent, naux), BF16),
        in_specs=[SMEM, SMEM, VMEM],
        out_specs=VMEM,
        compiler_params=params(8),
    )(where, pair_list, orbital_b)
    taken = swap(theirs, "c")
    outgoing = jax.ShapeDtypeStruct((16, sent - padded, 2 * naux), BF16)
    ours = pl.pallas_call(
        functools.partial(own_kernel, width, padded),
        out_shape=outgoing,
        in_specs=[SMEM, SMEM, VMEM],
        out_specs=VMEM,
        compiler_params=params(8),
    )(where, pair_list, orbital_b)
    ours = pl.pallas_call(
        functools.partial(other_kernel, padded),
        out_shape=outgoing,
        in_specs=[SMEM, VMEM, VMEM],
        out_specs=VMEM,
        input_output_aliases={2: 0},
        compiler_params=params(8),
    )(where, taken, ours)
    near = lax.all_to_all(ours, ("yh", "x", "yl"), split_axis=0, concat_axis=0, tiled=True)
    far = swap(near, "c")

    whole = jax.ShapeDtypeStruct((8, padded, nvir), F32)
    rows = jax.ShapeDtypeStruct((padded, nvir), F32)
    halves = jax.ShapeDtypeStruct((padded // 2, nvir), F32)
    flops = 16 * padded * 8 * slab * 2 * naux
    near_part = pl.pallas_call(
        functools.partial(near_kernel, padded),
        out_shape=jax.ShapeDtypeStruct((8, padded, nvir // 2), F32),
        in_specs=[VMEM],
        out_specs=VMEM,
        compiler_params=params(16),
        cost_estimate=cost(flops, 0),
    )(near)
    up, down = pl.pallas_call(
        functools.partial(first_kernel, padded),
        out_shape=(halves, halves),
        in_specs=[SMEM, VMEM, VMEM, VMEM],
        out_specs=(VMEM, VMEM),
        compiler_params=params(16),
        cost_estimate=cost(flops // 8, 0),
    )(where, near_part, near, far)
    up, down = shift(up, "z", 1), shift(down, "z", -1)
    part, denom = pl.pallas_call(
        functools.partial(rest_kernel, padded),
        out_shape=(whole, rows),
        in_specs=[SMEM, SMEM, SMEM, VMEM, VMEM, VMEM, VMEM],
        out_specs=(VMEM, VMEM),
        compiler_params=params(16),
        cost_estimate=cost(flops, 0),
    )(where, pair_list, eps_occ, eps_vir[None], near_part, near, far)
    for step in range(nz // 2 - 1, 0, -1):
        up, down = pl.pallas_call(
            functools.partial(hop_kernel, step),
            out_shape=(rows, rows),
            in_specs=[SMEM, VMEM, VMEM, VMEM],
            out_specs=(VMEM, VMEM),
            compiler_params=params(8),
        )(where, part, up, down)
        up, down = shift(up, "z", 1), shift(down, "z", -1)
    rows16 = jax.ShapeDtypeStruct((padded, nvir), BF16)
    amp_rows, mine = pl.pallas_call(
        amplitude_kernel,
        out_shape=(rows, rows16),
        in_specs=[SMEM, VMEM, VMEM, VMEM, VMEM],
        out_specs=(VMEM, VMEM),
        compiler_params=params(8),
    )(where, part, up, down, denom)

    other = swap(mine, "yh")
    columns = pl.pallas_call(
        blocks_kernel,
        out_shape=jax.ShapeDtypeStruct((nz, padded, slab), F32),
        in_specs=[VMEM],
        out_specs=VMEM,
        compiler_params=params(8),
    )(amp_rows)
    other, _ = lax.optimization_barrier((other, columns))
    columns = lax.all_to_all(columns, "z", split_axis=0, concat_axis=0, tiled=True)
    both = jnp.concatenate([mine, other])
    outward = pl.pallas_call(
        outward_kernel,
        out_shape=jax.ShapeDtypeStruct((nz, padded, slab // 2), F32),
        in_specs=[SMEM, VMEM],
        out_specs=VMEM,
        compiler_params=params(8),
    )(where, columns)
    ring = {}
    up = down = both
    for step in range(1, nz // 2 - 1):
        up, down = shift(up, "z", 1), shift(down, "z", -1)
        ring[nz - step], ring[step] = up, down
        if step == 1:
            up, down, outward = lax.optimization_barrier((up, down, outward))
    far = {r: swap(ring[r], "c") for r in (1, nz - 1)}
    far[0] = swap(both, "c")
    up, down, far = lax.optimization_barrier((up, down, far))
    outward = swap(outward, "yh")
    kept, sent = pl.pallas_call(
        inward_kernel,
        out_shape=(jax.ShapeDtypeStruct((nz, padded, 2 * padded), F32),) * 2,
        in_specs=[SMEM, VMEM, VMEM],
        out_specs=(VMEM, VMEM),
        compiler_params=params(8),
    )(where, columns, outward)
    taken = swap(sent, "c")
    half = jax.ShapeDtypeStruct((padded, nvir), BF16)
    half_up, half_down = pl.pallas_call(
        halves_kernel,
        out_shape=(half, half),
        in_specs=[VMEM, VMEM],
        out_specs=(VMEM, VMEM),
        compiler_params=params(8),
    )(up, down)
    last = (shift(down, "z", -1), shift(up, "z", 1), shift(half_up, "z", 2), shift(half_down, "z", -2))

    soon = (0, 1, nz - 1, 2, nz - 2)
    late = (3, nz - 3, nz // 2)
    far.update({r: swap(ring[r], "c") for r in (2, nz - 2)})
    ring[0] = both
    pieces = [v for r in soon for v in (ring[r], far[r])]
    state = pl.pallas_call(
        functools.partial(early_kernel, soon, nz, width, padded),
        out_shape=(
            rows,
            jax.ShapeDtypeStruct((nz, padded, slab), F32),
            rows16,
            jax.ShapeDtypeStruct((nz, 2, padded, 2 * padded), BF16),
        ),
        in_specs=[SMEM] + [VMEM] * (3 + 2 * len(soon)),
        out_specs=(VMEM,) * 4,
        compiler_params=params(16),
        cost_estimate=cost(len(soon) * 8 * padded * padded * nvir, len(soon) * 8 * padded * nvir),
    )(where, amp_rows, kept, taken, *pieces)
    last, state = lax.optimization_barrier((last, state))
    added = pl.pallas_call(
        functools.partial(late_kernel, late, nz, width, padded),
        out_shape=jax.ShapeDtypeStruct((nz, padded, slab), F32),
        in_specs=[SMEM] + [VMEM] * (6 + 2 * len(late)),
        out_specs=VMEM,
        compiler_params=params(16),
        cost_estimate=cost(len(late) * 8 * padded * padded * nvir, len(late) * 8 * padded * nvir),
    )(
        where,
        *state,
        last[0],
        swap(last[0], "c"),
        last[1],
        swap(last[1], "c"),
        last[2],
        last[3],
        swap(last[2], "c"),
        swap(last[3], "c"),
    )
    added = lax.all_to_all(added, SLABS, split_axis=0, concat_axis=0, tiled=True)
    return jnp.sum(added, axis=0)[:width]


def solution(mesh):
    fine = Mesh(mesh.devices.reshape(4, 2, 8, 2, 2), ("x", "yl", "z", "yh", "c"))
    pair, grid = SLABS, ("z", "yh", "c")
    in_specs = (P(None, pair, grid), P(), P(), P())
    return jax.shard_map(local, mesh=fine, in_specs=in_specs, out_specs=P(grid, pair), check_vma=False)
```

```python
import functools

import jax
import jax.numpy as jnp
from jax import lax
from jax.experimental import pallas as pl
from jax.experimental.pallas import tpu as pltpu
from jax.sharding import Mesh
from jax.sharding import PartitionSpec as P

F32 = jnp.float32
BF16 = jnp.bfloat16
SLABS = ("x", "yl")
VMEM = pl.BlockSpec(memory_space=pltpu.VMEM)
SMEM = pl.BlockSpec(memory_space=pltpu.SMEM)


def params(mib):
    return pltpu.CompilerParams(vmem_limit_bytes=mib * 1024 * 1024)


def swap(value, axis):
    return lax.ppermute(value, axis, [(0, 1), (1, 0)])


def shift(value, axis, step):
    size = lax.axis_size(axis)
    return lax.ppermute(value, axis, [(i, (i + step) % size) for i in range(size)])


def dot_nt(a, b):
    return lax.dot_general(a, b, (((1,), (1,)), ((), ())), preferred_element_type=F32)


def cost(flops, moved):
    return pl.CostEstimate(flops=flops, bytes_accessed=moved, transcendentals=0)


def fill(side, width, padded, pair_ref, orbital_ref, put):
    half = orbital_ref.shape[1] // 2
    gap = jnp.zeros((padded - width, orbital_ref.shape[2]), BF16)
    for p in range(pair_ref.shape[1]):
        left = orbital_ref[pair_ref[0, p]]
        right = orbital_ref[pair_ref[1, p]]
        for y in range(2):
            at = (2 * y + side) * width
            put(p, y, jnp.concatenate([left[at : at + width], gap], axis=0))
        put(p, 2, right[side * half : (side + 1) * half])


def select_kernel(width, padded, where_ref, pair_ref, orbital_ref, out_ref):
    def put(p, block, value):
        out_ref[p, block * padded : block * padded + value.shape[0]] = value

    for c in range(2):

        @pl.when(where_ref[1] == c)
        def _():
            fill(1 - c, width, padded, pair_ref, orbital_ref, put)


def own_kernel(width, padded, where_ref, pair_ref, orbital_ref, out_ref):
    groups, naux = pair_ref.shape[1], orbital_ref.shape[2]
    for c in range(2):
        lanes = slice(c * naux, (c + 1) * naux)

        def put(p, block, value, lanes=lanes):
            if block < 2:
                out_ref[block * groups + p, :padded, lanes] = value
            else:
                for y in range(2):
                    out_ref[y * groups + p, padded:, lanes] = value

        @pl.when(where_ref[1] == c)
        def _(c=c, put=put):
            fill(c, width, padded, pair_ref, orbital_ref, put)


def other_kernel(padded, where_ref, taken_ref, own_ref, out_ref):
    groups, naux = taken_ref.shape[0], taken_ref.shape[2]
    for c in range(2):
        lanes = slice((1 - c) * naux, (2 - c) * naux)

        @pl.when(where_ref[1] == c)
        def _(lanes=lanes):
            for p in range(groups):
                for y in range(2):
                    out_ref[y * groups + p, :padded, lanes] = taken_ref[p, y * padded : (y + 1) * padded]
                    out_ref[y * groups + p, padded:, lanes] = taken_ref[p, 2 * padded :]


def half_product(left, right_ref, padded):
    sources = right_ref.shape[0]
    half = sources // 2
    total = None
    for y in range(2):
        right = jnp.concatenate([right_ref[half * y + k, padded:, :] for k in range(half)], axis=0)
        term = dot_nt(left(y), right)
        total = term if total is None else total + term
    return total


def all_rows(near_ref, padded):
    half = near_ref.shape[0] // 2

    def left(y):
        return near_ref[half * y : half * (y + 1), :padded, :].reshape(half * padded, near_ref.shape[2])

    return left


def near_kernel(padded, near_ref, out_ref):
    out_ref[...] = half_product(all_rows(near_ref, padded), near_ref, padded).reshape(out_ref.shape)


def first_kernel(padded, where_ref, near_part_ref, near_ref, far_ref, *out_refs):
    nz = near_part_ref.shape[0]
    half = near_ref.shape[0] // 2
    cut = padded // 2
    places = [lax.rem(where_ref[0] + offset, nz) for offset in (nz // 2, nz // 2 - 1, nz // 2 + 1)]

    def left(y):
        return jnp.concatenate([near_ref[half * y + at, :padded, :] for at in places], axis=0)

    total = half_product(left, far_ref, padded)
    sums = [
        jnp.concatenate([near_part_ref[at], total[n * padded : (n + 1) * padded]], axis=1)
        for n, at in enumerate(places)
    ]
    for ref, value in zip(out_refs, (sums[0][:cut], sums[0][cut:], sums[1], sums[2])):
        ref[...] = value


def rest_kernel(padded, where_ref, pair_ref, occ_ref, vir_ref, near_part_ref, near_ref, far_ref, out_ref, denom_ref):
    total = half_product(all_rows(near_ref, padded), far_ref, padded).reshape(near_part_ref.shape)
    for k in range(near_part_ref.shape[0]):
        out_ref[k] = jnp.concatenate([near_part_ref[k], total[k]], axis=1)
    chunk, group, width = where_ref[2], where_ref[3], where_ref[5]
    columns = jnp.broadcast_to(vir_ref[...], denom_ref.shape)
    place = lax.broadcasted_iota(jnp.int32, denom_ref.shape, 1)
    row = lax.broadcasted_iota(jnp.int32, denom_ref.shape, 0)
    own = jnp.sum(jnp.where(place == chunk * width + row, columns, 0.0), axis=1, keepdims=True)
    denom_ref[...] = (own + columns) - occ_ref[pair_ref[0, group]] - occ_ref[pair_ref[1, group]]


def hop_kernel(step, where_ref, part_ref, *refs):
    nz, rows = part_ref.shape[:2]
    above = lax.rem(where_ref[0] + step, nz)
    below = lax.rem(where_ref[0] + nz - step, nz)
    up_in, down_in = refs[:2]
    up_ref, down_ref = refs[-2:]
    up_ref[...] = part_ref[above] + up_in[...]
    down_ref[...] = part_ref[below] + down_in[...]
    if len(refs) > 4:
        cut = rows // 2
        up_ref[:cut] += refs[2][...]
        down_ref[cut:] += refs[3][...]


def amplitude_kernel(where_ref, part_ref, up_in, down_in, denom_ref, out_ref, rounded_ref):
    sums = part_ref[where_ref[0]] + (up_in[...] + down_in[...])
    half = sums.shape[1] // 2
    near, far = sums[:, :half], sums[:, half:]
    halves = (jnp.where(where_ref[1] == 0, near, far), jnp.where(where_ref[1] == 0, far, near))
    step = half // part_ref.shape[0]
    parts = [h[:, k * step : (k + 1) * step] for k in range(part_ref.shape[0]) for h in halves]
    amps = jnp.concatenate(parts, axis=1) / denom_ref[...]
    out_ref[...] = amps
    rounded_ref[...] = amps.astype(BF16)


def blocks_kernel(rows_ref, blocks_ref):
    count, half, lanes = blocks_ref.shape
    width = rows_ref.shape[1] // count
    gap = jnp.zeros((half, lanes // 2 - width), F32)
    for k in range(count):
        block = rows_ref[:, k * width : (k + 1) * width]
        blocks_ref[k] = jnp.concatenate([block[:half], gap, block[half:], gap], axis=1)


def merge_kernel(width, first_ref, second_ref, out_ref):
    out_ref[...] = jnp.concatenate([first_ref[:width], second_ref[:width]], axis=0)


def halves_kernel(up_ref, down_ref, first_ref, second_ref):
    first_ref[...] = up_ref[: first_ref.shape[0]]
    second_ref[...] = down_ref[first_ref.shape[0] :]


def natural(c, yh, near, far):
    width = near.shape[1] // 2
    parts = []
    for y in range(2):
        for h in range(2):
            side = jnp.where(c == h, near, far)
            parts.append(jnp.where(yh == y, side[:, :width], side[:, width:]))
    return jnp.concatenate(parts, axis=1)


def relative(c, yh, block):
    width = block.shape[1] // 4
    sides = []
    for h in range(2):
        first, second = block[:, h * width : (h + 1) * width], block[:, (2 + h) * width : (3 + h) * width]
        sides.append(jnp.concatenate([jnp.where(yh == 0, first, second), jnp.where(yh == 0, second, first)], axis=1))
    return jnp.where(c == 0, sides[0], sides[1]), jnp.where(c == 0, sides[1], sides[0])


def density_pieces(steps, nz, where_ref, tilde, tilde_t_ref, pieces, total, blocks_ref):
    z, c, yh = where_ref[0], where_ref[1], where_ref[6]
    rows = tilde_t_ref.shape[3]
    pieces = list(pieces)
    for r in steps:
        at = lax.rem(z + r, nz)
        sides = []
        for slot in range(2):
            piece = pieces.pop(0)[...]
            if piece.shape[0] < rows:
                piece = jnp.concatenate([piece, pieces.pop(0)[...]], axis=0)
            term = jnp.dot(tilde_t_ref[at, slot], piece, preferred_element_type=F32)
            total = term if total is None else total + term
            sides.append(dot_nt(tilde, piece))
        blocks_ref[at] = natural(c, yh, sides[0], sides[1])
    return total


def early_kernel(steps, nz, where_ref, rows_ref, columns_ref, *refs):
    pieces = refs[:-4]
    total_ref, blocks_ref, tilde_ref, tilde_t_ref = refs[-4:]
    c, yh = where_ref[1], where_ref[6]
    rows = rows_ref[...]
    padded, nvir = rows.shape
    slab = nvir // nz
    width = slab // 4

    def turn(at):
        flipped = columns_ref[at].T
        return jnp.concatenate([flipped[:padded], flipped[padded:, : width - padded // 2]], axis=1)

    turned = []
    for k in range(nz):
        near, far = (
            jnp.concatenate([turn(4 * k + 2 * yh + h), turn(4 * k + 2 * (1 - yh) + h)], axis=1) for h in (c, 1 - c)
        )
        mine = relative(c, yh, rows[:, k * slab : (k + 1) * slab])
        tilde_t_ref[k, 0] = (2.0 * near - mine[0]).astype(BF16)
        tilde_t_ref[k, 1] = (2.0 * far - mine[1]).astype(BF16)
        turned.append(natural(c, yh, near, far))
    tilde = (2.0 * rows - jnp.concatenate(turned, axis=1)).astype(BF16)
    tilde_ref[...] = tilde
    total_ref[...] = density_pieces(steps, nz, where_ref, tilde, tilde_t_ref, pieces, None, blocks_ref)


def late_kernel(steps, nz, where_ref, total_ref, blocks_ref, tilde_ref, tilde_t_ref, *refs):
    pieces, out_ref = refs[:-1], refs[-1]
    slab = total_ref.shape[1] // nz
    for k in range(nz):
        out_ref[k] = blocks_ref[k]
    total = density_pieces(
        steps, nz, where_ref, tilde_ref[...], tilde_t_ref, pieces, total_ref[...], out_ref
    )
    for k in range(nz):
        out_ref[k] += total[:, k * slab : (k + 1) * slab]


def local(orbital_b, pair_list, eps_occ, eps_vir):
    slab, naux = orbital_b.shape[1:]
    nvir = eps_vir.shape[0]
    z, yh, c = (lax.axis_index(a) for a in ("z", "yh", "c"))
    nz = lax.axis_size("z")
    width = slab // 4
    padded = (width + 8) // 8 * 8
    where = jnp.stack([z, c, z * 4 + yh * 2 + c, lax.axis_index(SLABS), yh * 2 + c, jnp.int32(width), yh])

    pairs = pair_list.T

    sent = 2 * padded + slab // 2
    theirs = pl.pallas_call(
        functools.partial(select_kernel, width, padded),
        out_shape=jax.ShapeDtypeStruct((8, sent, naux), BF16),
        in_specs=[SMEM, SMEM, VMEM],
        out_specs=VMEM,
        compiler_params=params(8),
    )(where, pairs, orbital_b)
    taken = swap(theirs, "c")
    outgoing = jax.ShapeDtypeStruct((16, sent - padded, 2 * naux), BF16)
    ours = pl.pallas_call(
        functools.partial(own_kernel, width, padded),
        out_shape=outgoing,
        in_specs=[SMEM, SMEM, VMEM],
        out_specs=VMEM,
        compiler_params=params(8),
    )(where, pairs, orbital_b)
    ours = pl.pallas_call(
        functools.partial(other_kernel, padded),
        out_shape=outgoing,
        in_specs=[SMEM, VMEM, VMEM],
        out_specs=VMEM,
        input_output_aliases={2: 0},
        compiler_params=params(8),
    )(where, taken, ours)
    near = lax.all_to_all(ours, ("yh", "x", "yl"), split_axis=0, concat_axis=0, tiled=True)
    far = swap(near, "c")

    whole = jax.ShapeDtypeStruct((8, padded, nvir), F32)
    rows = jax.ShapeDtypeStruct((padded, nvir), F32)
    halves = jax.ShapeDtypeStruct((padded // 2, nvir), F32)
    flops = 16 * padded * 8 * slab * 2 * naux
    near_part = pl.pallas_call(
        functools.partial(near_kernel, padded),
        out_shape=jax.ShapeDtypeStruct((8, padded, nvir // 2), F32),
        in_specs=[VMEM],
        out_specs=VMEM,
        compiler_params=params(16),
        cost_estimate=cost(flops, 0),
    )(near)
    half_up, half_down, up, down = pl.pallas_call(
        functools.partial(first_kernel, padded),
        out_shape=(halves, halves, rows, rows),
        in_specs=[SMEM, VMEM, VMEM, VMEM],
        out_specs=(VMEM,) * 4,
        compiler_params=params(16),
        cost_estimate=cost(flops // 4, 0),
    )(where, near_part, near, far)
    sums = (shift(up, "z", 1), shift(down, "z", -1), shift(half_up, "z", 2), shift(half_down, "z", -2))
    part, denom = pl.pallas_call(
        functools.partial(rest_kernel, padded),
        out_shape=(whole, rows),
        in_specs=[SMEM, SMEM, SMEM, VMEM, VMEM, VMEM, VMEM],
        out_specs=(VMEM, VMEM),
        compiler_params=params(16),
        cost_estimate=cost(flops, 0),
    )(where, pairs, eps_occ, eps_vir[None], near_part, near, far)
    for step in range(nz // 2 - 2, 0, -1):
        up, down = pl.pallas_call(
            functools.partial(hop_kernel, step),
            out_shape=(rows, rows),
            in_specs=[SMEM] + [VMEM] * (1 + len(sums)),
            out_specs=(VMEM, VMEM),
            compiler_params=params(8),
        )(where, part, *sums)
        sums = (shift(up, "z", 1), shift(down, "z", -1))
    up, down = sums
    rows16 = jax.ShapeDtypeStruct((padded, nvir), BF16)
    amp_rows, mine = pl.pallas_call(
        amplitude_kernel,
        out_shape=(rows, rows16),
        in_specs=[SMEM, VMEM, VMEM, VMEM, VMEM],
        out_specs=(VMEM, VMEM),
        compiler_params=params(8),
    )(where, part, up, down, denom)

    other = swap(mine, "yh")
    columns = pl.pallas_call(
        blocks_kernel,
        out_shape=jax.ShapeDtypeStruct((4 * nz, padded // 2, 2 * padded), F32),
        in_specs=[VMEM],
        out_specs=VMEM,
        compiler_params=params(8),
    )(amp_rows)
    other, _ = lax.optimization_barrier((other, columns))
    columns = lax.all_to_all(columns, ("z", "yh", "c"), split_axis=0, concat_axis=0, tiled=True)
    both = pl.pallas_call(
        functools.partial(merge_kernel, width),
        out_shape=jax.ShapeDtypeStruct((2 * width, nvir), BF16),
        in_specs=[VMEM, VMEM],
        out_specs=VMEM,
        compiler_params=params(8),
    )(mine, other)
    ring = {0: both}
    up = down = both
    for step in range(1, nz // 2 - 1):
        up, down = shift(up, "z", 1), shift(down, "z", -1)
        ring[nz - step], ring[step] = up, down
        up, down = lax.optimization_barrier((up, down))
    far = {r: swap(ring[r], "c") for r in (0, 1, nz - 1)}
    up, down, far = lax.optimization_barrier((up, down, far))
    half_up, half_down = pl.pallas_call(
        halves_kernel,
        out_shape=(rows16, jax.ShapeDtypeStruct((2 * width - padded, nvir), BF16)),
        in_specs=[VMEM, VMEM],
        out_specs=(VMEM, VMEM),
        compiler_params=params(8),
    )(up, down)
    half_up, half_down, columns = lax.optimization_barrier((half_up, half_down, columns))
    last = (shift(down, "z", -1), shift(up, "z", 1), shift(half_up, "z", 2), shift(half_down, "z", -2))

    soon = (0, 1, nz - 1, 2, nz - 2)
    late = (3, nz - 3, nz // 2)
    far.update({r: swap(ring[r], "c") for r in (2, nz - 2)})
    ring[0] = both
    pieces = [v for r in soon for v in (ring[r], far[r])]
    state = pl.pallas_call(
        functools.partial(early_kernel, soon, nz),
        out_shape=(
            rows,
            jax.ShapeDtypeStruct((nz, padded, slab), F32),
            rows16,
            jax.ShapeDtypeStruct((nz, 2, padded, 2 * width), BF16),
        ),
        in_specs=[SMEM] + [VMEM] * (2 + 2 * len(soon)),
        out_specs=(VMEM,) * 4,
        compiler_params=params(16),
        cost_estimate=cost(len(soon) * 8 * padded * padded * nvir, len(soon) * 8 * padded * nvir),
    )(where, amp_rows, columns, *pieces)
    last, state = lax.optimization_barrier((last, state))
    added = pl.pallas_call(
        functools.partial(late_kernel, late, nz),
        out_shape=jax.ShapeDtypeStruct((nz, padded, slab), F32),
        in_specs=[SMEM] + [VMEM] * (6 + 2 * len(late)),
        out_specs=VMEM,
        compiler_params=params(16),
        cost_estimate=cost(len(late) * 8 * padded * padded * nvir, len(late) * 8 * padded * nvir),
    )(
        where,
        *state,
        last[0],
        swap(last[0], "c"),
        last[1],
        swap(last[1], "c"),
        last[2],
        last[3],
        swap(last[2], "c"),
        swap(last[3], "c"),
    )
    added = lax.all_to_all(added, SLABS, split_axis=0, concat_axis=0, tiled=True)
    return jnp.sum(added, axis=0)[:width]


def solution(mesh):
    fine = Mesh(mesh.devices.reshape(4, 2, 8, 2, 2), ("x", "yl", "z", "yh", "c"))
    pair, grid = SLABS, ("z", "yh", "c")
    in_specs = (P(None, pair, grid), P(), P(), P())
    return jax.shard_map(local, mesh=fine, in_specs=in_specs, out_specs=P(grid, pair), check_vma=False)
```

```python
import functools

import jax
import jax.numpy as jnp
from jax import lax
from jax.experimental import pallas as pl
from jax.experimental.pallas import tpu as pltpu
from jax.sharding import Mesh
from jax.sharding import PartitionSpec as P

F32 = jnp.float32
BF16 = jnp.bfloat16
SLABS = ("x", "yl")
VMEM = pl.BlockSpec(memory_space=pltpu.VMEM)
SMEM = pl.BlockSpec(memory_space=pltpu.SMEM)


def params(mib):
    return pltpu.CompilerParams(vmem_limit_bytes=mib * 1024 * 1024)


def swap(value, axis):
    return lax.ppermute(value, axis, [(0, 1), (1, 0)])


def shift(value, axis, step):
    size = lax.axis_size(axis)
    return lax.ppermute(value, axis, [(i, (i + step) % size) for i in range(size)])


def dot_nt(a, b):
    return lax.dot_general(a, b, (((1,), (1,)), ((), ())), preferred_element_type=F32)


def cost(flops, moved):
    return pl.CostEstimate(flops=flops, bytes_accessed=moved, transcendentals=0)


def fill(side, width, padded, pair_ref, orbital_ref, put):
    half = orbital_ref.shape[1] // 2
    gap = jnp.zeros((padded - width, orbital_ref.shape[2]), BF16)
    for p in range(pair_ref.shape[1]):
        left = orbital_ref[pair_ref[0, p]]
        right = orbital_ref[pair_ref[1, p]]
        for y in range(2):
            at = (2 * y + side) * width
            put(p, y, jnp.concatenate([left[at : at + width], gap], axis=0))
        put(p, 2, right[side * half : (side + 1) * half])


def select_kernel(width, padded, where_ref, pair_ref, orbital_ref, out_ref):
    def put(p, block, value):
        out_ref[p, block * padded : block * padded + value.shape[0]] = value

    for c in range(2):

        @pl.when(where_ref[1] == c)
        def _():
            fill(1 - c, width, padded, pair_ref, orbital_ref, put)


def own_kernel(width, padded, where_ref, pair_ref, orbital_ref, out_ref):
    groups, naux = pair_ref.shape[1], orbital_ref.shape[2]
    for c in range(2):
        lanes = slice(c * naux, (c + 1) * naux)

        def put(p, block, value, lanes=lanes):
            if block < 2:
                out_ref[block * groups + p, :padded, lanes] = value
            else:
                for y in range(2):
                    out_ref[y * groups + p, padded:, lanes] = value

        @pl.when(where_ref[1] == c)
        def _(c=c, put=put):
            fill(c, width, padded, pair_ref, orbital_ref, put)


def other_kernel(padded, where_ref, taken_ref, own_ref, out_ref):
    groups, naux = taken_ref.shape[0], taken_ref.shape[2]
    for c in range(2):
        lanes = slice((1 - c) * naux, (2 - c) * naux)

        @pl.when(where_ref[1] == c)
        def _(lanes=lanes):
            for p in range(groups):
                for y in range(2):
                    out_ref[y * groups + p, :padded, lanes] = taken_ref[p, y * padded : (y + 1) * padded]
                    out_ref[y * groups + p, padded:, lanes] = taken_ref[p, 2 * padded :]


def half_product(left, right_ref, padded):
    sources = right_ref.shape[0]
    half = sources // 2
    total = None
    for y in range(2):
        right = jnp.concatenate([right_ref[half * y + k, padded:, :] for k in range(half)], axis=0)
        term = dot_nt(left(y), right)
        total = term if total is None else total + term
    return total


def all_rows(near_ref, padded):
    half = near_ref.shape[0] // 2

    def left(y):
        return near_ref[half * y : half * (y + 1), :padded, :].reshape(half * padded, near_ref.shape[2])

    return left


def near_kernel(padded, where_ref, near_ref, out_ref, up_ref, down_ref):
    out_ref[...] = half_product(all_rows(near_ref, padded), near_ref, padded).reshape(out_ref.shape)
    nz, cut = out_ref.shape[0], padded // 2
    across = out_ref[lax.rem(where_ref[0] + nz // 2, nz)]
    up_ref[...] = across[:cut]
    down_ref[...] = across[cut:]


def first_kernel(padded, nz, where_ref, near_ref, far_ref, up_ref, down_ref):
    half, cut = near_ref.shape[0] // 2, padded // 2
    at = lax.rem(where_ref[0] + nz // 2, nz)
    across = half_product(lambda y: near_ref[half * y + at, :padded, :], far_ref, padded)
    up_ref[...] = across[:cut]
    down_ref[...] = across[cut:]


def rest_kernel(padded, where_ref, pair_ref, occ_ref, vir_ref, near_part_ref, near_ref, far_ref, out_ref, denom_ref):
    total = half_product(all_rows(near_ref, padded), far_ref, padded).reshape(near_part_ref.shape)
    for k in range(near_part_ref.shape[0]):
        out_ref[k] = jnp.concatenate([near_part_ref[k], total[k]], axis=1)
    chunk, group, width = where_ref[2], where_ref[3], where_ref[5]
    columns = jnp.broadcast_to(vir_ref[...], denom_ref.shape)
    place = lax.broadcasted_iota(jnp.int32, denom_ref.shape, 1)
    row = lax.broadcasted_iota(jnp.int32, denom_ref.shape, 0)
    own = jnp.sum(jnp.where(place == chunk * width + row, columns, 0.0), axis=1, keepdims=True)
    denom_ref[...] = (own + columns) - occ_ref[pair_ref[0, group]] - occ_ref[pair_ref[1, group]]


def hop_kernel(step, where_ref, part_ref, *refs):
    nz, rows = part_ref.shape[:2]
    above = lax.rem(where_ref[0] + step, nz)
    below = lax.rem(where_ref[0] + nz - step, nz)
    up_ref, down_ref = refs[-2:]
    if len(refs) == 4:
        up_ref[...] = part_ref[above] + refs[0][...]
        down_ref[...] = part_ref[below] + refs[1][...]
    else:
        cut = rows // 2
        up_ref[...] = part_ref[above]
        down_ref[...] = part_ref[below]
        up_ref[:cut] += jnp.concatenate([refs[0][...], refs[2][...]], axis=1)
        down_ref[cut:] += jnp.concatenate([refs[1][...], refs[3][...]], axis=1)


def amplitude_kernel(where_ref, part_ref, up_in, down_in, denom_ref, out_ref, rounded_ref):
    sums = part_ref[where_ref[0]] + (up_in[...] + down_in[...])
    half = sums.shape[1] // 2
    near, far = sums[:, :half], sums[:, half:]
    halves = (jnp.where(where_ref[1] == 0, near, far), jnp.where(where_ref[1] == 0, far, near))
    step = half // part_ref.shape[0]
    parts = [h[:, k * step : (k + 1) * step] for k in range(part_ref.shape[0]) for h in halves]
    amps = jnp.concatenate(parts, axis=1) / denom_ref[...]
    out_ref[...] = amps
    rounded_ref[...] = amps.astype(BF16)


def blocks_kernel(rows_ref, blocks_ref):
    count, half, lanes = blocks_ref.shape
    width = rows_ref.shape[1] // count
    gap = jnp.zeros((half, lanes // 2 - width), F32)
    for k in range(count):
        block = rows_ref[:, k * width : (k + 1) * width]
        blocks_ref[k] = jnp.concatenate([block[:half], gap, block[half:], gap], axis=1)


def merge_kernel(width, *refs):
    count = len(refs) // 3
    for n in range(count):
        first, second = refs[2 * n], refs[2 * n + 1]
        refs[2 * count + n][...] = jnp.concatenate([first[:width], second[:width]], axis=0)


def halves_kernel(up_ref, down_ref, first_ref, second_ref):
    first_ref[...] = up_ref[: first_ref.shape[0]]
    second_ref[...] = down_ref[first_ref.shape[0] :]


def natural(c, yh, near, far):
    width = near.shape[1] // 2
    parts = []
    for y in range(2):
        for h in range(2):
            side = jnp.where(c == h, near, far)
            parts.append(jnp.where(yh == y, side[:, :width], side[:, width:]))
    return jnp.concatenate(parts, axis=1)


def relative(c, yh, block):
    width = block.shape[1] // 4
    sides = []
    for h in range(2):
        first, second = block[:, h * width : (h + 1) * width], block[:, (2 + h) * width : (3 + h) * width]
        sides.append(jnp.concatenate([jnp.where(yh == 0, first, second), jnp.where(yh == 0, second, first)], axis=1))
    return jnp.where(c == 0, sides[0], sides[1]), jnp.where(c == 0, sides[1], sides[0])


def density_pieces(steps, nz, where_ref, tilde, tilde_t_ref, pieces, total, blocks_ref):
    z, c, yh = where_ref[0], where_ref[1], where_ref[6]
    rows = tilde_t_ref.shape[3]
    pieces = list(pieces)
    for r in steps:
        at = lax.rem(z + r, nz)
        sides = []
        for slot in range(2):
            piece = pieces.pop(0)[...]
            if piece.shape[0] < rows:
                piece = jnp.concatenate([piece, pieces.pop(0)[...]], axis=0)
            term = jnp.dot(tilde_t_ref[at, slot], piece, preferred_element_type=F32)
            total = term if total is None else total + term
            sides.append(dot_nt(tilde, piece))
        blocks_ref[at] = natural(c, yh, sides[0], sides[1])
    return total


def early_kernel(steps, nz, where_ref, rows_ref, columns_ref, *refs):
    pieces = refs[:-4]
    total_ref, blocks_ref, tilde_ref, tilde_t_ref = refs[-4:]
    c, yh = where_ref[1], where_ref[6]
    rows = rows_ref[...]
    padded, nvir = rows.shape
    slab = nvir // nz
    width = slab // 4

    def turn(at):
        flipped = columns_ref[at].T
        return jnp.concatenate([flipped[:padded], flipped[padded:, : width - padded // 2]], axis=1)

    turned = []
    for k in range(nz):
        near, far = (
            jnp.concatenate([turn(4 * k + 2 * yh + h), turn(4 * k + 2 * (1 - yh) + h)], axis=1) for h in (c, 1 - c)
        )
        mine = relative(c, yh, rows[:, k * slab : (k + 1) * slab])
        tilde_t_ref[k, 0] = (2.0 * near - mine[0]).astype(BF16)
        tilde_t_ref[k, 1] = (2.0 * far - mine[1]).astype(BF16)
        turned.append(natural(c, yh, near, far))
    tilde = (2.0 * rows - jnp.concatenate(turned, axis=1)).astype(BF16)
    tilde_ref[...] = tilde
    total_ref[...] = density_pieces(steps, nz, where_ref, tilde, tilde_t_ref, pieces, None, blocks_ref)


def late_kernel(steps, nz, where_ref, total_ref, blocks_ref, tilde_ref, tilde_t_ref, *refs):
    pieces, out_ref = refs[:-1], refs[-1]
    slab = total_ref.shape[1] // nz
    for k in range(nz):
        out_ref[k] = blocks_ref[k]
    total = density_pieces(
        steps, nz, where_ref, tilde_ref[...], tilde_t_ref, pieces, total_ref[...], out_ref
    )
    for k in range(nz):
        out_ref[k] += total[:, k * slab : (k + 1) * slab]


def local(orbital_b, pair_list, eps_occ, eps_vir):
    slab, naux = orbital_b.shape[1:]
    nvir = eps_vir.shape[0]
    z, yh, c = (lax.axis_index(a) for a in ("z", "yh", "c"))
    nz = lax.axis_size("z")
    width = slab // 4
    padded = (width + 8) // 8 * 8
    where = jnp.stack([z, c, z * 4 + yh * 2 + c, lax.axis_index(SLABS), yh * 2 + c, jnp.int32(width), yh])

    pairs = pair_list.T

    sent = 2 * padded + slab // 2
    theirs = pl.pallas_call(
        functools.partial(select_kernel, width, padded),
        out_shape=jax.ShapeDtypeStruct((8, sent, naux), BF16),
        in_specs=[SMEM, SMEM, VMEM],
        out_specs=VMEM,
        compiler_params=params(8),
    )(where, pairs, orbital_b)
    taken = swap(theirs, "c")
    outgoing = jax.ShapeDtypeStruct((16, sent - padded, 2 * naux), BF16)
    ours = pl.pallas_call(
        functools.partial(own_kernel, width, padded),
        out_shape=outgoing,
        in_specs=[SMEM, SMEM, VMEM],
        out_specs=VMEM,
        compiler_params=params(8),
    )(where, pairs, orbital_b)
    ours = pl.pallas_call(
        functools.partial(other_kernel, padded),
        out_shape=outgoing,
        in_specs=[SMEM, VMEM, VMEM],
        out_specs=VMEM,
        input_output_aliases={2: 0},
        compiler_params=params(8),
    )(where, taken, ours)
    near = lax.all_to_all(ours, ("yh", "x", "yl"), split_axis=0, concat_axis=0, tiled=True)
    far = swap(near, "c")

    whole = jax.ShapeDtypeStruct((8, padded, nvir), F32)
    rows = jax.ShapeDtypeStruct((padded, nvir), F32)
    quarter = jax.ShapeDtypeStruct((padded // 2, nvir // 2), F32)
    flops = 16 * padded * 8 * slab * 2 * naux
    near_part, up, down = pl.pallas_call(
        functools.partial(near_kernel, padded),
        out_shape=(jax.ShapeDtypeStruct((8, padded, nvir // 2), F32), quarter, quarter),
        in_specs=[SMEM, VMEM],
        out_specs=(VMEM,) * 3,
        compiler_params=params(16),
        cost_estimate=cost(flops, 0),
    )(where, near)
    sums = (shift(up, "z", 1), shift(down, "z", -1))
    up, down = pl.pallas_call(
        functools.partial(first_kernel, padded, nz),
        out_shape=(quarter, quarter),
        in_specs=[SMEM, VMEM, VMEM],
        out_specs=(VMEM, VMEM),
        compiler_params=params(16),
        cost_estimate=cost(flops // 8, 0),
    )(where, near, far)
    sums += (shift(up, "z", 1), shift(down, "z", -1))
    part, denom = pl.pallas_call(
        functools.partial(rest_kernel, padded),
        out_shape=(whole, rows),
        in_specs=[SMEM, SMEM, SMEM, VMEM, VMEM, VMEM, VMEM],
        out_specs=(VMEM, VMEM),
        compiler_params=params(16),
        cost_estimate=cost(flops, 0),
    )(where, pairs, eps_occ, eps_vir[None], near_part, near, far)
    for step in range(nz // 2 - 1, 0, -1):
        up, down = pl.pallas_call(
            functools.partial(hop_kernel, step),
            out_shape=(rows, rows),
            in_specs=[SMEM] + [VMEM] * (1 + len(sums)),
            out_specs=(VMEM, VMEM),
            compiler_params=params(8),
        )(where, part, *sums)
        sums = (shift(up, "z", 1), shift(down, "z", -1))
    up, down = sums
    rows16 = jax.ShapeDtypeStruct((padded, nvir), BF16)
    amp_rows, mine = pl.pallas_call(
        amplitude_kernel,
        out_shape=(rows, rows16),
        in_specs=[SMEM, VMEM, VMEM, VMEM, VMEM],
        out_specs=(VMEM, VMEM),
        compiler_params=params(8),
    )(where, part, up, down, denom)

    other = swap(mine, "yh")
    columns = pl.pallas_call(
        blocks_kernel,
        out_shape=jax.ShapeDtypeStruct((4 * nz, padded // 2, 2 * padded), F32),
        in_specs=[VMEM],
        out_specs=VMEM,
        compiler_params=params(8),
    )(amp_rows)
    other, _ = lax.optimization_barrier((other, columns))
    columns = lax.all_to_all(columns, ("z", "yh", "c"), split_axis=0, concat_axis=0, tiled=True)

    def merge(*halves):
        count = len(halves) // 2
        return pl.pallas_call(
            functools.partial(merge_kernel, width),
            out_shape=(jax.ShapeDtypeStruct((2 * width, nvir), BF16),) * count,
            in_specs=[VMEM] * (2 * count),
            out_specs=(VMEM,) * count,
            compiler_params=params(8),
        )(*halves)

    up, down = merge(shift(mine, "z", 1), shift(other, "z", 1), shift(mine, "z", -1), shift(other, "z", -1))
    (both,) = merge(mine, other)
    ring = {0: both, nz - 1: up, 1: down}
    up, down = shift(up, "z", 1), shift(down, "z", -1)
    ring[nz - 2], ring[2] = up, down
    far = {r: swap(ring[r], "c") for r in (0, 1, nz - 1)}
    up, down, far = lax.optimization_barrier((up, down, far))
    half_up, half_down = pl.pallas_call(
        halves_kernel,
        out_shape=(rows16, jax.ShapeDtypeStruct((2 * width - padded, nvir), BF16)),
        in_specs=[VMEM, VMEM],
        out_specs=(VMEM, VMEM),
        compiler_params=params(8),
    )(up, down)
    half_up, half_down, columns = lax.optimization_barrier((half_up, half_down, columns))
    last = (shift(down, "z", -1), shift(up, "z", 1), shift(half_up, "z", 2), shift(half_down, "z", -2))

    soon = (0, 1, nz - 1, 2, nz - 2)
    late = (3, nz - 3, nz // 2)
    far.update({r: swap(ring[r], "c") for r in (2, nz - 2)})
    ring[0] = both
    pieces = [v for r in soon for v in (ring[r], far[r])]
    state = pl.pallas_call(
        functools.partial(early_kernel, soon, nz),
        out_shape=(
            rows,
            jax.ShapeDtypeStruct((nz, padded, slab), F32),
            rows16,
            jax.ShapeDtypeStruct((nz, 2, padded, 2 * width), BF16),
        ),
        in_specs=[SMEM] + [VMEM] * (2 + 2 * len(soon)),
        out_specs=(VMEM,) * 4,
        compiler_params=params(16),
        cost_estimate=cost(len(soon) * 8 * padded * padded * nvir, len(soon) * 8 * padded * nvir),
    )(where, amp_rows, columns, *pieces)
    last, state = lax.optimization_barrier((last, state))
    added = pl.pallas_call(
        functools.partial(late_kernel, late, nz),
        out_shape=jax.ShapeDtypeStruct((nz, padded, slab), F32),
        in_specs=[SMEM] + [VMEM] * (6 + 2 * len(late)),
        out_specs=VMEM,
        compiler_params=params(16),
        cost_estimate=cost(len(late) * 8 * padded * padded * nvir, len(late) * 8 * padded * nvir),
    )(
        where,
        *state,
        last[0],
        swap(last[0], "c"),
        last[1],
        swap(last[1], "c"),
        last[2],
        last[3],
        swap(last[2], "c"),
        swap(last[3], "c"),
    )
    added = lax.all_to_all(added, SLABS, split_axis=0, concat_axis=0, tiled=True)
    return jnp.sum(added, axis=0)[:width]


def solution(mesh):
    fine = Mesh(mesh.devices.reshape(4, 2, 8, 2, 2), ("x", "yl", "z", "yh", "c"))
    pair, grid = SLABS, ("z", "yh", "c")
    in_specs = (P(None, pair, grid), P(), P(), P())
    return jax.shard_map(local, mesh=fine, in_specs=in_specs, out_specs=P(grid, pair), check_vma=False)
```

```python
import functools

import jax
import jax.numpy as jnp
from jax import lax
from jax.experimental import pallas as pl
from jax.experimental.pallas import tpu as pltpu
from jax.sharding import Mesh
from jax.sharding import PartitionSpec as P

F32 = jnp.float32
BF16 = jnp.bfloat16
SLABS = ("x", "yl")
VMEM = pl.BlockSpec(memory_space=pltpu.VMEM)
SMEM = pl.BlockSpec(memory_space=pltpu.SMEM)


def params(mib):
    return pltpu.CompilerParams(vmem_limit_bytes=mib * 1024 * 1024)


def swap(value, axis):
    return lax.ppermute(value, axis, [(0, 1), (1, 0)])


def shift(value, axis, step):
    size = lax.axis_size(axis)
    return lax.ppermute(value, axis, [(i, (i + step) % size) for i in range(size)])


def dot_nt(a, b):
    return lax.dot_general(a, b, (((1,), (1,)), ((), ())), preferred_element_type=F32)


def cost(flops, moved):
    return pl.CostEstimate(flops=flops, bytes_accessed=moved, transcendentals=0)


def fill(side, width, padded, pair_ref, orbital_ref, put):
    half = orbital_ref.shape[1] // 2
    gap = jnp.zeros((padded - width, orbital_ref.shape[2]), BF16)
    for p in range(pair_ref.shape[1]):
        left = orbital_ref[pair_ref[0, p]]
        right = orbital_ref[pair_ref[1, p]]
        for y in range(2):
            at = (2 * y + side) * width
            put(p, y, jnp.concatenate([left[at : at + width], gap], axis=0))
        put(p, 2, right[side * half : (side + 1) * half])


def select_kernel(width, padded, where_ref, pair_ref, orbital_ref, out_ref):
    def put(p, block, value):
        out_ref[p, block * padded : block * padded + value.shape[0]] = value

    for c in range(2):

        @pl.when(where_ref[1] == c)
        def _():
            fill(1 - c, width, padded, pair_ref, orbital_ref, put)


def own_kernel(width, padded, where_ref, pair_ref, orbital_ref, out_ref):
    groups, naux = pair_ref.shape[1], orbital_ref.shape[2]
    for c in range(2):
        lanes = slice(c * naux, (c + 1) * naux)

        def put(p, block, value, lanes=lanes):
            if block < 2:
                out_ref[block * groups + p, :padded, lanes] = value
            else:
                for y in range(2):
                    out_ref[y * groups + p, padded:, lanes] = value

        @pl.when(where_ref[1] == c)
        def _(c=c, put=put):
            fill(c, width, padded, pair_ref, orbital_ref, put)


def other_kernel(padded, where_ref, taken_ref, own_ref, out_ref):
    groups, naux = taken_ref.shape[0], taken_ref.shape[2]
    for c in range(2):
        lanes = slice((1 - c) * naux, (2 - c) * naux)

        @pl.when(where_ref[1] == c)
        def _(lanes=lanes):
            for p in range(groups):
                for y in range(2):
                    out_ref[y * groups + p, :padded, lanes] = taken_ref[p, y * padded : (y + 1) * padded]
                    out_ref[y * groups + p, padded:, lanes] = taken_ref[p, 2 * padded :]


def half_product(left, right_ref, padded):
    sources = right_ref.shape[0]
    half = sources // 2
    total = None
    for y in range(2):
        right = jnp.concatenate([right_ref[half * y + k, padded:, :] for k in range(half)], axis=0)
        term = dot_nt(left(y), right)
        total = term if total is None else total + term
    return total


def all_rows(near_ref, padded):
    half = near_ref.shape[0] // 2

    def left(y):
        return near_ref[half * y : half * (y + 1), :padded, :].reshape(half * padded, near_ref.shape[2])

    return left


def near_kernel(padded, where_ref, near_ref, out_ref, up_ref, down_ref):
    out_ref[...] = half_product(all_rows(near_ref, padded), near_ref, padded).reshape(out_ref.shape)
    nz, cut = out_ref.shape[0], padded // 2
    across = out_ref[lax.rem(where_ref[0] + nz // 2, nz)]
    up_ref[...] = across[:cut]
    down_ref[...] = across[cut:]


def first_kernel(padded, nz, where_ref, near_ref, far_ref, up_ref, down_ref):
    half, cut = near_ref.shape[0] // 2, padded // 2
    at = lax.rem(where_ref[0] + nz // 2, nz)
    across = half_product(lambda y: near_ref[half * y + at, :padded, :], far_ref, padded)
    up_ref[...] = across[:cut]
    down_ref[...] = across[cut:]


def rest_kernel(padded, where_ref, pair_ref, occ_ref, vir_ref, near_part_ref, near_ref, far_ref, out_ref, denom_ref):
    total = half_product(all_rows(near_ref, padded), far_ref, padded).reshape(near_part_ref.shape)
    for k in range(near_part_ref.shape[0]):
        out_ref[k] = jnp.concatenate([near_part_ref[k], total[k]], axis=1)
    chunk, group, width = where_ref[2], where_ref[3], where_ref[5]
    columns = jnp.broadcast_to(vir_ref[...], denom_ref.shape)
    place = lax.broadcasted_iota(jnp.int32, denom_ref.shape, 1)
    row = lax.broadcasted_iota(jnp.int32, denom_ref.shape, 0)
    own = jnp.sum(jnp.where(place == chunk * width + row, columns, 0.0), axis=1, keepdims=True)
    denom_ref[...] = (own + columns) - occ_ref[pair_ref[0, group]] - occ_ref[pair_ref[1, group]]


def hop_kernel(step, where_ref, part_ref, *refs):
    nz, rows = part_ref.shape[:2]
    above = lax.rem(where_ref[0] + step, nz)
    below = lax.rem(where_ref[0] + nz - step, nz)
    up_ref, down_ref = refs[-2:]
    if len(refs) == 4:
        up_ref[...] = part_ref[above] + refs[0][...]
        down_ref[...] = part_ref[below] + refs[1][...]
    else:
        cut = rows // 2
        up_ref[...] = part_ref[above]
        down_ref[...] = part_ref[below]
        up_ref[:cut] += jnp.concatenate([refs[0][...], refs[2][...]], axis=1)
        down_ref[cut:] += jnp.concatenate([refs[1][...], refs[3][...]], axis=1)


def amplitude_kernel(where_ref, part_ref, up_in, down_in, denom_ref, out_ref, rounded_ref):
    sums = part_ref[where_ref[0]] + (up_in[...] + down_in[...])
    half = sums.shape[1] // 2
    near, far = sums[:, :half], sums[:, half:]
    halves = (jnp.where(where_ref[1] == 0, near, far), jnp.where(where_ref[1] == 0, far, near))
    step = half // part_ref.shape[0]
    parts = [h[:, k * step : (k + 1) * step] for k in range(part_ref.shape[0]) for h in halves]
    amps = jnp.concatenate(parts, axis=1) / denom_ref[...]
    out_ref[...] = amps
    rounded_ref[...] = amps.astype(BF16)


def blocks_kernel(rows_ref, blocks_ref):
    count, rows, lanes = blocks_ref.shape
    width = rows_ref.shape[1] // count
    rest, room = width - 2 * rows, lanes - 2 * width
    left = width - room
    tails = [rows_ref[2 * rows : 3 * rows, (k + 1) * width - left : (k + 1) * width] for k in range(count)]
    tails = jnp.concatenate(tails, axis=1).T
    gap = jnp.zeros((left, room - rows), F32)
    for k in range(count):
        block = rows_ref[:, k * width : (k + 1) * width]
        tail = jnp.concatenate([tails[k * left : (k + 1) * left], gap], axis=1)
        third = jnp.concatenate([block[2 * rows : width, :room], tail], axis=0)
        blocks_ref[k] = jnp.concatenate([block[:rows], block[rows : 2 * rows], third], axis=1)


def merge_kernel(width, *refs):
    count = len(refs) // 3
    for n in range(count):
        first, second = refs[2 * n], refs[2 * n + 1]
        refs[2 * count + n][...] = jnp.concatenate([first[:width], second[:width]], axis=0)


def halves_kernel(up_ref, down_ref, first_ref, second_ref):
    first_ref[...] = up_ref[: first_ref.shape[0]]
    second_ref[...] = down_ref[first_ref.shape[0] :]


def natural(c, yh, near, far):
    width = near.shape[1] // 2
    parts = []
    for y in range(2):
        for h in range(2):
            side = jnp.where(c == h, near, far)
            parts.append(jnp.where(yh == y, side[:, :width], side[:, width:]))
    return jnp.concatenate(parts, axis=1)


def relative(c, yh, block):
    width = block.shape[1] // 4
    sides = []
    for h in range(2):
        first, second = block[:, h * width : (h + 1) * width], block[:, (2 + h) * width : (3 + h) * width]
        sides.append(jnp.concatenate([jnp.where(yh == 0, first, second), jnp.where(yh == 0, second, first)], axis=1))
    return jnp.where(c == 0, sides[0], sides[1]), jnp.where(c == 0, sides[1], sides[0])


def density_pieces(steps, nz, where_ref, tilde, tilde_t_ref, pieces, total, blocks_ref):
    z, c, yh = where_ref[0], where_ref[1], where_ref[6]
    rows = tilde_t_ref.shape[3]
    pieces = list(pieces)
    for r in steps:
        at = lax.rem(z + r, nz)
        sides = []
        for slot in range(2):
            piece = pieces.pop(0)[...]
            if piece.shape[0] < rows:
                piece = jnp.concatenate([piece, pieces.pop(0)[...]], axis=0)
            term = jnp.dot(tilde_t_ref[at, slot], piece, preferred_element_type=F32)
            total = term if total is None else total + term
            sides.append(dot_nt(tilde, piece))
        blocks_ref[at] = natural(c, yh, sides[0], sides[1])
    return total


def early_kernel(steps, nz, where_ref, rows_ref, columns_ref, *refs):
    pieces = refs[:-4]
    total_ref, blocks_ref, tilde_ref, tilde_t_ref = refs[-4:]
    c, yh = where_ref[1], where_ref[6]
    rows = rows_ref[...]
    padded, nvir = rows.shape
    slab = nvir // nz
    width = slab // 4

    def turn(at):
        block = columns_ref[at]
        flipped = block.T
        lanes, rows = flipped.shape
        rest = width - 2 * rows
        third = jnp.concatenate([flipped[2 * width :, :rest], block[rest:, 2 * width : 2 * width + rest]], axis=0)
        found = jnp.concatenate([flipped[:width], flipped[width : 2 * width], third], axis=1)
        return jnp.concatenate([found, jnp.zeros((padded - width, width), F32)], axis=0)

    turned = []
    for k in range(nz):
        near, far = (
            jnp.concatenate([turn(4 * k + 2 * yh + h), turn(4 * k + 2 * (1 - yh) + h)], axis=1) for h in (c, 1 - c)
        )
        mine = relative(c, yh, rows[:, k * slab : (k + 1) * slab])
        tilde_t_ref[k, 0] = (2.0 * near - mine[0]).astype(BF16)
        tilde_t_ref[k, 1] = (2.0 * far - mine[1]).astype(BF16)
        turned.append(natural(c, yh, near, far))
    tilde = (2.0 * rows - jnp.concatenate(turned, axis=1)).astype(BF16)
    tilde_ref[...] = tilde
    total_ref[...] = density_pieces(steps, nz, where_ref, tilde, tilde_t_ref, pieces, None, blocks_ref)


def late_kernel(steps, nz, where_ref, total_ref, blocks_ref, tilde_ref, tilde_t_ref, *refs):
    pieces, out_ref = refs[:-1], refs[-1]
    slab = total_ref.shape[1] // nz
    for k in range(nz):
        out_ref[k] = blocks_ref[k]
    total = density_pieces(
        steps, nz, where_ref, tilde_ref[...], tilde_t_ref, pieces, total_ref[...], out_ref
    )
    for k in range(nz):
        out_ref[k] += total[:, k * slab : (k + 1) * slab]


def local(orbital_b, pair_list, eps_occ, eps_vir):
    slab, naux = orbital_b.shape[1:]
    nvir = eps_vir.shape[0]
    z, yh, c = (lax.axis_index(a) for a in ("z", "yh", "c"))
    nz = lax.axis_size("z")
    width = slab // 4
    padded = (width + 8) // 8 * 8
    where = jnp.stack([z, c, z * 4 + yh * 2 + c, lax.axis_index(SLABS), yh * 2 + c, jnp.int32(width), yh])

    pairs = pair_list.T

    sent = 2 * padded + slab // 2
    theirs = pl.pallas_call(
        functools.partial(select_kernel, width, padded),
        out_shape=jax.ShapeDtypeStruct((8, sent, naux), BF16),
        in_specs=[SMEM, SMEM, VMEM],
        out_specs=VMEM,
        compiler_params=params(8),
    )(where, pairs, orbital_b)
    taken = swap(theirs, "c")
    outgoing = jax.ShapeDtypeStruct((16, sent - padded, 2 * naux), BF16)
    ours = pl.pallas_call(
        functools.partial(own_kernel, width, padded),
        out_shape=outgoing,
        in_specs=[SMEM, SMEM, VMEM],
        out_specs=VMEM,
        compiler_params=params(8),
    )(where, pairs, orbital_b)
    ours = pl.pallas_call(
        functools.partial(other_kernel, padded),
        out_shape=outgoing,
        in_specs=[SMEM, VMEM, VMEM],
        out_specs=VMEM,
        input_output_aliases={2: 0},
        compiler_params=params(8),
    )(where, taken, ours)
    near = lax.all_to_all(ours, ("yh", "x", "yl"), split_axis=0, concat_axis=0, tiled=True)
    far = swap(near, "c")

    whole = jax.ShapeDtypeStruct((8, padded, nvir), F32)
    rows = jax.ShapeDtypeStruct((padded, nvir), F32)
    quarter = jax.ShapeDtypeStruct((padded // 2, nvir // 2), F32)
    flops = 16 * padded * 8 * slab * 2 * naux
    near_part, up, down = pl.pallas_call(
        functools.partial(near_kernel, padded),
        out_shape=(jax.ShapeDtypeStruct((8, padded, nvir // 2), F32), quarter, quarter),
        in_specs=[SMEM, VMEM],
        out_specs=(VMEM,) * 3,
        compiler_params=params(16),
        cost_estimate=cost(flops, 0),
    )(where, near)
    sums = (shift(up, "z", 1), shift(down, "z", -1))
    up, down = pl.pallas_call(
        functools.partial(first_kernel, padded, nz),
        out_shape=(quarter, quarter),
        in_specs=[SMEM, VMEM, VMEM],
        out_specs=(VMEM, VMEM),
        compiler_params=params(16),
        cost_estimate=cost(flops // 8, 0),
    )(where, near, far)
    sums += (shift(up, "z", 1), shift(down, "z", -1))
    part, denom = pl.pallas_call(
        functools.partial(rest_kernel, padded),
        out_shape=(whole, rows),
        in_specs=[SMEM, SMEM, SMEM, VMEM, VMEM, VMEM, VMEM],
        out_specs=(VMEM, VMEM),
        compiler_params=params(16),
        cost_estimate=cost(flops, 0),
    )(where, pairs, eps_occ, eps_vir[None], near_part, near, far)
    for step in range(nz // 2 - 1, 0, -1):
        up, down = pl.pallas_call(
            functools.partial(hop_kernel, step),
            out_shape=(rows, rows),
            in_specs=[SMEM] + [VMEM] * (1 + len(sums)),
            out_specs=(VMEM, VMEM),
            compiler_params=params(8),
        )(where, part, *sums)
        sums = (shift(up, "z", 1), shift(down, "z", -1))
    up, down = sums
    rows16 = jax.ShapeDtypeStruct((padded, nvir), BF16)
    amp_rows, mine = pl.pallas_call(
        amplitude_kernel,
        out_shape=(rows, rows16),
        in_specs=[SMEM, VMEM, VMEM, VMEM, VMEM],
        out_specs=(VMEM, VMEM),
        compiler_params=params(8),
    )(where, part, up, down, denom)

    other = swap(mine, "yh")
    columns = pl.pallas_call(
        blocks_kernel,
        out_shape=jax.ShapeDtypeStruct((4 * nz, 16, 128), F32),
        in_specs=[VMEM],
        out_specs=VMEM,
        compiler_params=params(8),
    )(amp_rows)
    other, _ = lax.optimization_barrier((other, columns))
    columns = lax.all_to_all(columns, ("z", "yh", "c"), split_axis=0, concat_axis=0, tiled=True)

    def merge(*halves):
        count = len(halves) // 2
        return pl.pallas_call(
            functools.partial(merge_kernel, width),
            out_shape=(jax.ShapeDtypeStruct((2 * width, nvir), BF16),) * count,
            in_specs=[VMEM] * (2 * count),
            out_specs=(VMEM,) * count,
            compiler_params=params(8),
        )(*halves)

    up, down = merge(shift(mine, "z", 1), shift(other, "z", 1), shift(mine, "z", -1), shift(other, "z", -1))
    (both,) = merge(mine, other)
    ring = {0: both, nz - 1: up, 1: down}
    up, down = shift(up, "z", 1), shift(down, "z", -1)
    ring[nz - 2], ring[2] = up, down
    far = {r: swap(ring[r], "c") for r in (0, 1, nz - 1)}
    up, down, far = lax.optimization_barrier((up, down, far))
    half_up, half_down = pl.pallas_call(
        halves_kernel,
        out_shape=(rows16, jax.ShapeDtypeStruct((2 * width - padded, nvir), BF16)),
        in_specs=[VMEM, VMEM],
        out_specs=(VMEM, VMEM),
        compiler_params=params(8),
    )(up, down)
    half_up, half_down, columns = lax.optimization_barrier((half_up, half_down, columns))
    last = (shift(down, "z", -1), shift(up, "z", 1), shift(half_up, "z", 2), shift(half_down, "z", -2))

    soon = (0, 1, nz - 1, 2, nz - 2)
    late = (3, nz - 3, nz // 2)
    far.update({r: swap(ring[r], "c") for r in (2, nz - 2)})
    ring[0] = both
    pieces = [v for r in soon for v in (ring[r], far[r])]
    state = pl.pallas_call(
        functools.partial(early_kernel, soon, nz),
        out_shape=(
            rows,
            jax.ShapeDtypeStruct((nz, padded, slab), F32),
            rows16,
            jax.ShapeDtypeStruct((nz, 2, padded, 2 * width), BF16),
        ),
        in_specs=[SMEM] + [VMEM] * (2 + 2 * len(soon)),
        out_specs=(VMEM,) * 4,
        compiler_params=params(16),
        cost_estimate=cost(len(soon) * 8 * padded * padded * nvir, len(soon) * 8 * padded * nvir),
    )(where, amp_rows, columns, *pieces)
    last, state = lax.optimization_barrier((last, state))
    added = pl.pallas_call(
        functools.partial(late_kernel, late, nz),
        out_shape=jax.ShapeDtypeStruct((nz, padded, slab), F32),
        in_specs=[SMEM] + [VMEM] * (6 + 2 * len(late)),
        out_specs=VMEM,
        compiler_params=params(16),
        cost_estimate=cost(len(late) * 8 * padded * padded * nvir, len(late) * 8 * padded * nvir),
    )(
        where,
        *state,
        last[0],
        swap(last[0], "c"),
        last[1],
        swap(last[1], "c"),
        last[2],
        last[3],
        swap(last[2], "c"),
        swap(last[3], "c"),
    )
    added = lax.all_to_all(added, SLABS, split_axis=0, concat_axis=0, tiled=True)
    return jnp.sum(added, axis=0)[:width]


def solution(mesh):
    fine = Mesh(mesh.devices.reshape(4, 2, 8, 2, 2), ("x", "yl", "z", "yh", "c"))
    pair, grid = SLABS, ("z", "yh", "c")
    in_specs = (P(None, pair, grid), P(), P(), P())
    return jax.shard_map(local, mesh=fine, in_specs=in_specs, out_specs=P(grid, pair), check_vma=False)
```

```python
import functools

import jax
import jax.numpy as jnp
from jax import lax
from jax.experimental import pallas as pl
from jax.experimental.pallas import tpu as pltpu
from jax.sharding import Mesh
from jax.sharding import PartitionSpec as P

F32 = jnp.float32
BF16 = jnp.bfloat16
SLABS = ("x", "yl")
VMEM = pl.BlockSpec(memory_space=pltpu.VMEM)
SMEM = pl.BlockSpec(memory_space=pltpu.SMEM)


def params(mib):
    return pltpu.CompilerParams(vmem_limit_bytes=mib * 1024 * 1024)


def swap(value, axis):
    return lax.ppermute(value, axis, [(0, 1), (1, 0)])


def shift(value, axis, step):
    size = lax.axis_size(axis)
    return lax.ppermute(value, axis, [(i, (i + step) % size) for i in range(size)])


def dot_nt(a, b):
    return lax.dot_general(a, b, (((1,), (1,)), ((), ())), preferred_element_type=F32)


def cost(flops, moved):
    return pl.CostEstimate(flops=flops, bytes_accessed=moved, transcendentals=0)


def fill(side, width, padded, pair_ref, orbital_ref, put):
    half = orbital_ref.shape[1] // 2
    gap = jnp.zeros((padded - width, orbital_ref.shape[2]), BF16)
    for p in range(pair_ref.shape[1]):
        left = orbital_ref[pair_ref[0, p]]
        right = orbital_ref[pair_ref[1, p]]
        for y in range(2):
            at = (2 * y + side) * width
            put(p, y, jnp.concatenate([left[at : at + width], gap], axis=0))
        put(p, 2, right[side * half : (side + 1) * half])


def select_kernel(width, padded, where_ref, pair_ref, orbital_ref, out_ref):
    def put(p, block, value):
        out_ref[p, block * padded : block * padded + value.shape[0]] = value

    for c in range(2):

        @pl.when(where_ref[1] == c)
        def _():
            fill(1 - c, width, padded, pair_ref, orbital_ref, put)


def own_kernel(width, padded, where_ref, pair_ref, orbital_ref, out_ref):
    groups, naux = pair_ref.shape[1], orbital_ref.shape[2]
    for c in range(2):
        lanes = slice(c * naux, (c + 1) * naux)

        def put(p, block, value, lanes=lanes):
            if block < 2:
                out_ref[block * groups + p, :padded, lanes] = value
            else:
                for y in range(2):
                    out_ref[y * groups + p, padded:, lanes] = value

        @pl.when(where_ref[1] == c)
        def _(c=c, put=put):
            fill(c, width, padded, pair_ref, orbital_ref, put)


def other_kernel(padded, where_ref, taken_ref, own_ref, out_ref):
    groups, naux = taken_ref.shape[0], taken_ref.shape[2]
    for c in range(2):
        lanes = slice((1 - c) * naux, (2 - c) * naux)

        @pl.when(where_ref[1] == c)
        def _(lanes=lanes):
            for p in range(groups):
                for y in range(2):
                    out_ref[y * groups + p, :padded, lanes] = taken_ref[p, y * padded : (y + 1) * padded]
                    out_ref[y * groups + p, padded:, lanes] = taken_ref[p, 2 * padded :]


def half_product(left, right_ref, padded):
    sources = right_ref.shape[0]
    half = sources // 2
    total = None
    for y in range(2):
        right = jnp.concatenate([right_ref[half * y + k, padded:, :] for k in range(half)], axis=0)
        term = dot_nt(left(y), right)
        total = term if total is None else total + term
    return total


def all_rows(near_ref, padded):
    half = near_ref.shape[0] // 2

    def left(y):
        return near_ref[half * y : half * (y + 1), :padded, :].reshape(half * padded, near_ref.shape[2])

    return left


def near_kernel(padded, where_ref, near_ref, out_ref, up_ref, down_ref):
    out_ref[...] = half_product(all_rows(near_ref, padded), near_ref, padded).reshape(out_ref.shape)
    nz, cut = out_ref.shape[0], padded // 2
    across = out_ref[lax.rem(where_ref[0] + nz // 2, nz)]
    up_ref[...] = across[:cut]
    down_ref[...] = across[cut:]


def first_kernel(padded, nz, where_ref, near_ref, far_ref, up_ref, down_ref):
    half, cut = near_ref.shape[0] // 2, padded // 2
    at = lax.rem(where_ref[0] + nz // 2, nz)
    across = half_product(lambda y: near_ref[half * y + at, :padded, :], far_ref, padded)
    up_ref[...] = across[:cut]
    down_ref[...] = across[cut:]


def rest_kernel(padded, where_ref, pair_ref, occ_ref, vir_ref, near_part_ref, near_ref, far_ref, out_ref, denom_ref):
    total = half_product(all_rows(near_ref, padded), far_ref, padded).reshape(near_part_ref.shape)
    for k in range(near_part_ref.shape[0]):
        out_ref[k] = jnp.concatenate([near_part_ref[k], total[k]], axis=1)
    chunk, group, width = where_ref[2], where_ref[3], where_ref[5]
    columns = jnp.broadcast_to(vir_ref[...], denom_ref.shape)
    place = lax.broadcasted_iota(jnp.int32, denom_ref.shape, 1)
    row = lax.broadcasted_iota(jnp.int32, denom_ref.shape, 0)
    own = jnp.sum(jnp.where(place == chunk * width + row, columns, 0.0), axis=1, keepdims=True)
    denom_ref[...] = (own + columns) - occ_ref[pair_ref[0, group]] - occ_ref[pair_ref[1, group]]


def hop_kernel(step, where_ref, part_ref, *refs):
    nz, rows = part_ref.shape[:2]
    above = lax.rem(where_ref[0] + step, nz)
    below = lax.rem(where_ref[0] + nz - step, nz)
    up_ref, down_ref = refs[-2:]
    if len(refs) == 4:
        up_ref[...] = part_ref[above] + refs[0][...]
        down_ref[...] = part_ref[below] + refs[1][...]
    else:
        cut = rows // 2
        up_ref[...] = part_ref[above]
        down_ref[...] = part_ref[below]
        up_ref[:cut] += jnp.concatenate([refs[0][...], refs[2][...]], axis=1)
        down_ref[cut:] += jnp.concatenate([refs[1][...], refs[3][...]], axis=1)


def amplitude_kernel(where_ref, part_ref, up_in, down_in, denom_ref, out_ref, rounded_ref):
    sums = part_ref[where_ref[0]] + (up_in[...] + down_in[...])
    half = sums.shape[1] // 2
    near, far = sums[:, :half], sums[:, half:]
    halves = (jnp.where(where_ref[1] == 0, near, far), jnp.where(where_ref[1] == 0, far, near))
    step = half // part_ref.shape[0]
    parts = [h[:, k * step : (k + 1) * step] for k in range(part_ref.shape[0]) for h in halves]
    amps = jnp.concatenate(parts, axis=1) / denom_ref[...]
    out_ref[...] = amps
    rounded_ref[...] = amps.astype(BF16)


def blocks_kernel(rows_ref, blocks_ref):
    count, rows, lanes = blocks_ref.shape
    width = rows_ref.shape[1] // count
    rest, room = width - 2 * rows, lanes - 2 * width
    left = width - room
    tails = [rows_ref[2 * rows : 3 * rows, (k + 1) * width - left : (k + 1) * width] for k in range(count)]
    tails = jnp.concatenate(tails, axis=1).T
    gap = jnp.zeros((left, room - rows), F32)
    for k in range(count):
        block = rows_ref[:, k * width : (k + 1) * width]
        tail = jnp.concatenate([tails[k * left : (k + 1) * left], gap], axis=1)
        third = jnp.concatenate([block[2 * rows : width, :room], tail], axis=0)
        blocks_ref[k] = jnp.concatenate([block[:rows], block[rows : 2 * rows], third], axis=1)


def merge_kernel(width, *refs):
    count = len(refs) // 3
    for n in range(count):
        first, second = refs[2 * n], refs[2 * n + 1]
        refs[2 * count + n][...] = jnp.concatenate([first[:width], second[:width]], axis=0)


def halves_kernel(up_ref, down_ref, after_ref, first_ref, second_ref):
    first_ref[...] = up_ref[: first_ref.shape[0]]
    second_ref[...] = down_ref[down_ref.shape[0] - second_ref.shape[0] :]


def natural(c, yh, near, far):
    width = near.shape[1] // 2
    parts = []
    for y in range(2):
        for h in range(2):
            side = jnp.where(c == h, near, far)
            parts.append(jnp.where(yh == y, side[:, :width], side[:, width:]))
    return jnp.concatenate(parts, axis=1)


def relative(c, yh, block):
    width = block.shape[1] // 4
    sides = []
    for h in range(2):
        first, second = block[:, h * width : (h + 1) * width], block[:, (2 + h) * width : (3 + h) * width]
        sides.append(jnp.concatenate([jnp.where(yh == 0, first, second), jnp.where(yh == 0, second, first)], axis=1))
    return jnp.where(c == 0, sides[0], sides[1]), jnp.where(c == 0, sides[1], sides[0])


def density_pieces(steps, nz, where_ref, tilde, tilde_t_ref, pieces, total, blocks_ref):
    z, c, yh = where_ref[0], where_ref[1], where_ref[6]
    rows = tilde_t_ref.shape[3]
    pieces = list(pieces)
    for r in steps:
        at = lax.rem(z + r, nz)
        sides = []
        for slot in range(2):
            piece = pieces.pop(0)[...]
            if piece.shape[0] < rows:
                piece = jnp.concatenate([piece, pieces.pop(0)[2 * piece.shape[0] - rows :]], axis=0)
            term = jnp.dot(tilde_t_ref[at, slot], piece, preferred_element_type=F32)
            total = term if total is None else total + term
            sides.append(dot_nt(tilde, piece))
        blocks_ref[at] = natural(c, yh, sides[0], sides[1])
    return total


def early_kernel(steps, nz, where_ref, rows_ref, columns_ref, *refs):
    pieces = refs[:-4]
    total_ref, blocks_ref, tilde_ref, tilde_t_ref = refs[-4:]
    c, yh = where_ref[1], where_ref[6]
    rows = rows_ref[...]
    padded, nvir = rows.shape
    slab = nvir // nz
    width = slab // 4

    def turn(at):
        block = columns_ref[at]
        flipped = block.T
        lanes, rows = flipped.shape
        rest = width - 2 * rows
        third = jnp.concatenate([flipped[2 * width :, :rest], block[rest:, 2 * width : 2 * width + rest]], axis=0)
        found = jnp.concatenate([flipped[:width], flipped[width : 2 * width], third], axis=1)
        return jnp.concatenate([found, jnp.zeros((padded - width, width), F32)], axis=0)

    turned = []
    for k in range(nz):
        near, far = (
            jnp.concatenate([turn(4 * k + 2 * yh + h), turn(4 * k + 2 * (1 - yh) + h)], axis=1) for h in (c, 1 - c)
        )
        mine = relative(c, yh, rows[:, k * slab : (k + 1) * slab])
        tilde_t_ref[k, 0] = (2.0 * near - mine[0]).astype(BF16)
        tilde_t_ref[k, 1] = (2.0 * far - mine[1]).astype(BF16)
        turned.append(natural(c, yh, near, far))
    tilde = (2.0 * rows - jnp.concatenate(turned, axis=1)).astype(BF16)
    tilde_ref[...] = tilde
    total_ref[...] = density_pieces(steps, nz, where_ref, tilde, tilde_t_ref, pieces, None, blocks_ref)


def late_kernel(steps, nz, where_ref, total_ref, blocks_ref, tilde_ref, tilde_t_ref, *refs):
    pieces, out_ref, sums_ref = refs[:-2], refs[-2], refs[-1]
    padded, nvir = total_ref.shape
    slab = nvir // nz
    lanes = out_ref.shape[2]
    gap = jnp.zeros((padded // 2, 3 * lanes - 2 * slab), F32)
    for k in range(nz):
        sums_ref[k] = blocks_ref[k]
    total = density_pieces(
        steps, nz, where_ref, tilde_ref[...], tilde_t_ref, pieces, total_ref[...], sums_ref
    )
    for k in range(nz):
        block = sums_ref[k] + total[:, k * slab : (k + 1) * slab]
        out_ref[k, :padded] = block[:, :lanes]
        rest = block[:, lanes:]
        out_ref[k, padded:] = jnp.concatenate([rest[: padded // 2], rest[padded // 2 :], gap], axis=1)


def sum_kernel(parts_ref, out_ref):
    width, slab = out_ref.shape
    total = parts_ref[0]
    for k in range(1, parts_ref.shape[0]):
        total = total + parts_ref[k]
    rows, lanes = total.shape[0] * 2 // 3, total.shape[1]
    rest = total[rows:]
    extra = slab - lanes
    rest = jnp.concatenate([rest[:, :extra], rest[:, extra : 2 * extra]], axis=0)
    out_ref[...] = jnp.concatenate([total[:rows], rest], axis=1)[:width]


def local(orbital_b, pair_list, eps_occ, eps_vir):
    slab, naux = orbital_b.shape[1:]
    nvir = eps_vir.shape[0]
    z, yh, c = (lax.axis_index(a) for a in ("z", "yh", "c"))
    nz = lax.axis_size("z")
    width = slab // 4
    padded = (width + 8) // 8 * 8
    where = jnp.stack([z, c, z * 4 + yh * 2 + c, lax.axis_index(SLABS), yh * 2 + c, jnp.int32(width), yh])

    pairs = pair_list.T

    sent = 2 * padded + slab // 2
    theirs = pl.pallas_call(
        functools.partial(select_kernel, width, padded),
        out_shape=jax.ShapeDtypeStruct((8, sent, naux), BF16),
        in_specs=[SMEM, SMEM, VMEM],
        out_specs=VMEM,
        compiler_params=params(8),
    )(where, pairs, orbital_b)
    taken = swap(theirs, "c")
    outgoing = jax.ShapeDtypeStruct((16, sent - padded, 2 * naux), BF16)
    ours = pl.pallas_call(
        functools.partial(own_kernel, width, padded),
        out_shape=outgoing,
        in_specs=[SMEM, SMEM, VMEM],
        out_specs=VMEM,
        compiler_params=params(8),
    )(where, pairs, orbital_b)
    ours = pl.pallas_call(
        functools.partial(other_kernel, padded),
        out_shape=outgoing,
        in_specs=[SMEM, VMEM, VMEM],
        out_specs=VMEM,
        input_output_aliases={2: 0},
        compiler_params=params(8),
    )(where, taken, ours)
    near = lax.all_to_all(ours, ("yh", "x", "yl"), split_axis=0, concat_axis=0, tiled=True)
    far = swap(near, "c")

    whole = jax.ShapeDtypeStruct((8, padded, nvir), F32)
    rows = jax.ShapeDtypeStruct((padded, nvir), F32)
    quarter = jax.ShapeDtypeStruct((padded // 2, nvir // 2), F32)
    flops = 16 * padded * 8 * slab * 2 * naux
    near_part, up, down = pl.pallas_call(
        functools.partial(near_kernel, padded),
        out_shape=(jax.ShapeDtypeStruct((8, padded, nvir // 2), F32), quarter, quarter),
        in_specs=[SMEM, VMEM],
        out_specs=(VMEM,) * 3,
        compiler_params=params(16),
        cost_estimate=cost(flops, 0),
    )(where, near)
    sums = (shift(up, "z", 1), shift(down, "z", -1))
    up, down = pl.pallas_call(
        functools.partial(first_kernel, padded, nz),
        out_shape=(quarter, quarter),
        in_specs=[SMEM, VMEM, VMEM],
        out_specs=(VMEM, VMEM),
        compiler_params=params(16),
        cost_estimate=cost(flops // 8, 0),
    )(where, near, far)
    sums += (shift(up, "z", 1), shift(down, "z", -1))
    part, denom = pl.pallas_call(
        functools.partial(rest_kernel, padded),
        out_shape=(whole, rows),
        in_specs=[SMEM, SMEM, SMEM, VMEM, VMEM, VMEM, VMEM],
        out_specs=(VMEM, VMEM),
        compiler_params=params(16),
        cost_estimate=cost(flops, 0),
    )(where, pairs, eps_occ, eps_vir[None], near_part, near, far)
    for step in range(nz // 2 - 1, 0, -1):
        up, down = pl.pallas_call(
            functools.partial(hop_kernel, step),
            out_shape=(rows, rows),
            in_specs=[SMEM] + [VMEM] * (1 + len(sums)),
            out_specs=(VMEM, VMEM),
            compiler_params=params(8),
        )(where, part, *sums)
        sums = (shift(up, "z", 1), shift(down, "z", -1))
    up, down = sums
    rows16 = jax.ShapeDtypeStruct((padded, nvir), BF16)
    amp_rows, mine = pl.pallas_call(
        amplitude_kernel,
        out_shape=(rows, rows16),
        in_specs=[SMEM, VMEM, VMEM, VMEM, VMEM],
        out_specs=(VMEM, VMEM),
        compiler_params=params(8),
    )(where, part, up, down, denom)

    other = swap(mine, "yh")
    columns = pl.pallas_call(
        blocks_kernel,
        out_shape=jax.ShapeDtypeStruct((4 * nz, 16, 128), F32),
        in_specs=[VMEM],
        out_specs=VMEM,
        compiler_params=params(8),
    )(amp_rows)
    other, _ = lax.optimization_barrier((other, columns))
    columns = lax.all_to_all(columns, ("z", "yh", "c"), split_axis=0, concat_axis=0, tiled=True)

    def merge(*halves):
        count = len(halves) // 2
        return pl.pallas_call(
            functools.partial(merge_kernel, width),
            out_shape=(jax.ShapeDtypeStruct((2 * width, nvir), BF16),) * count,
            in_specs=[VMEM] * (2 * count),
            out_specs=(VMEM,) * count,
            compiler_params=params(8),
        )(*halves)

    up, down = merge(shift(mine, "z", 1), shift(other, "z", 1), shift(mine, "z", -1), shift(other, "z", -1))
    (both,) = merge(mine, other)
    ring = {0: both, nz - 1: up, 1: down}
    up, down = shift(up, "z", 1), shift(down, "z", -1)
    ring[nz - 2], ring[2] = up, down
    far = {r: swap(ring[r], "c") for r in (0, 1, nz - 1)}
    up, down, far = lax.optimization_barrier((up, down, far))
    half_up, half_down = pl.pallas_call(
        halves_kernel,
        out_shape=(rows16, rows16),
        in_specs=[VMEM, VMEM, pl.BlockSpec(memory_space=pl.ANY)],
        out_specs=(VMEM, VMEM),
        compiler_params=params(8),
    )(up, down, columns)
    last = (shift(down, "z", -1), shift(up, "z", 1), shift(half_up, "z", 2), shift(half_down, "z", -2))

    soon = (0, 1, nz - 1, 2, nz - 2)
    late = (3, nz - 3, nz // 2)
    far.update({r: swap(ring[r], "c") for r in (2, nz - 2)})
    ring[0] = both
    pieces = [v for r in soon for v in (ring[r], far[r])]
    state = pl.pallas_call(
        functools.partial(early_kernel, soon, nz),
        out_shape=(
            rows,
            jax.ShapeDtypeStruct((nz, padded, slab), F32),
            rows16,
            jax.ShapeDtypeStruct((nz, 2, padded, 2 * width), BF16),
        ),
        in_specs=[SMEM] + [VMEM] * (2 + 2 * len(soon)),
        out_specs=(VMEM,) * 4,
        compiler_params=params(16),
        cost_estimate=cost(len(soon) * 8 * padded * padded * nvir, len(soon) * 8 * padded * nvir),
    )(where, amp_rows, columns, *pieces)
    last, state = lax.optimization_barrier((last, state))
    added = pl.pallas_call(
        functools.partial(late_kernel, late, nz),
        out_shape=jax.ShapeDtypeStruct((nz, padded * 3 // 2, 128), F32),
        in_specs=[SMEM] + [VMEM] * (6 + 2 * len(late)),
        out_specs=VMEM,
        scratch_shapes=[pltpu.VMEM((nz, padded, slab), F32)],
        compiler_params=params(16),
        cost_estimate=cost(len(late) * 8 * padded * padded * nvir, len(late) * 8 * padded * nvir),
    )(
        where,
        *state,
        last[0],
        swap(last[0], "c"),
        last[1],
        swap(last[1], "c"),
        last[2],
        last[3],
        swap(last[2], "c"),
        swap(last[3], "c"),
    )
    added = lax.all_to_all(added, SLABS, split_axis=0, concat_axis=0, tiled=True)
    return pl.pallas_call(
        sum_kernel,
        out_shape=jax.ShapeDtypeStruct((width, slab), F32),
        in_specs=[VMEM],
        out_specs=VMEM,
        compiler_params=params(8),
    )(added)


def solution(mesh):
    fine = Mesh(mesh.devices.reshape(4, 2, 8, 2, 2), ("x", "yl", "z", "yh", "c"))
    pair, grid = SLABS, ("z", "yh", "c")
    in_specs = (P(None, pair, grid), P(), P(), P())
    return jax.shard_map(local, mesh=fine, in_specs=in_specs, out_specs=P(grid, pair), check_vma=False)
```

```python
import functools

import jax
import jax.numpy as jnp
from jax import lax
from jax.experimental import pallas as pl
from jax.experimental.pallas import tpu as pltpu
from jax.sharding import Mesh
from jax.sharding import PartitionSpec as P

F32 = jnp.float32
BF16 = jnp.bfloat16
SLABS = ("x", "yl")
VMEM = pl.BlockSpec(memory_space=pltpu.VMEM)
SMEM = pl.BlockSpec(memory_space=pltpu.SMEM)


def params(mib):
    return pltpu.CompilerParams(vmem_limit_bytes=mib * 1024 * 1024)


def swap(value, axis):
    return lax.ppermute(value, axis, [(0, 1), (1, 0)])


def shift(value, axis, step):
    size = lax.axis_size(axis)
    return lax.ppermute(value, axis, [(i, (i + step) % size) for i in range(size)])


def dot_nt(a, b):
    return lax.dot_general(a, b, (((1,), (1,)), ((), ())), preferred_element_type=F32)


def cost(flops, moved):
    return pl.CostEstimate(flops=flops, bytes_accessed=moved, transcendentals=0)


def fill(side, width, padded, pair_ref, orbital_ref, put):
    half = orbital_ref.shape[1] // 2
    gap = jnp.zeros((padded - width, orbital_ref.shape[2]), BF16)
    for p in range(pair_ref.shape[1]):
        left = orbital_ref[pair_ref[0, p]]
        right = orbital_ref[pair_ref[1, p]]
        for y in range(2):
            at = (2 * y + side) * width
            put(p, y, jnp.concatenate([left[at : at + width], gap], axis=0))
        put(p, 2, right[side * half : (side + 1) * half])


def select_kernel(width, padded, where_ref, pair_ref, orbital_ref, out_ref):
    def put(p, block, value):
        out_ref[p, block * padded : block * padded + value.shape[0]] = value

    for c in range(2):

        @pl.when(where_ref[1] == c)
        def _():
            fill(1 - c, width, padded, pair_ref, orbital_ref, put)


def own_kernel(width, padded, where_ref, pair_ref, orbital_ref, out_ref):
    groups, naux = pair_ref.shape[1], orbital_ref.shape[2]
    for c in range(2):
        lanes = slice(c * naux, (c + 1) * naux)

        def put(p, block, value, lanes=lanes):
            if block < 2:
                out_ref[block * groups + p, :padded, lanes] = value
            else:
                for y in range(2):
                    out_ref[y * groups + p, padded:, lanes] = value

        @pl.when(where_ref[1] == c)
        def _(c=c, put=put):
            fill(c, width, padded, pair_ref, orbital_ref, put)


def other_kernel(padded, where_ref, taken_ref, own_ref, out_ref):
    groups, naux = taken_ref.shape[0], taken_ref.shape[2]
    for c in range(2):
        lanes = slice((1 - c) * naux, (2 - c) * naux)

        @pl.when(where_ref[1] == c)
        def _(lanes=lanes):
            for p in range(groups):
                for y in range(2):
                    out_ref[y * groups + p, :padded, lanes] = taken_ref[p, y * padded : (y + 1) * padded]
                    out_ref[y * groups + p, padded:, lanes] = taken_ref[p, 2 * padded :]


def half_product(left, right_ref, start):
    sources = right_ref.shape[0]
    half = sources // 2
    total = None
    for y in range(2):
        right = jnp.concatenate([right_ref[half * y + k, start:, :] for k in range(half)], axis=0)
        term = dot_nt(left(y), right)
        total = term if total is None else total + term
    return total


def all_rows(near_ref, padded):
    half = near_ref.shape[0] // 2

    def left(y):
        return near_ref[half * y : half * (y + 1), :padded, :].reshape(half * padded, near_ref.shape[2])

    return left


def near_kernel(padded, where_ref, near_ref, out_ref, up_ref, down_ref):
    out_ref[...] = half_product(all_rows(near_ref, padded), near_ref, padded).reshape(out_ref.shape)
    nz, cut = out_ref.shape[0], padded // 2
    across = out_ref[lax.rem(where_ref[0] + nz // 2, nz)]
    up_ref[...] = across[:cut]
    down_ref[...] = across[cut:]


def first_kernel(padded, nz, where_ref, near_ref, far_ref, up_ref, down_ref):
    half, cut = near_ref.shape[0] // 2, padded // 2
    at = lax.rem(where_ref[0] + nz // 2, nz)
    across = half_product(lambda y: near_ref[half * y + at, :padded, :], far_ref, 0)
    up_ref[...] = across[:cut]
    down_ref[...] = across[cut:]


def rest_kernel(padded, where_ref, pair_ref, occ_ref, vir_ref, near_part_ref, near_ref, far_ref, out_ref, denom_ref):
    total = half_product(all_rows(near_ref, padded), far_ref, 0).reshape(near_part_ref.shape)
    for k in range(near_part_ref.shape[0]):
        out_ref[k] = jnp.concatenate([near_part_ref[k], total[k]], axis=1)
    chunk, group, width = where_ref[2], where_ref[3], where_ref[5]
    columns = jnp.broadcast_to(vir_ref[...], denom_ref.shape)
    place = lax.broadcasted_iota(jnp.int32, denom_ref.shape, 1)
    row = lax.broadcasted_iota(jnp.int32, denom_ref.shape, 0)
    own = jnp.sum(jnp.where(place == chunk * width + row, columns, 0.0), axis=1, keepdims=True)
    denom_ref[...] = (own + columns) - occ_ref[pair_ref[0, group]] - occ_ref[pair_ref[1, group]]


def hop_kernel(step, where_ref, part_ref, *refs):
    nz, rows = part_ref.shape[:2]
    above = lax.rem(where_ref[0] + step, nz)
    below = lax.rem(where_ref[0] + nz - step, nz)
    up_ref, down_ref = refs[-2:]
    if len(refs) == 4:
        up_ref[...] = part_ref[above] + refs[0][...]
        down_ref[...] = part_ref[below] + refs[1][...]
    else:
        cut = rows // 2
        up_ref[...] = part_ref[above]
        down_ref[...] = part_ref[below]
        up_ref[:cut] += jnp.concatenate([refs[0][...], refs[2][...]], axis=1)
        down_ref[cut:] += jnp.concatenate([refs[1][...], refs[3][...]], axis=1)


def amplitude_kernel(where_ref, part_ref, up_in, down_in, denom_ref, out_ref, rounded_ref):
    sums = part_ref[where_ref[0]] + (up_in[...] + down_in[...])
    half = sums.shape[1] // 2
    near, far = sums[:, :half], sums[:, half:]
    halves = (jnp.where(where_ref[1] == 0, near, far), jnp.where(where_ref[1] == 0, far, near))
    step = half // part_ref.shape[0]
    parts = [h[:, k * step : (k + 1) * step] for k in range(part_ref.shape[0]) for h in halves]
    amps = jnp.concatenate(parts, axis=1) / denom_ref[...]
    out_ref[...] = amps
    rounded_ref[...] = amps.astype(BF16)


def blocks_kernel(rows_ref, blocks_ref):
    count, rows, lanes = blocks_ref.shape
    width = rows_ref.shape[1] // count
    rest, room = width - 2 * rows, lanes - 2 * width
    left = width - room
    tails = [rows_ref[2 * rows : 3 * rows, (k + 1) * width - left : (k + 1) * width] for k in range(count)]
    tails = jnp.concatenate(tails, axis=1).T
    gap = jnp.zeros((left, room - rows), F32)
    for k in range(count):
        block = rows_ref[:, k * width : (k + 1) * width]
        tail = jnp.concatenate([tails[k * left : (k + 1) * left], gap], axis=1)
        third = jnp.concatenate([block[2 * rows : width, :room], tail], axis=0)
        blocks_ref[k] = jnp.concatenate([block[:rows], block[rows : 2 * rows], third], axis=1)


def merge_kernel(width, *refs):
    count = len(refs) // 3
    for n in range(count):
        first, second = refs[2 * n], refs[2 * n + 1]
        refs[2 * count + n][...] = jnp.concatenate([first[:width], second[:width]], axis=0)


def halves_kernel(up_ref, down_ref, after_ref, first_ref, second_ref):
    first_ref[...] = up_ref[: first_ref.shape[0]]
    second_ref[...] = down_ref[down_ref.shape[0] - second_ref.shape[0] :]


def natural(c, yh, near, far):
    width = near.shape[1] // 2
    parts = []
    for y in range(2):
        for h in range(2):
            side = jnp.where(c == h, near, far)
            parts.append(jnp.where(yh == y, side[:, :width], side[:, width:]))
    return jnp.concatenate(parts, axis=1)


def relative(c, yh, block):
    width = block.shape[1] // 4
    sides = []
    for h in range(2):
        first, second = block[:, h * width : (h + 1) * width], block[:, (2 + h) * width : (3 + h) * width]
        sides.append(jnp.concatenate([jnp.where(yh == 0, first, second), jnp.where(yh == 0, second, first)], axis=1))
    return jnp.where(c == 0, sides[0], sides[1]), jnp.where(c == 0, sides[1], sides[0])


def density_pieces(steps, nz, where_ref, tilde, tilde_t_ref, pieces, total, blocks_ref):
    z, c, yh = where_ref[0], where_ref[1], where_ref[6]
    rows = tilde_t_ref.shape[3]
    pieces = list(pieces)
    for r in steps:
        at = lax.rem(z + r, nz)
        sides = []
        for slot in range(2):
            piece = pieces.pop(0)[...]
            if piece.shape[0] < rows:
                piece = jnp.concatenate([piece, pieces.pop(0)[2 * piece.shape[0] - rows :]], axis=0)
            term = jnp.dot(tilde_t_ref[at, slot], piece, preferred_element_type=F32)
            total = term if total is None else total + term
            sides.append(dot_nt(tilde, piece))
        blocks_ref[at] = natural(c, yh, sides[0], sides[1])
    return total


def early_kernel(steps, nz, where_ref, rows_ref, columns_ref, *refs):
    pieces = refs[:-4]
    total_ref, blocks_ref, tilde_ref, tilde_t_ref = refs[-4:]
    c, yh = where_ref[1], where_ref[6]
    rows = rows_ref[...]
    padded, nvir = rows.shape
    slab = nvir // nz
    width = slab // 4

    def turn(at):
        block = columns_ref[at]
        flipped = block.T
        lanes, rows = flipped.shape
        rest = width - 2 * rows
        third = jnp.concatenate([flipped[2 * width :, :rest], block[rest:, 2 * width : 2 * width + rest]], axis=0)
        found = jnp.concatenate([flipped[:width], flipped[width : 2 * width], third], axis=1)
        return jnp.concatenate([found, jnp.zeros((padded - width, width), F32)], axis=0)

    turned = []
    for k in range(nz):
        near, far = (
            jnp.concatenate([turn(4 * k + 2 * yh + h), turn(4 * k + 2 * (1 - yh) + h)], axis=1) for h in (c, 1 - c)
        )
        mine = relative(c, yh, rows[:, k * slab : (k + 1) * slab])
        tilde_t_ref[k, 0] = (2.0 * near - mine[0]).astype(BF16)
        tilde_t_ref[k, 1] = (2.0 * far - mine[1]).astype(BF16)
        turned.append(natural(c, yh, near, far))
    tilde = (2.0 * rows - jnp.concatenate(turned, axis=1)).astype(BF16)
    tilde_ref[...] = tilde
    total_ref[...] = density_pieces(steps, nz, where_ref, tilde, tilde_t_ref, pieces, None, blocks_ref)


def late_kernel(steps, nz, where_ref, total_ref, blocks_ref, tilde_ref, tilde_t_ref, *refs):
    pieces, out_ref, sums_ref = refs[:-2], refs[-2], refs[-1]
    padded, nvir = total_ref.shape
    slab = nvir // nz
    lanes = out_ref.shape[2]
    gap = jnp.zeros((padded // 2, 3 * lanes - 2 * slab), F32)
    for k in range(nz):
        sums_ref[k] = blocks_ref[k]
    total = density_pieces(
        steps, nz, where_ref, tilde_ref[...], tilde_t_ref, pieces, total_ref[...], sums_ref
    )
    for k in range(nz):
        block = sums_ref[k] + total[:, k * slab : (k + 1) * slab]
        out_ref[k, :padded] = block[:, :lanes]
        rest = block[:, lanes:]
        out_ref[k, padded:] = jnp.concatenate([rest[: padded // 2], rest[padded // 2 :], gap], axis=1)


def sum_kernel(parts_ref, out_ref):
    width, slab = out_ref.shape
    total = parts_ref[0]
    for k in range(1, parts_ref.shape[0]):
        total = total + parts_ref[k]
    rows, lanes = total.shape[0] * 2 // 3, total.shape[1]
    rest = total[rows:]
    extra = slab - lanes
    rest = jnp.concatenate([rest[:, :extra], rest[:, extra : 2 * extra]], axis=0)
    out_ref[...] = jnp.concatenate([total[:rows], rest], axis=1)[:width]


def local(orbital_b, pair_list, eps_occ, eps_vir):
    slab, naux = orbital_b.shape[1:]
    nvir = eps_vir.shape[0]
    z, yh, c = (lax.axis_index(a) for a in ("z", "yh", "c"))
    nz = lax.axis_size("z")
    width = slab // 4
    padded = (width + 8) // 8 * 8
    where = jnp.stack([z, c, z * 4 + yh * 2 + c, lax.axis_index(SLABS), yh * 2 + c, jnp.int32(width), yh])

    pairs = pair_list.T

    sent = 2 * padded + slab // 2
    theirs = pl.pallas_call(
        functools.partial(select_kernel, width, padded),
        out_shape=jax.ShapeDtypeStruct((8, sent, naux), BF16),
        in_specs=[SMEM, SMEM, VMEM],
        out_specs=VMEM,
        compiler_params=params(8),
    )(where, pairs, orbital_b)
    taken = swap(theirs, "c")
    outgoing = jax.ShapeDtypeStruct((16, sent - padded, 2 * naux), BF16)
    ours = pl.pallas_call(
        functools.partial(own_kernel, width, padded),
        out_shape=outgoing,
        in_specs=[SMEM, SMEM, VMEM],
        out_specs=VMEM,
        compiler_params=params(8),
    )(where, pairs, orbital_b)
    ours = pl.pallas_call(
        functools.partial(other_kernel, padded),
        out_shape=outgoing,
        in_specs=[SMEM, VMEM, VMEM],
        out_specs=VMEM,
        input_output_aliases={2: 0},
        compiler_params=params(8),
    )(where, taken, ours)
    near = lax.all_to_all(ours, ("yh", "x", "yl"), split_axis=0, concat_axis=0, tiled=True)
    far = swap(near[:, padded:], "c")

    whole = jax.ShapeDtypeStruct((8, padded, nvir), F32)
    rows = jax.ShapeDtypeStruct((padded, nvir), F32)
    quarter = jax.ShapeDtypeStruct((padded // 2, nvir // 2), F32)
    flops = 16 * padded * 8 * slab * 2 * naux
    near_part, up, down = pl.pallas_call(
        functools.partial(near_kernel, padded),
        out_shape=(jax.ShapeDtypeStruct((8, padded, nvir // 2), F32), quarter, quarter),
        in_specs=[SMEM, VMEM],
        out_specs=(VMEM,) * 3,
        compiler_params=params(16),
        cost_estimate=cost(flops, 0),
    )(where, near)
    sums = (shift(up, "z", 1), shift(down, "z", -1))
    up, down = pl.pallas_call(
        functools.partial(first_kernel, padded, nz),
        out_shape=(quarter, quarter),
        in_specs=[SMEM, VMEM, VMEM],
        out_specs=(VMEM, VMEM),
        compiler_params=params(16),
        cost_estimate=cost(flops // 8, 0),
    )(where, near, far)
    sums += (shift(up, "z", 1), shift(down, "z", -1))
    part, denom = pl.pallas_call(
        functools.partial(rest_kernel, padded),
        out_shape=(whole, rows),
        in_specs=[SMEM, SMEM, SMEM, VMEM, VMEM, VMEM, VMEM],
        out_specs=(VMEM, VMEM),
        compiler_params=params(16),
        cost_estimate=cost(flops, 0),
    )(where, pairs, eps_occ, eps_vir[None], near_part, near, far)
    for step in range(nz // 2 - 1, 0, -1):
        up, down = pl.pallas_call(
            functools.partial(hop_kernel, step),
            out_shape=(rows, rows),
            in_specs=[SMEM] + [VMEM] * (1 + len(sums)),
            out_specs=(VMEM, VMEM),
            compiler_params=params(8),
        )(where, part, *sums)
        sums = (shift(up, "z", 1), shift(down, "z", -1))
    up, down = sums
    rows16 = jax.ShapeDtypeStruct((padded, nvir), BF16)
    amp_rows, mine = pl.pallas_call(
        amplitude_kernel,
        out_shape=(rows, rows16),
        in_specs=[SMEM, VMEM, VMEM, VMEM, VMEM],
        out_specs=(VMEM, VMEM),
        compiler_params=params(8),
    )(where, part, up, down, denom)

    other = swap(mine, "yh")
    columns = pl.pallas_call(
        blocks_kernel,
        out_shape=jax.ShapeDtypeStruct((4 * nz, 16, 128), F32),
        in_specs=[VMEM],
        out_specs=VMEM,
        compiler_params=params(8),
    )(amp_rows)
    other, _ = lax.optimization_barrier((other, columns))
    columns = lax.all_to_all(columns, ("z", "yh", "c"), split_axis=0, concat_axis=0, tiled=True)

    def merge(*halves):
        count = len(halves) // 2
        return pl.pallas_call(
            functools.partial(merge_kernel, width),
            out_shape=(jax.ShapeDtypeStruct((2 * width, nvir), BF16),) * count,
            in_specs=[VMEM] * (2 * count),
            out_specs=(VMEM,) * count,
            compiler_params=params(8),
        )(*halves)

    up, down = merge(shift(mine, "z", 1), shift(other, "z", 1), shift(mine, "z", -1), shift(other, "z", -1))
    (both,) = merge(mine, other)
    ring = {0: both, nz - 1: up, 1: down}
    up, down = shift(up, "z", 1), shift(down, "z", -1)
    ring[nz - 2], ring[2] = up, down
    far = {r: swap(ring[r], "c") for r in (0, 1, nz - 1)}
    up, down, far = lax.optimization_barrier((up, down, far))
    half_up, half_down = pl.pallas_call(
        halves_kernel,
        out_shape=(rows16, rows16),
        in_specs=[VMEM, VMEM, pl.BlockSpec(memory_space=pl.ANY)],
        out_specs=(VMEM, VMEM),
        compiler_params=params(8),
    )(up, down, columns)
    last = (shift(down, "z", -1), shift(up, "z", 1), shift(half_up, "z", 2), shift(half_down, "z", -2))

    soon = (0, 1, nz - 1, 2, nz - 2)
    late = (3, nz - 3, nz // 2)
    far.update({r: swap(ring[r], "c") for r in (2, nz - 2)})
    ring[0] = both
    pieces = [v for r in soon for v in (ring[r], far[r])]
    state = pl.pallas_call(
        functools.partial(early_kernel, soon, nz),
        out_shape=(
            rows,
            jax.ShapeDtypeStruct((nz, padded, slab), F32),
            rows16,
            jax.ShapeDtypeStruct((nz, 2, padded, 2 * width), BF16),
        ),
        in_specs=[SMEM] + [VMEM] * (2 + 2 * len(soon)),
        out_specs=(VMEM,) * 4,
        compiler_params=params(16),
        cost_estimate=cost(len(soon) * 8 * padded * padded * nvir, len(soon) * 8 * padded * nvir),
    )(where, amp_rows, columns, *pieces)
    last, state = lax.optimization_barrier((last, state))
    added = pl.pallas_call(
        functools.partial(late_kernel, late, nz),
        out_shape=jax.ShapeDtypeStruct((nz, padded * 3 // 2, 128), F32),
        in_specs=[SMEM] + [VMEM] * (6 + 2 * len(late)),
        out_specs=VMEM,
        scratch_shapes=[pltpu.VMEM((nz, padded, slab), F32)],
        compiler_params=params(16),
        cost_estimate=cost(len(late) * 8 * padded * padded * nvir, len(late) * 8 * padded * nvir),
    )(
        where,
        *state,
        last[0],
        swap(last[0], "c"),
        last[1],
        swap(last[1], "c"),
        last[2],
        last[3],
        swap(last[2], "c"),
        swap(last[3], "c"),
    )
    added = lax.all_to_all(added, SLABS, split_axis=0, concat_axis=0, tiled=True)
    return pl.pallas_call(
        sum_kernel,
        out_shape=jax.ShapeDtypeStruct((width, slab), F32),
        in_specs=[VMEM],
        out_specs=VMEM,
        compiler_params=params(8),
    )(added)


def solution(mesh):
    fine = Mesh(mesh.devices.reshape(4, 2, 8, 2, 2), ("x", "yl", "z", "yh", "c"))
    pair, grid = SLABS, ("z", "yh", "c")
    in_specs = (P(None, pair, grid), P(), P(), P())
    return jax.shard_map(local, mesh=fine, in_specs=in_specs, out_specs=P(grid, pair), check_vma=False)
```
